32 devices in a mesh: dp: 8 (over y, x, core), tensor: 4 (over z).
Axes of the slice: x: 2, y: 2, z: 4, core: 2. Of those that a mesh axis runs over, the one named last changes fastest.
Arguments:
- tokens: int32 [8, 1024], P('dp', 'tensor'), may hold values from 0 to 50271
- segments: int32 [8, 1024], P('dp'), may hold values from 0 to 12, never falling along the last dimension, each value on 1 to 256 neighbouring positions
- parents: int32 [8, 13], P('dp'), may hold values from 0 to 4, as said below
- completion: int32 [8, 256], P('dp', 'tensor'), may hold values from -1 to 1023, as said below
- targets: int32 [8, 256], P('dp', 'tensor'), may hold values from 0 to 50271
- table: float32 [50272, 512], P('dp')
- table_moment: float32 [50272, 512], P('dp'), may hold values from -0.00390625 to 0.00390625
- vectors: float32 [12, 1024], replicated
- vector_moment: float32 [12, 1024], replicated, may hold values from -0.0234375 to 0.0234375
- w_in: float32 [512, 1024], P('dp'), may hold values from -3 to 3
- moment_in: float32 [512, 1024], P('dp'), may hold values from -0.0234375 to 0.0234375
- error_in: float32 [8, 512, 1024], P('dp'), may hold values from -0.0078125 to 0.0078125
- factor_in: float32 [1024, 8], replicated, may hold values from -6 to 6
- w_qkv: float32 [1024, 3, 1024], P('dp', None, 'tensor'), may hold values from -0.1875 to 0.1875
- moment_qkv: float32 [1024, 3, 1024], P('dp', None, 'tensor'), may hold values from -0.0234375 to 0.0234375
- error_qkv: float32 [8, 1024, 3, 1024], P('dp', None, None, 'tensor'), may hold values from -0.0078125 to 0.0078125
- factor_qkv: float32 [3, 1024, 8], P(None, 'tensor'), may hold values from -6 to 6
- w_proj: float32 [1024, 1024], P('tensor', 'dp'), may hold values from -3.5 to 3.5
- moment_proj: float32 [1024, 1024], P('tensor', 'dp'), may hold values from -0.0234375 to 0.0234375
- error_proj: float32 [8, 1024, 1024], P('dp', 'tensor'), may hold values from -0.0078125 to 0.0078125
- factor_proj: float32 [4, 1024, 8], P('tensor'), may hold values from -6 to 6
- w_up: float32 [1024, 4096], P('dp', 'tensor'), may hold values from -0.1875 to 0.1875
- moment_up: float32 [1024, 4096], P('dp', 'tensor'), may hold values from -0.0234375 to 0.0234375
- error_up: float32 [8, 1024, 4096], P('dp', None, 'tensor'), may hold values from -0.0078125 to 0.0078125
- factor_up: float32 [4096, 8], P('tensor'), may hold values from -6 to 6
- w_down: float32 [4096, 1024], P('tensor', 'dp'), may hold values from -0.09375 to 0.09375
- moment_down: float32 [4096, 1024], P('tensor', 'dp'), may hold values from -0.0234375 to 0.0234375
- error_down: float32 [8, 4096, 1024], P('dp', 'tensor'), may hold values from -0.0078125 to 0.0078125
- factor_down: float32 [4, 1024, 8], P('tensor'), may hold values from -6 to 6
- w_out: float32 [1024, 512], P('dp'), may hold values from -0.1875 to 0.1875
- moment_out: float32 [1024, 512], P('dp'), may hold values from -0.0234375 to 0.0234375
- error_out: float32 [8, 1024, 512], P('dp'), may hold values from -0.0078125 to 0.0078125
- factor_out: float32 [512, 8], replicated, may hold values from -6 to 6
Outputs:
- loss_sum: float32 [], replicated
- new_table: float32 [50272, 512], P('dp')
- new_table_moment: float32 [50272, 512], P('dp')
- new_vectors: float32 [12, 1024], replicated
- new_vector_moment: float32 [12, 1024], replicated
- new_w_in: float32 [512, 1024], P('dp')
- new_moment_in: float32 [512, 1024], P('dp')
- new_error_in: float32 [8, 512, 1024], P('dp')
- new_factor_in: float32 [1024, 8], replicated
- new_w_qkv: float32 [1024, 3, 1024], P('dp', None, 'tensor')
- new_moment_qkv: float32 [1024, 3, 1024], P('dp', None, 'tensor')
- new_error_qkv: float32 [8, 1024, 3, 1024], P('dp', None, None, 'tensor')
- new_factor_qkv: float32 [3, 1024, 8], P(None, 'tensor')
- new_w_proj: float32 [1024, 1024], P('tensor', 'dp')
- new_moment_proj: float32 [1024, 1024], P('tensor', 'dp')
- new_error_proj: float32 [8, 1024, 1024], P('dp', 'tensor')
- new_factor_proj: float32 [4, 1024, 8], P('tensor')
- new_w_up: float32 [1024, 4096], P('dp', 'tensor')
- new_moment_up: float32 [1024, 4096], P('dp', 'tensor')
- new_error_up: float32 [8, 1024, 4096], P('dp', None, 'tensor')
- new_factor_up: float32 [4096, 8], P('tensor')
- new_w_down: float32 [4096, 1024], P('tensor', 'dp')
- new_moment_down: float32 [4096, 1024], P('tensor', 'dp')
- new_error_down: float32 [8, 4096, 1024], P('dp', 'tensor')
- new_factor_down: float32 [4, 1024, 8], P('tensor')
- new_w_out: float32 [1024, 512], P('dp')
- new_moment_out: float32 [1024, 512], P('dp')
- new_error_out: float32 [8, 1024, 512], P('dp')
- new_factor_out: float32 [512, 8], replicated
The draws below stay inside these ranges and needn't reach their ends.
Inputs may be any that keep to these rules, and one draw needn't show every extreme that they name: `parents`: in every tree segment 0 is the trunk and its own parent, segments 1 to 4 are branches with parent 0, and segments 5 to 12 are leaves, two under each branch. `completion`: each device's 64 slots hold distinct positions of that device's 256 positions of its tree; the live slots come first, slot 0 holds the block's last position, the rest are -1; on the last tree every slot is live.
All inputs are finite; a program needn't handle non-finite values.
Results may differ from the reference program's by a relative error of at most 0.012.
The reference program's roundings to bfloat16 on the way (of `embedded`, `qkv`, `attn` and `act`) count: a program that leaves them out, or rounds other values in their place, can miss the bound.
Values may be sent and summed in bfloat16 or wider, within the bound.
No kernel may reach another device: no remote copies, remote signals or barrier semaphores. Data moves between devices by JAX's collectives and lax.ppermute only.
A program may use at most 320 MiB of HBM per device.

```python
import math
import jax
import jax.numpy as jnp
import numpy as np
from jax import lax

V = 50272
D = 1024
D_EMB = 512
H = 16
HD = 64
FF = 4096
NSEG = 13
RANK = 8
TOK_DEV = 256
L = 1024
C_DEV = 64
N_DP = 8
N_TENSOR = 4


def draw_parents(key, part):
    key = jax.random.fold_in(key, 11)
    tree_keys = jax.random.split(key, N_DP)

    def one_tree(tree_key):
        shuffled = jax.random.permutation(tree_key, 4).astype(jnp.int32)
        return jnp.concatenate([jnp.zeros((5,), jnp.int32), 1 + jnp.repeat(shuffled, 2)])
    return jax.vmap(one_tree)(tree_keys)


def draw_completion(key, part):
    key = jax.random.fold_in(key, 12)
    block_keys = jax.random.split(key, N_DP * N_TENSOR)

    def one_block(block_key, block_number):
        tree_row = block_number // N_TENSOR
        column = block_number % N_TENSOR
        first_key, second_key = jax.random.split(block_key)
        shuffled = jax.random.permutation(first_key, TOK_DEV - 1).astype(jnp.int32)
        positions = jnp.concatenate([jnp.full((1,), TOK_DEV - 1, jnp.int32), shuffled[:C_DEV - 1]]) + column * TOK_DEV
        floor_count = C_DEV * (N_DP - 1 + 2 * tree_row) // (3 * (N_DP - 1))
        shortfall = jax.random.randint(second_key, (), 0, C_DEV // 6 + 1)
        live_count = jnp.where(tree_row == N_DP - 1, C_DEV, jnp.maximum(floor_count - shortfall, 1))
        return jnp.where(jnp.arange(C_DEV) < live_count, positions, -1).astype(jnp.int32)
    blocks = jax.vmap(one_block)(block_keys, jnp.arange(N_DP * N_TENSOR))
    return blocks.reshape(N_DP, N_TENSOR * C_DEV)


def draw_table(key, part):
    key = jax.random.fold_in(key, 13)
    ramp = jnp.arange(V, dtype=jnp.float32) / (V - 1)
    values = jax.random.truncated_normal(key, -6.0, 6.0, (V, D_EMB), jnp.float32) * (1.0 + 2.0 * ramp)[:, None]
    return values / D_EMB ** 0.5


def draw_vectors(key, part):
    key = jax.random.fold_in(key, 14)
    first_key, second_key = jax.random.split(key)
    count = 8 + FF // D
    gains = jax.random.uniform(first_key, (count, D), jnp.float32, 0.5, 1.5)
    shifts = 0.3 * jax.random.truncated_normal(second_key, -3.0, 3.0, (count, D), jnp.float32)
    rows = jnp.arange(count)
    is_gain = (rows == 0) | (rows == 2)
    return jnp.where(is_gain[:, None], gains, shifts)


def with_ends(values, own_key, smallest, high):
    longest = values.shape.index(max(values.shape))
    spots = []
    for shift in (0, 1):
        where = [jax.random.randint(jax.random.fold_in(own_key, axis), (), 0, length) for axis, length in enumerate(values.shape)]
        where[longest] = (where[longest] + shift) % values.shape[longest]
        spots.append(tuple(where))
    return values.at[spots[0]].set(smallest).at[spots[1]].set(high)


def levels(key, shape, shards, smallest, largest):
    loudness = 1.0
    for axis_at, parts in shards:
        draws = jax.random.uniform(jax.random.fold_in(jax.random.fold_in(key, 6), axis_at), (parts,), jnp.float32, smallest / len(shards), largest / len(shards))
        loudness = loudness * jnp.repeat(jnp.exp(draws), shape[axis_at] // parts).reshape((-1,) + (1,) * (len(shape) - 1 - axis_at))
    return loudness


def cumulative_ranks(number_of, lean):
    weights = [(1 << 20) // math.isqrt(grade ** lean) + 1 for grade in range(1, number_of + 1)]
    width = 1 + sum(weights) // (1 << 30)
    return np.cumsum(np.array([max(1, weight // width) for weight in weights]))


def skewed_ids(own_key, shape, number_of, skew):
    listing = cumulative_ranks(number_of, skew)
    lot = jax.random.randint(jax.random.fold_in(own_key, 1), shape, 0, int(listing[number_of - 1]))
    grade = jnp.searchsorted(jnp.asarray(listing, jnp.int32), lot, side="right")
    return jax.random.permutation(jax.random.fold_in(own_key, 2), number_of)[grade].astype(jnp.int32)


def split_up(count, total, limit, skew):
    weights = [(1 << 20) // math.isqrt(grade ** skew) + 1 for grade in range(2, count + 1)]
    rest, given = total - limit - (count - 1), [1] * (count - 1)
    while rest > 0:
        movable = [i for i in range(count - 1) if given[i] < limit]
        mass, left = sum([weights[i] for i in movable]), rest
        for i in movable:
            addition = min(limit - given[i], max(1, left * weights[i] // mass), rest)
            given[i] = given[i] + addition
            rest = rest - addition
    return np.array([limit] + given)


def ragged(stream_key, number_of, total, most, slope):
    if number_of == 2:
        one = jax.random.randint(stream_key, (), max(1, total - most), min(most, total - 1) + 1)
        return jnp.stack([one, total - one])
    tallies = jnp.asarray(split_up(number_of, total, most, slope), jnp.int32)
    pairs = (number_of - 1) // 2
    giver, taker = tallies[1:1 + 2 * pairs:2], tallies[2:2 + 2 * pairs:2]
    room = jnp.minimum(giver - 1, most - taker)
    shifted = jax.random.randint(jax.random.fold_in(stream_key, 1), (pairs,), 0, 1 << 20) % (room + 1)
    tallies = tallies.at[1:1 + 2 * pairs:2].set(giver - shifted).at[2:2 + 2 * pairs:2].set(taker + shifted)
    return tallies[jax.random.permutation(jax.random.fold_in(stream_key, 2), number_of)]


def bell_draw(own_key, extent, scale, bound, cuts=(), kind=jnp.bfloat16):
    values = scale * jax.random.normal(own_key, extent, jnp.float32)
    if cuts:
        values = values * levels(own_key, extent, cuts, -0.22, 0.18)
    return jnp.clip(values, -bound, bound).astype(kind)


def setup_inputs(seed: int = 0) -> dict:
    key_list = jax.random.split(jax.random.key(seed), 34)
    tokens = with_ends(skewed_ids(key_list[0], (N_DP, L), V, 2), jax.random.fold_in(key_list[0], 3), 0, V - 1).astype(jnp.int32)
    segments = jax.vmap(lambda own: jnp.searchsorted(jnp.cumsum(ragged(own, NSEG, L, L // 4, 2)), jnp.arange(L), side="right"))(jax.random.split(key_list[1], N_DP)).reshape((N_DP, L)).astype(jnp.int32)
    parents = draw_parents(jax.random.fold_in(key_list[33], 71), 0)
    completion = draw_completion(jax.random.fold_in(key_list[33], 71), 0)
    targets = with_ends(skewed_ids(key_list[4], (N_DP, N_TENSOR * C_DEV), V, 2), jax.random.fold_in(key_list[4], 3), 0, V - 1).astype(jnp.int32)
    table = draw_table(jax.random.fold_in(key_list[33], 71), 0)
    table_moment = bell_draw(key_list[6], (V, D_EMB), (0.3 / (N_DP * N_TENSOR * C_DEV * D_EMB) ** 0.5), 0.00390625, ((0, 8),), jnp.float32)
    vectors = draw_vectors(jax.random.fold_in(key_list[33], 71), 0)
    vector_moment = bell_draw(key_list[8], (8 + FF // D, D), (1.5 / (N_DP * N_TENSOR * C_DEV * D_EMB) ** 0.5), 0.0234375, (), jnp.float32)
    w_in = bell_draw(key_list[9], (D_EMB, D), 4 ** -0.5, 3.0, ((0, 8),), jnp.float32)
    moment_in = bell_draw(key_list[10], (D_EMB, D), (1.5 / (N_DP * N_TENSOR * C_DEV * D_EMB) ** 0.5), 0.0234375, ((0, 8),), jnp.float32)
    error_in = bell_draw(key_list[11], (N_DP, D_EMB, D), (1.5 / (N_DP * N_DP * N_TENSOR * C_DEV * D_EMB) ** 0.5), 0.0078125, ((0, 8),), jnp.float32)
    factor_in = bell_draw(key_list[12], (D, RANK), 1.0, 6.0, (), jnp.float32)
    w_qkv = bell_draw(key_list[13], (D, 3, D), D ** -0.5, 0.1875, ((0, 8), (2, 4)), jnp.float32)
    moment_qkv = bell_draw(key_list[14], (D, 3, D), (1.5 / (N_DP * N_TENSOR * C_DEV * D_EMB) ** 0.5), 0.0234375, ((0, 8), (2, 4)), jnp.float32)
    error_qkv = bell_draw(key_list[15], (N_DP, D, 3, D), (1.5 / (N_DP * N_DP * N_TENSOR * C_DEV * D_EMB) ** 0.5), 0.0078125, ((0, 8), (3, 4)), jnp.float32)
    factor_qkv = bell_draw(key_list[16], (3, D, RANK), 1.0, 6.0, ((1, 4),), jnp.float32)
    w_proj = bell_draw(key_list[17], (D, D), (max(1, 3 * D // L)) ** -0.5, 3.5, ((0, 4), (1, 8)), jnp.float32)
    moment_proj = bell_draw(key_list[18], (D, D), (1.5 / (N_DP * N_TENSOR * C_DEV * D_EMB) ** 0.5), 0.0234375, ((0, 4), (1, 8)), jnp.float32)
    error_proj = bell_draw(key_list[19], (N_DP, D, D), (1.5 / (N_DP * N_DP * N_TENSOR * C_DEV * D_EMB) ** 0.5), 0.0078125, ((0, 8), (1, 4)), jnp.float32)
    factor_proj = bell_draw(key_list[20], (N_TENSOR, D, RANK), 1.0, 6.0, ((0, 4),), jnp.float32)
    w_up = bell_draw(key_list[21], (D, FF), D ** -0.5, 0.1875, ((0, 8), (1, 4)), jnp.float32)
    moment_up = bell_draw(key_list[22], (D, FF), (1.5 / (N_DP * N_TENSOR * C_DEV * D_EMB) ** 0.5), 0.0234375, ((0, 8), (1, 4)), jnp.float32)
    error_up = bell_draw(key_list[23], (N_DP, D, FF), (1.5 / (N_DP * N_DP * N_TENSOR * C_DEV * D_EMB) ** 0.5), 0.0078125, ((0, 8), (2, 4)), jnp.float32)
    factor_up = bell_draw(key_list[24], (FF, RANK), 1.0, 6.0, ((0, 4),), jnp.float32)
    w_down = bell_draw(key_list[25], (FF, D), FF ** -0.5, 0.09375, ((0, 4), (1, 8)), jnp.float32)
    moment_down = bell_draw(key_list[26], (FF, D), (1.5 / (N_DP * N_TENSOR * C_DEV * D_EMB) ** 0.5), 0.0234375, ((0, 4), (1, 8)), jnp.float32)
    error_down = bell_draw(key_list[27], (N_DP, FF, D), (1.5 / (N_DP * N_DP * N_TENSOR * C_DEV * D_EMB) ** 0.5), 0.0078125, ((0, 8), (1, 4)), jnp.float32)
    factor_down = bell_draw(key_list[28], (N_TENSOR, D, RANK), 1.0, 6.0, ((0, 4),), jnp.float32)
    w_out = bell_draw(key_list[29], (D, D_EMB), D ** -0.5, 0.1875, ((0, 8),), jnp.float32)
    moment_out = bell_draw(key_list[30], (D, D_EMB), (1.5 / (N_DP * N_TENSOR * C_DEV * D_EMB) ** 0.5), 0.0234375, ((0, 8),), jnp.float32)
    error_out = bell_draw(key_list[31], (N_DP, D, D_EMB), (1.5 / (N_DP * N_DP * N_TENSOR * C_DEV * D_EMB) ** 0.5), 0.0078125, ((0, 8),), jnp.float32)
    factor_out = bell_draw(key_list[32], (D_EMB, RANK), 1.0, 6.0, (), jnp.float32)
    return dict(tokens=tokens, segments=segments, parents=parents, completion=completion, targets=targets, table=table, table_moment=table_moment, vectors=vectors, vector_moment=vector_moment, w_in=w_in, moment_in=moment_in, error_in=error_in, factor_in=factor_in, w_qkv=w_qkv, moment_qkv=moment_qkv, error_qkv=error_qkv, factor_qkv=factor_qkv, w_proj=w_proj, moment_proj=moment_proj, error_proj=error_proj, factor_proj=factor_proj, w_up=w_up, moment_up=moment_up, error_up=error_up, factor_up=factor_up, w_down=w_down, moment_down=moment_down, error_down=error_down, factor_down=factor_down, w_out=w_out, moment_out=moment_out, error_out=error_out, factor_out=factor_out)


@jax.custom_vjp
def low(v):
    return lax.optimization_barrier(v.astype(jnp.bfloat16)).astype(jnp.float32)

@jax.custom_vjp
def low_back(v):
    return v

def low_keep(v):
    return (low(v), None)

def low_pass(kept, grad):
    return (grad,)

def back_keep(v):
    return (v, None)

def back_low(kept, grad):
    return (low(grad),)
low.defvjp(low_keep, low_pass)
low_back.defvjp(back_keep, back_low)
HIGH = lax.Precision.HIGHEST
momentum_decay = 0.9
table_rate = 300.0
vector_rate = 1000.0
matrix_rates = (1500.0, 80.0, 3000.0, 80.0, 40.0, 80.0)

def product(left, right):
    return jnp.dot(left, right, precision=HIGH)

def layer_norm(values, gain, shift):
    center = values - lax.optimization_barrier(jnp.mean(values, -1, keepdims=True))
    spread = lax.optimization_barrier(jnp.mean(center * center, -1, keepdims=True))
    return center * lax.rsqrt(spread + 1e-05) * gain + shift

def tree_loss(table, vectors, w_in, w_qkv, w_proj, w_up, w_down, w_out, ids, segs, parent_row, comp, tgt):
    length = ids.shape[0]
    table_low = low(table)
    embedded = low_back(jnp.take(table_low, ids, axis=0))
    x_zero = low_back(product(embedded, low(w_in)))
    bias_three = jnp.stack([vectors[4], jnp.zeros_like(vectors[4]), vectors[5]])
    qkv = jnp.einsum('ld,dch->lch', low(x_zero), low(w_qkv), precision=HIGH) + bias_three
    qkv = low(low_back(qkv))
    queries = qkv[:, 0].reshape(length, H, HD)
    keys_all = qkv[:, 1].reshape(length, H, HD)
    values_all = qkv[:, 2].reshape(length, H, HD)
    first = parent_row[segs]
    second = parent_row[first]
    columns = jnp.arange(length)
    block = min(512, length)

    def attend(start):
        query_block = lax.dynamic_slice_in_dim(queries, start, block, 0)
        rows = start + jnp.arange(block)
        own = lax.dynamic_slice_in_dim(segs, start, block)
        upper_one = lax.dynamic_slice_in_dim(first, start, block)
        upper_two = lax.dynamic_slice_in_dim(second, start, block)
        related = (segs[None, :] == own[:, None]) | (segs[None, :] == upper_one[:, None]) | (segs[None, :] == upper_two[:, None])
        visible = related & (columns[None, :] <= rows[:, None])
        scores = jnp.einsum('qhe,khe->hqk', query_block, keys_all, precision=HIGH) * HD ** (-0.5)
        scores = low_back(scores)
        scores = jnp.where(visible[None], scores, -1e+30)
        probs = low(jax.nn.softmax(scores, axis=-1))
        return jnp.einsum('hqk,khe->qhe', probs, values_all, precision=HIGH)
    attended = lax.map(jax.checkpoint(attend), jnp.arange(0, length, block))
    attn = low(low_back(attended.reshape(length, D)))
    z_branch = low_back(product(attn, low(w_proj)))
    h_one = layer_norm(x_zero + z_branch + vectors[6], vectors[0], vectors[1])
    upper = low_back(product(low(h_one), low(w_up)) + vectors[8:].reshape(-1))
    act = low(jax.nn.gelu(upper, approximate=True))
    f_branch = low_back(product(act, low(w_down)))
    h_two = layer_norm(h_one + f_branch + vectors[7], vectors[2], vectors[3])
    output = low_back(product(low(h_two), low(w_out)))
    valid = comp >= 0
    rows_low = low(jnp.take(output, jnp.maximum(comp, 0), axis=0))
    head_block = min(256, comp.shape[0])

    def head(pack):
        rows_blk, tgt_blk = pack
        logits = low_back(product(rows_blk, table_low.T))
        top = lax.optimization_barrier(jnp.max(logits, -1, keepdims=True))
        total = top[:, 0] + jnp.log(lax.optimization_barrier(jnp.sum(jnp.exp(logits - top), -1)))
        picked = jnp.take_along_axis(logits, tgt_blk[:, None], 1)[:, 0]
        return total - picked
    count = comp.shape[0] // head_block
    entropy = lax.map(jax.checkpoint(head), (rows_low.reshape(count, head_block, D_EMB), tgt.reshape(count, head_block)))
    return jnp.sum(jnp.where(valid, entropy.reshape(-1), 0.0))

def orthonormal(matrix):
    columns = []
    for index in range(matrix.shape[1]):
        vector = matrix[:, index]
        for previous in columns:
            vector = vector - jnp.sum(previous * vector) * previous
        vector = vector * lax.rsqrt(jnp.sum(vector * vector) + 1e-06)
        columns.append(vector)
    return jnp.stack(columns, 1)

def compress(grads, errors, factor):
    merged = grads + errors
    left = lax.optimization_barrier(jnp.sum(jnp.einsum('nrc,ck->nrk', merged, factor, precision=HIGH), 0))
    basis = orthonormal(left)
    fresh = lax.optimization_barrier(jnp.sum(jnp.einsum('nrc,rk->nck', merged, basis, precision=HIGH), 0))
    approx = product(basis, fresh.T)
    return (approx, merged - approx / N_DP, fresh)

def advance(weight, moment, approx, rate):
    fresh_moment = momentum_decay * moment + approx
    return (weight - rate * fresh_moment, fresh_moment)

def reference(tokens, segments, parents, completion, targets, table, table_moment, vectors, vector_moment, w_in, moment_in, error_in, factor_in, w_qkv, moment_qkv, error_qkv, factor_qkv, w_proj, moment_proj, error_proj, factor_proj, w_up, moment_up, error_up, factor_up, w_down, moment_down, error_down, factor_down, w_out, moment_out, error_out, factor_out):
    weights = (table, vectors, w_in, w_qkv, w_proj, w_up, w_down, w_out)
    scale_count = 1.0 / (N_DP * N_TENSOR * C_DEV)

    def one_tree(carry, data):
        ids, segs, parent_row, comp, tgt = data

        def scaled(*params):
            raw = tree_loss(*params, ids, segs, parent_row, comp, tgt)
            return (raw * scale_count, raw)
        value, pull, raw = jax.vjp(scaled, *weights, has_aux=True)
        grads = pull(jnp.ones_like(value))
        return ((carry[0] + grads[0], carry[1] + grads[1], carry[2] + raw), grads[2:])
    start = (jnp.zeros_like(table), jnp.zeros_like(vectors), jnp.zeros((), table.dtype))
    (grad_table, grad_vectors, loss_sum), stacks = lax.scan(one_tree, start, (tokens, segments, parents, completion, targets))
    wide = D // N_TENSOR
    share = FF // N_TENSOR
    approx_in, new_error_in, new_factor_in = compress(stacks[0], error_in, factor_in)
    pieces = [compress(stacks[1][:, :, :, t * wide:(t + 1) * wide].reshape(N_DP, D, 3 * wide), error_qkv[:, :, :, t * wide:(t + 1) * wide].reshape(N_DP, D, 3 * wide), factor_qkv[:, t * wide:(t + 1) * wide].reshape(3 * wide, RANK)) for t in range(N_TENSOR)]
    approx_qkv = jnp.concatenate([piece[0].reshape(D, 3, wide) for piece in pieces], 2)
    new_error_qkv = jnp.concatenate([piece[1].reshape(N_DP, D, 3, wide) for piece in pieces], 3)
    new_factor_qkv = jnp.concatenate([piece[2].reshape(3, wide, RANK) for piece in pieces], 1)
    pieces = [compress(stacks[2][:, t * wide:(t + 1) * wide], error_proj[:, t * wide:(t + 1) * wide], factor_proj[t]) for t in range(N_TENSOR)]
    approx_proj = jnp.concatenate([piece[0] for piece in pieces], 0)
    new_error_proj = jnp.concatenate([piece[1] for piece in pieces], 1)
    new_factor_proj = jnp.stack([piece[2] for piece in pieces], 0)
    pieces = [compress(stacks[3][:, :, t * share:(t + 1) * share], error_up[:, :, t * share:(t + 1) * share], factor_up[t * share:(t + 1) * share]) for t in range(N_TENSOR)]
    approx_up = jnp.concatenate([piece[0] for piece in pieces], 1)
    new_error_up = jnp.concatenate([piece[1] for piece in pieces], 2)
    new_factor_up = jnp.concatenate([piece[2] for piece in pieces], 0)
    pieces = [compress(stacks[4][:, t * share:(t + 1) * share], error_down[:, t * share:(t + 1) * share], factor_down[t]) for t in range(N_TENSOR)]
    approx_down = jnp.concatenate([piece[0] for piece in pieces], 0)
    new_error_down = jnp.concatenate([piece[1] for piece in pieces], 1)
    new_factor_down = jnp.stack([piece[2] for piece in pieces], 0)
    approx_out, new_error_out, new_factor_out = compress(stacks[5], error_out, factor_out)
    new_w_in, new_moment_in = advance(w_in, moment_in, approx_in, matrix_rates[0])
    new_w_qkv, new_moment_qkv = advance(w_qkv, moment_qkv, approx_qkv, matrix_rates[1])
    new_w_proj, new_moment_proj = advance(w_proj, moment_proj, approx_proj, matrix_rates[2])
    new_w_up, new_moment_up = advance(w_up, moment_up, approx_up, matrix_rates[3])
    new_w_down, new_moment_down = advance(w_down, moment_down, approx_down, matrix_rates[4])
    new_w_out, new_moment_out = advance(w_out, moment_out, approx_out, matrix_rates[5])
    new_table, new_table_moment = advance(table, table_moment, grad_table, table_rate)
    new_vectors, new_vector_moment = advance(vectors, vector_moment, grad_vectors, vector_rate)
    return (loss_sum, new_table, new_table_moment, new_vectors, new_vector_moment, new_w_in, new_moment_in, new_error_in, new_factor_in, new_w_qkv, new_moment_qkv, new_error_qkv, new_factor_qkv, new_w_proj, new_moment_proj, new_error_proj, new_factor_proj, new_w_up, new_moment_up, new_error_up, new_factor_up, new_w_down, new_moment_down, new_error_down, new_factor_down, new_w_out, new_moment_out, new_error_out, new_factor_out)
```

```python
import functools

import jax
import jax.numpy as jnp
from jax import lax
from jax.experimental import pallas as pl
from jax.experimental.pallas import tpu as pltpu
from jax.sharding import PartitionSpec as P

HD = 64


momentum_decay = 0.9
table_rate = 300.0
vector_rate = 1000.0
matrix_rates = (1500.0, 80.0, 3000.0, 80.0, 40.0, 80.0)


def to_low(values):
    return values.astype(jnp.bfloat16)


def dense(left, right):
    return jnp.dot(left, right, preferred_element_type=jnp.float32)


def dense_first(left, right):
    return lax.dot_general(
        left, right, (((0,), (0,)), ((), ())), preferred_element_type=jnp.float32
    )


def dense_last(left, right):
    return lax.dot_general(
        left, right, (((1,), (1,)), ((), ())), preferred_element_type=jnp.float32
    )


left_terms = (0, 0, 1, 1, 0, 2)
right_terms = (0, 1, 0, 1, 2, 0)


def left_factor(merged, factor):
    return lax.dot_general(factor, merged, (((0,), (1,)), ((), ())), precision=lax.Precision.HIGH)


def right_factor(merged, basis):
    return lax.dot_general(basis, merged, (((1,), (0,)), ((), ())), precision=lax.Precision.HIGH)


def layer_norm(values, gain, shift):
    center = values - jnp.mean(values, -1, keepdims=True)
    spread = jnp.mean(center * center, -1, keepdims=True)
    return center * lax.rsqrt(spread + 1e-05) * gain + shift


def gelu_tanh(values):
    return jax.nn.gelu(values, approximate=True)


def swap(values, axis, step):
    return lax.ppermute(values, axis, [(i, i ^ step) for i in range(lax.axis_size(axis))])


def gather_blocks(values, axis):
    return [values] + [swap(values, axis, s) for s in range(1, lax.axis_size(axis))]


def exchange_blocks(blocks, axis):
    return [blocks[0]] + [swap(blocks[s], axis, s) for s in range(1, lax.axis_size(axis))]


def summed_over(values, axis):
    step = 1
    while step < lax.axis_size(axis):
        values = jax.tree.map(lambda a, s=step: a + swap(a, axis, s), values)
        step *= 2
    return values


def add_up(parts):
    total = parts[0].astype(jnp.float32)
    for part in parts[1:]:
        total = total + part.astype(jnp.float32)
    return total


def add_pairs(parts):
    while len(parts) > 1:
        parts = [left + right for left, right in zip(parts[::2], parts[1::2])]
    return parts[0]


def orthonormal_kernel(columns_ref, bases_ref, terms_ref):
    count = columns_ref.shape[0]
    columns = [columns_ref[index] for index in range(count)]
    for index in range(count):
        vector = columns[index]
        vector = vector * lax.rsqrt(jnp.sum(vector * vector, -1, keepdims=True) + 1e-06)
        bases_ref[index] = vector
        for later in range(index + 1, count):
            other = columns[later]
            columns[later] = other - jnp.sum(vector * other, -1, keepdims=True) * vector
        terms = []
        for _ in range(3):
            terms.append(vector.astype(jnp.bfloat16))
            vector = vector - terms[-1].astype(jnp.float32)
        for place, term in enumerate(left_terms):
            terms_ref[place * count + index] = terms[term].astype(jnp.float32)


def orthonormal_all(lefts):
    longest = max(left.shape[1] for left in lefts)
    padded = jnp.stack(
        [jnp.pad(left, ((0, 0), (0, longest - left.shape[1]))) for left in lefts], 1
    )
    many = len(left_terms) * padded.shape[0]
    bases, terms = pl.pallas_call(
        orthonormal_kernel,
        out_shape=[
            jax.ShapeDtypeStruct(padded.shape, jnp.float32),
            jax.ShapeDtypeStruct((many,) + padded.shape[1:], jnp.float32),
        ],
    )(padded)
    return [bases[:, index, : left.shape[1]] for index, left in enumerate(lefts)], [
        to_low(terms[:, index, : left.shape[1]]) for index, left in enumerate(lefts)
    ]


def outer_terms(rights):
    terms = split_low(rights)
    return jnp.concatenate([terms[term] for term in right_terms], 0)


def coarse(values):
    return lax.reduce_precision(values, 8, 7)


def split_low(values):
    first = coarse(values)
    second = coarse(values - first)
    return [to_low(first), to_low(second), to_low(values - first - second)]


def join_low(terms):
    terms = [term.astype(jnp.float32) for term in terms]
    return terms[0] + (terms[1] + terms[2])


def vocab_tile(shard_rows, most=640):
    tiles = -(-shard_rows // most)
    return -(-(-(-shard_rows // tiles)) // 16) * 16


def head_kernel(shard_rows, rows_ref, table_ref, out_ref, total, stats):
    step = pl.program_id(0)
    tile_rows, wide = table_ref.shape

    @pl.when(step == 0)
    def _():
        total[...] = jnp.zeros_like(total)
        stats[0:1, :] = jnp.full((1, stats.shape[1]), -1e30, jnp.float32)
        stats[1:2, :] = jnp.zeros((1, stats.shape[1]), jnp.float32)

    row_ids = step * tile_rows + lax.broadcasted_iota(jnp.int32, (tile_rows, 1), 0)
    present = row_ids < shard_rows
    tile = jnp.where(present, table_ref[...], 0.0).astype(jnp.bfloat16)
    logits = lax.dot_general(
        tile, rows_ref[...], (((1,), (1,)), ((), ())), preferred_element_type=jnp.float32
    )
    logits = jnp.where(present, logits, -1e30)
    before = stats[0:1, :]
    top = jnp.maximum(before, jnp.max(logits, 0, keepdims=True))
    fade = jnp.exp(before - top)
    expo = jnp.exp(logits - top)
    stats[0:1, :] = top
    stats[1:2, :] = stats[1:2, :] * fade + jnp.sum(expo, 0, keepdims=True)
    total[...] = total[...] * fade + lax.dot_general(
        tile,
        expo.astype(jnp.bfloat16),
        (((0,), (0,)), ((), ())),
        preferred_element_type=jnp.float32,
    )

    @pl.when(step == pl.num_programs(0) - 1)
    def _():
        out_ref[:, :wide] = total[...].T.astype(jnp.bfloat16)
        terms = []
        for index in (0, 1):
            value = stats[index : index + 1, :]
            for _ in range(3):
                part = value.astype(jnp.bfloat16).astype(jnp.float32)
                terms.append(part)
                value = value - part
        spare = jnp.zeros((out_ref.shape[1] - wide - 6, value.shape[1]), jnp.float32)
        out_ref[:, wide:] = jnp.concatenate(terms + [spare], 0).T.astype(jnp.bfloat16)


def head_forward(rows, table):
    count, wide = rows.shape
    shard_rows = table.shape[0]
    tile = vocab_tile(shard_rows, 1280 if count <= 1024 else 640)
    return pl.pallas_call(
        functools.partial(head_kernel, shard_rows),
        grid=(pl.cdiv(shard_rows, tile),),
        in_specs=[
            pl.BlockSpec((count, wide), lambda i: (0, 0)),
            pl.BlockSpec((tile, wide), lambda i: (i, 0)),
        ],
        out_specs=pl.BlockSpec((count, wide + 128), lambda i: (0, 0)),
        out_shape=jax.ShapeDtypeStruct((count, wide + 128), jnp.bfloat16),
        scratch_shapes=[
            pltpu.VMEM((wide, count), jnp.float32),
            pltpu.VMEM((8, count), jnp.float32),
        ],
        compiler_params=pltpu.CompilerParams(vmem_limit_bytes=56 * 2**20),
        cost_estimate=pl.CostEstimate(
            flops=4 * shard_rows * count * wide,
            bytes_accessed=4 * shard_rows * wide,
            transcendentals=shard_rows * count,
        ),
    )(rows, table)


def table_kernel(
    rows_ref, shift_ref, added_ref, ids_ref, table_ref, moment_ref, new_table_ref, new_moment_ref
):
    tile_rows, wide = table_ref.shape
    row_ids = pl.program_id(0) * tile_rows
    row_ids = row_ids + lax.broadcasted_iota(jnp.int32, (tile_rows, 1), 0)
    hits = (row_ids == ids_ref[...]).astype(jnp.bfloat16)
    new_moment_ref[...] = momentum_decay * moment_ref[...] + dense(hits, added_ref[...])
    tile = table_ref[...].astype(jnp.bfloat16)
    chunk = min(512, rows_ref.shape[0])

    def one(spot):
        rows = rows_ref[spot, :wide]
        grad = jnp.exp(dense_last(tile, rows) - shift_ref[0:1, spot])
        return dense(grad.astype(jnp.bfloat16), rows)

    together = 4 * chunk if rows_ref.shape[0] % (4 * chunk) == 0 else chunk

    def some(index, carry):
        begin = pl.multiple_of(index * together, together)
        parts = [one(pl.ds(begin + k * chunk, chunk)) for k in range(together // chunk)]
        new_moment_ref[...] += sum(parts[1:], parts[0])
        return carry

    if rows_ref.shape[0] == together:
        some(0, 0)
    else:
        lax.fori_loop(0, rows_ref.shape[0] // together, some, 0)
    new_table_ref[...] = table_ref[...] - table_rate * new_moment_ref[...]


def table_update(rows, shift, added, ids, table, moment):
    shard_rows, wide = table.shape
    tile = vocab_tile(shard_rows)
    whole = lambda array: pl.BlockSpec(
        array.shape, lambda i: (0, 0), pipeline_mode=pl.Buffered(buffer_count=1)
    )
    part = pl.BlockSpec((tile, wide), lambda i: (i, 0))
    return pl.pallas_call(
        table_kernel,
        grid=(pl.cdiv(shard_rows, tile),),
        in_specs=[whole(rows), whole(shift), whole(added), whole(ids), part, part],
        out_specs=[part, part],
        out_shape=[jax.ShapeDtypeStruct(table.shape, jnp.float32)] * 2,
        compiler_params=pltpu.CompilerParams(vmem_limit_bytes=56 * 2**20),
        cost_estimate=pl.CostEstimate(
            flops=shard_rows * wide * (4 * rows.shape[0] + 2 * ids.shape[1]),
            bytes_accessed=16 * shard_rows * wide,
            transcendentals=shard_rows * rows.shape[0],
        ),
    )(rows, shift, added, ids, table, moment)


def visible_pairs(key_ref, row_ref):
    spots, segs = key_ref[:, 0:1], key_ref[:, 1:2]
    related = (segs == row_ref[1:2, :]) | (segs == row_ref[2:3, :]) | (segs == row_ref[3:4, :])
    return related & (spots <= row_ref[0:1, :])


def head_columns(width, head):
    columns = lax.broadcasted_iota(jnp.int32, (1, width), 1)
    return (columns >= head * HD) & (columns < (head + 1) * HD)


def attend_kernel(
    shard_in,
    emb_ref,
    pack_ref,
    bias_ref,
    key_ref,
    row_ref,
    index_ref,
    x_ref,
    x_rows_ref,
    emb_rows_ref,
    query_ref,
    key_value_ref,
    attn_ref,
    lse_ref,
    in_ref,
):
    length = x_ref.shape[0]
    count, width = query_ref.shape
    block = min(256, length)
    share = pack_ref.shape[1] - 3 * width
    halves = in_ref.shape[1] // share
    for owner in range(in_ref.shape[0] // shard_in):
        for part in range(halves):
            begin = (owner * halves + part) * shard_in
            in_ref[owner * shard_in : (owner + 1) * shard_in, part * share : (part + 1) * share] = (
                pack_ref[begin : begin + shard_in, :share]
            )

    def one_block(index, carry):
        spot = pl.ds(pl.multiple_of(index * block, block), block)
        x_low = to_low(dense(emb_ref[spot, :], in_ref[...]))
        x_ref[spot, :] = x_low
        mixed = dense(x_low, pack_ref[:, share + width :]) + bias_ref[:, width:]
        key_value_ref[spot, :] = to_low(mixed)
        return carry

    lax.fori_loop(0, length // block, one_block, 0)
    chosen = index_ref[...] == lax.broadcasted_iota(jnp.int32, (count, length), 1)
    emb_rows = to_low(dense(chosen.astype(jnp.bfloat16), emb_ref[:length, :]))
    emb_rows_ref[...] = emb_rows
    x_rows = dense(emb_rows, in_ref[...])
    x_rows_ref[...] = x_rows
    queries = to_low(dense(to_low(x_rows), pack_ref[:, share : share + width]) + bias_ref[:, :width])
    query_ref[...] = queries
    keys_all = key_value_ref[:, :width]
    values_turned = key_value_ref[:, width:].T
    blocked = jnp.where(visible_pairs(key_ref, row_ref), 0.0, -1e30)
    features = lax.broadcasted_iota(jnp.int32, (width, 1), 0)
    attended = jnp.zeros((width, count), jnp.float32)
    for head in range(width // HD):
        own = jnp.where(head_columns(width, head), queries, jnp.zeros_like(queries))
        scores = dense_last(keys_all, own) * HD ** (-0.5) + blocked
        top = jnp.max(scores, 0, keepdims=True)
        expo = jnp.exp(scores - top)
        total = jnp.sum(expo, 0, keepdims=True)
        lse_ref[head : head + 1, :] = top + jnp.log(total)
        result = dense(values_turned, to_low(expo / total))
        mine = (features >= head * HD) & (features < (head + 1) * HD)
        attended = jnp.where(mine, result, attended)
    attn_ref[...] = to_low(attended.T)


def attend(id_rows, pack, shard_in, width, bias, key_facts, row_facts, row_index):
    emb_width = id_rows.shape[1]
    model_width = pack.shape[0]
    length = key_facts.shape[0]
    count = row_index.shape[0]
    low = lambda *shape: jax.ShapeDtypeStruct(shape, jnp.bfloat16)
    full = lambda *shape: jax.ShapeDtypeStruct(shape, jnp.float32)
    return pl.pallas_call(
        functools.partial(attend_kernel, shard_in),
        out_shape=[
            low(length, model_width),
            full(count, model_width),
            low(count, emb_width),
            low(count, width),
            low(length, 2 * width),
            low(count, width),
            full(8, count),
            low(emb_width, model_width),
        ],
        compiler_params=pltpu.CompilerParams(vmem_limit_bytes=48 * 2**20),
        cost_estimate=pl.CostEstimate(
            flops=2 * length * model_width * (emb_width + 2 * width) + 4 * length * count * width,
            bytes_accessed=2 * length * (emb_width + model_width + 2 * width),
            transcendentals=length * count * width // HD,
        ),
    )(id_rows, pack, bias, key_facts, row_facts, row_index)


def attend_back_kernel(
    z_ref,
    proj_ref,
    query_ref,
    key_value_ref,
    lse_ref,
    key_ref,
    row_ref,
    pack_ref,
    in_ref,
    pre_ref,
    query_grad_ref,
    key_value_grad_ref,
    x_part_ref,
    row_part_ref,
    emb_part_ref,
):
    count, width = query_ref.shape
    length = key_value_ref.shape[0]
    slots = pre_ref.shape[0]
    share = pack_ref.shape[1] - 3 * width
    scale = HD ** (-0.5)
    queries = query_ref[...]
    keys_all = key_value_ref[:, :width]
    values_all = key_value_ref[:, width:]
    keys_turned = keys_all.T
    attn_grad = to_low(dense(z_ref[...], proj_ref[...]))
    blocked = jnp.where(visible_pairs(key_ref, row_ref), 0.0, -1e30)
    features = lax.broadcasted_iota(jnp.int32, (width, 1), 0)
    key_grad = jnp.zeros((length, width), jnp.float32)
    value_grad = jnp.zeros((length, width), jnp.float32)
    query_grad = jnp.zeros((width, count), jnp.float32)
    for head in range(width // HD):
        mine = head_columns(width, head)
        own = jnp.where(mine, queries, jnp.zeros_like(queries))
        own_grad = jnp.where(mine, attn_grad, jnp.zeros_like(attn_grad))
        scores = dense_last(keys_all, own) * scale + blocked
        probs = jnp.exp(scores - lse_ref[head : head + 1, :])
        probs_grad = dense_last(values_all, own_grad)
        rowdot = jnp.sum(probs * probs_grad, 0, keepdims=True)
        scores_grad = to_low(probs * (probs_grad - rowdot))
        value_grad += dense(to_low(probs), own_grad)
        key_grad += dense(scores_grad, own)
        rows = (features >= head * HD) & (features < (head + 1) * HD)
        query_grad = jnp.where(rows, dense(keys_turned, scores_grad), query_grad)
    query_grad = to_low((query_grad * scale).T)
    query_grad_ref[...] = query_grad
    key_value_grad_ref[:, :width] = to_low(key_grad * scale)
    key_value_grad_ref[:, width:] = to_low(value_grad)
    row_part = dense_last(query_grad, pack_ref[:, share : share + width])
    row_part_ref[:slots, :] = to_low(row_part[:slots] + pre_ref[...])
    row_part_ref[slots:, :] = to_low(row_part[slots:])
    row_emb = to_low(dense_last(row_part_ref[...], in_ref[...]))
    block = min(256, length)

    def one_block(index, carry):
        begin = pl.multiple_of(index * block, block)
        spot = pl.ds(begin, block)
        x_part = to_low(dense_last(key_value_grad_ref[spot, :], pack_ref[:, share + width :]))
        x_part_ref[spot, :] = x_part
        places = begin + lax.broadcasted_iota(jnp.int32, (block, 1), 0)
        chosen = (places == row_ref[4:5, :]).astype(jnp.bfloat16)
        emb_part_ref[spot, :] = to_low(dense_last(x_part, in_ref[...]) + dense(chosen, row_emb))
        return carry

    lax.fori_loop(0, length // block, one_block, 0)


def attend_back(
    z_rows, own_proj_t, queries, key_value, lse, key_facts, row_facts, pack, full_in, pre_grad
):
    count, width = queries.shape
    length = key_value.shape[0]
    emb_width, model_width = full_in.shape
    low = lambda *shape: jax.ShapeDtypeStruct(shape, jnp.bfloat16)
    return pl.pallas_call(
        attend_back_kernel,
        out_shape=[
            low(count, width),
            low(length, 2 * width),
            low(length, model_width),
            low(count, model_width),
            low(length, emb_width),
        ],
        compiler_params=pltpu.CompilerParams(vmem_limit_bytes=48 * 2**20),
        cost_estimate=pl.CostEstimate(
            flops=2 * length * model_width * (emb_width + 2 * width) + 10 * length * count * width,
            bytes_accessed=2 * length * (emb_width + model_width + 2 * width),
            transcendentals=length * count * width // HD,
        ),
    )(z_rows, own_proj_t, queries, key_value, lse, key_facts, row_facts, pack, full_in, pre_grad)


def lookup(codes, table_row):
    hits = codes[:, None] == jnp.arange(table_row.shape[0])[None, :]
    return jnp.sum(jnp.where(hits, table_row[None, :], 0), 1)


def after(values, *others):
    return lax.optimization_barrier((values, *others))[0]


def together(*values):
    return lax.optimization_barrier(values)


def columns_of(values, sizes):
    cuts = [sum(sizes[:i]) for i in range(len(sizes) + 1)]
    return [values[:, cuts[i] : cuts[i + 1]] for i in range(len(sizes))]


def advance(weight, moment, approx, rate):
    fresh_moment = momentum_decay * moment + approx
    return (weight - rate * fresh_moment, fresh_moment)


def per_device(
    tokens,
    segments,
    parents,
    completion,
    targets,
    table,
    table_moment,
    vectors,
    vector_moment,
    w_in,
    moment_in,
    error_in,
    factor_in,
    w_qkv,
    moment_qkv,
    error_qkv,
    factor_qkv,
    w_proj,
    moment_proj,
    error_proj,
    factor_proj,
    w_up,
    moment_up,
    error_up,
    factor_up,
    w_down,
    moment_down,
    error_down,
    factor_down,
    w_out,
    moment_out,
    error_out,
    factor_out,
):
    dp_count = lax.axis_size("dp")
    tensor_count = lax.axis_size("tensor")
    dp_index = lax.axis_index("dp")
    tensor_index = lax.axis_index("tensor")
    token_ids = tokens[0]
    comp_row = completion[0]
    target_row = targets[0]
    local_count = token_ids.shape[0]
    slots = comp_row.shape[0]
    segs = segments[0]
    length = segs.shape[0]
    shard_rows, emb_width = table.shape
    vocab_start = dp_index * shard_rows
    width = w_qkv.shape[2]
    hidden_share = w_up.shape[1]
    model_width = vectors.shape[1]
    heads_here = width // HD
    scale = HD ** (-0.5)
    shard_width = w_qkv.shape[0]
    blocks = range(tensor_count)

    halves = shard_width // w_in.shape[0]
    share_in = model_width // halves
    in_low = to_low(w_in)
    in_stack = jnp.concatenate(
        [in_low[:, h * share_in : (h + 1) * share_in] for h in range(halves)], 0
    )
    qkv_low = to_low(w_qkv).reshape(shard_width, 3 * width)
    pack_first = lax.all_gather(
        jnp.concatenate([in_stack, qkv_low], 1), "dp", axis=0, tiled=True
    )
    pack_second = lax.all_gather(
        jnp.concatenate([to_low(w_proj).T, to_low(w_up)], 1), "dp", axis=0, tiled=True
    )
    pack_third = lax.all_gather(
        jnp.concatenate([to_low(w_down).T, to_low(w_out)], 1), "dp", axis=0, tiled=True
    )
    full_proj_t = pack_second[:, :width]
    full_up = pack_second[:, width:]
    full_down_t = pack_third[:, :hidden_share]
    full_out = pack_third[:, hidden_share:]

    meta = jnp.stack(gather_blocks(jnp.concatenate([token_ids, comp_row, target_row]), "tensor"))
    comp_tree = meta[:, local_count : local_count + slots]
    ids = jnp.concatenate(
        [meta[:, :local_count].reshape(-1), meta[:, local_count + slots :].reshape(-1)]
    )

    id_count = ids.shape[0]
    share = -(-id_count // (16 * dp_count)) * 16
    owner = (ids // shard_rows) ^ dp_index
    order = jnp.arange(id_count)
    before = order[None, :] < order[:, None]
    same = ids[:, None] == ids[None, :]
    first_one = ~jnp.any(same & before, 1)
    rank = jnp.sum((owner[:, None] == owner[None, :]) & before & first_one[None, :], 1)
    rank = jnp.sum(jnp.where(same & first_one[None, :], rank[None, :], 0), 1)
    rounds_here = jnp.max(rank) // share + 1

    def listed(turn):
        place = rank - turn * share
        place = jnp.where((place >= 0) & (place < share), owner * share + place, -1)
        hits = place[None, :] == jnp.arange(dp_count * share)[:, None]
        entries = jnp.max(jnp.where(hits, ids[None, :], -1), 1)
        return hits.astype(jnp.bfloat16), entries.reshape(dp_count, share)

    def fetch(asked, kind):
        spots = jnp.clip(asked - vocab_start, 0, shard_rows - 1)
        picked = jnp.take(table, spots.reshape(-1), axis=0).astype(kind).reshape(dp_count, share, -1)
        return jnp.concatenate(exchange_blocks([picked[s] for s in range(dp_count)], "dp"), 0)

    hits_first, entries = listed(0)
    notes = [jnp.concatenate([entries[s], rounds_here[None]]) for s in range(dp_count)]
    notes = jnp.stack(exchange_blocks(notes, "dp"))
    asked_first = notes[:, :share]
    rounds = jnp.max(notes[:, share])

    def fetch_more(turn, rows):
        hits, entries = listed(turn)
        asked = jnp.stack(exchange_blocks([entries[s] for s in range(dp_count)], "dp"))
        return rows + to_low(dense_first(hits, to_low(coarse(fetch(asked, jnp.float32)))))

    id_rows = to_low(dense_first(hits_first, fetch(asked_first, jnp.bfloat16)))
    id_rows = lax.fori_loop(1, rounds, fetch_more, id_rows)
    emb_all = id_rows[:length]
    target_rows = id_rows[length : length + slots].astype(jnp.float32)

    starts = [(tensor_index ^ s) * local_count for s in blocks]
    key_spots = jnp.concatenate([start + jnp.arange(local_count) for start in starts])
    key_segs = jnp.concatenate([lax.dynamic_slice_in_dim(segs, a, local_count) for a in starts])
    slot_local = [
        jnp.clip(comp_tree[s] - starts[s], 0, local_count - 1) for s in blocks
    ]
    row_index = jnp.concatenate([s * local_count + slot_local[s] for s in blocks])
    row_spots = jnp.concatenate([starts[s] + slot_local[s] for s in blocks])
    chosen = row_index[:, None] == jnp.arange(length)[None, :]
    row_segs = jnp.sum(jnp.where(chosen, key_segs[None, :], 0), 1)
    row_first = lookup(row_segs, parents[0])
    row_second = lookup(row_first, parents[0])
    key_facts = jnp.stack([key_spots, key_segs], 1)
    row_facts = jnp.stack(
        [row_spots, row_segs, row_first, row_second, row_index] + [jnp.zeros_like(row_index)] * 3
    )
    bias_query = lax.dynamic_slice_in_dim(vectors[4], tensor_index * width, width)
    bias_value = lax.dynamic_slice_in_dim(vectors[5], tensor_index * width, width)
    bias = jnp.concatenate([bias_query, jnp.zeros_like(bias_query), bias_value])[None]
    x_low, x_rows, emb_rows, queries, key_value, attn_low, lse_keys, full_in = attend(
        id_rows, pack_first, w_in.shape[0], width, bias, key_facts, row_facts, row_index[:, None]
    )
    z_part = to_low(dense_last(attn_low, full_proj_t))
    z_branch = add_up(
        exchange_blocks([z_part[s * slots : (s + 1) * slots] for s in blocks], "tensor")
    )
    pre_one = x_rows[:slots] + z_branch + vectors[6]
    h_one = layer_norm(pre_one, vectors[0], vectors[1])
    h_rows = jnp.concatenate(gather_blocks(to_low(h_one), "tensor"), 0)
    bias_up = lax.dynamic_slice_in_dim(
        vectors[8:].reshape(-1), tensor_index * hidden_share, hidden_share
    )
    upper = dense(h_rows, full_up) + bias_up
    act_low = to_low(gelu_tanh(upper))
    f_part = to_low(dense_last(act_low, full_down_t))
    f_branch = add_up(
        exchange_blocks([f_part[s * slots : (s + 1) * slots] for s in blocks], "tensor")
    )
    pre_two = h_one + f_branch + vectors[7]
    h_two = layer_norm(pre_two, vectors[2], vectors[3])
    h_two_low = to_low(h_two)
    rows_low = to_low(dense(h_two_low, full_out))

    h_two_rows = gather_blocks(jnp.concatenate([h_two_low, rows_low], 1), "tensor")
    h_two_rows = jnp.concatenate(h_two_rows, 0)
    tree_rows = h_two_rows[:, model_width:]
    h_two_rows = h_two_rows[:, :model_width]
    rows_group = lax.all_gather(rows_low, "dp", axis=0, tiled=True)
    rows_group, tree_rows, h_two_rows = lax.optimization_barrier(
        (rows_group, tree_rows, h_two_rows)
    )
    parts = head_forward(rows_group, table)
    parts = lax.all_to_all(parts, "dp", 0, 0, tiled=True).reshape(dp_count, slots, -1)
    part_tops = join_low([parts[:, :, emb_width + i] for i in range(3)])
    part_sums = join_low([parts[:, :, emb_width + 3 + i] for i in range(3)])
    head_top = jnp.max(part_tops, 0)
    shares = jnp.exp(part_tops - head_top)
    total = jnp.sum(shares * part_sums, 0)
    lse = head_top + jnp.log(total)
    valid = comp_row >= 0
    target_logits = jnp.sum(rows_low.astype(jnp.float32) * target_rows, -1)
    loss_part = jnp.sum(jnp.where(valid, lse - target_logits, 0.0))
    slot_weight = 1.0 / (dp_count * tensor_count * slots)
    weight = jnp.where(valid, slot_weight, 0.0)
    mean = add_up(
        [parts[s, :, :emb_width] * (shares[s] / total)[:, None] for s in range(dp_count)]
    )
    out_low = to_low((mean - target_rows) * weight[:, None])

    shift = jnp.where(valid, lse - jnp.log(slot_weight), 1e30)
    shift = jnp.pad(jnp.stack(split_low(shift), 1), ((0, 0), (0, 125)))

    h_two_grad = dense_last(out_low, full_out)
    norm_two = jax.vjp(layer_norm, pre_two, vectors[2], vectors[3])[1]
    pre_two_grad, gain_two_grad, shift_two_grad = norm_two(h_two_grad)
    f_rows = gather_blocks(jnp.concatenate([to_low(pre_two_grad), shift], 1), "tensor")
    f_rows = jnp.concatenate(f_rows, 0)
    rows_all = lax.all_gather(
        jnp.concatenate([tree_rows, f_rows[:, model_width:]], 1), "dp", axis=0, tiled=True
    )
    shift_all = join_low([rows_all[:, emb_width + i] for i in range(3)])[None]
    f_rows = f_rows[:, :model_width]
    grad_down = dense_first(act_low, f_rows)
    act_grad = dense(f_rows, full_down_t)
    upper_low = to_low(jax.vjp(gelu_tanh, upper)[1](act_grad)[0])
    grad_up = dense_first(h_rows, upper_low)
    h_part = to_low(dense_last(upper_low, full_up))
    h_parts = exchange_blocks([h_part[s * slots : (s + 1) * slots] for s in blocks], "tensor")
    early = (3, 4)
    early_merged = [grad_up + error_up[0], grad_down + error_down[0]]
    early_lefts = [left_factor(*pair) for pair in zip(early_merged, (factor_up, factor_down[0]))]
    early_sizes = [left.shape[1] for left in early_lefts]
    early_lefts = jnp.concatenate(early_lefts, 1)
    h_parts[0], early_lefts = together(h_parts[0], early_lefts)
    h_one_grad = pre_two_grad + add_up(h_parts)
    norm_one = jax.vjp(layer_norm, pre_one, vectors[0], vectors[1])[1]
    pre_one_grad, gain_one_grad, shift_one_grad = norm_one(h_one_grad)
    z_low = to_low(pre_one_grad)
    z_rows = gather_blocks(jnp.concatenate([z_low, out_low], 1), "tensor")
    early_lefts = summed_over(early_lefts, "dp")
    z_rows[0], early_lefts = together(z_rows[0], early_lefts)
    z_rows = jnp.concatenate(z_rows, 0)
    grad_out = dense_first(h_two_rows, z_rows[:, model_width:])
    z_rows = z_rows[:, :model_width]
    grad_proj = dense_first(attn_low, z_rows)
    query_grad, key_value_grad, x_part, row_part, emb_part = attend_back(
        z_rows,
        full_proj_t,
        queries,
        key_value,
        lse_keys,
        key_facts,
        row_facts,
        pack_first,
        full_in,
        pre_one_grad,
    )
    x_rows_low = to_low(x_rows)
    value_grad = key_value_grad[:, width:]
    grad_query = dense_first(x_rows_low, query_grad)
    grad_key = dense_first(x_low, key_value_grad[:, :width])
    grad_value = dense_first(x_low, value_grad)

    grad_in = dense_first(emb_all, x_part) + dense_first(emb_rows, row_part)
    emb_parts = exchange_blocks(
        [emb_part[s * local_count : (s + 1) * local_count] for s in blocks], "tensor"
    )
    def placed(values, size, total_size):
        return lax.dynamic_update_slice_in_dim(
            jnp.zeros((total_size,), jnp.float32), values, tensor_index * size, 0
        )

    head_rows = jnp.stack(
        [
            gain_one_grad,
            shift_one_grad,
            gain_two_grad,
            shift_two_grad,
            placed(jnp.sum(query_grad.astype(jnp.float32), 0), width, model_width),
            placed(jnp.sum(value_grad.astype(jnp.float32), 0), width, model_width),
            jnp.sum(pre_one_grad, 0),
            jnp.sum(pre_two_grad, 0),
        ]
    )
    up_rows = placed(
        jnp.sum(upper_low.astype(jnp.float32), 0), hidden_share, hidden_share * tensor_count
    ).reshape(-1, model_width)
    loss_row = jnp.full((1, model_width), loss_part)
    vector_part = jnp.concatenate([head_rows, up_rows, loss_row], 0)

    merged = (
        grad_in + error_in[0] * (1.0 / tensor_count),
        None,
        grad_proj + error_proj[0],
    ) + tuple(early_merged) + (grad_out + error_out[0],)
    factors = (
        factor_in,
        factor_qkv.reshape(3 * width, -1),
        factor_proj[0],
        None,
        None,
        factor_out,
    )
    bases = [None] * 6
    fresh = [None] * 6
    parts_of = [None] * 6
    merged_qkv = [
        grad + error_qkv[0, :, part]
        for part, grad in enumerate((grad_query, grad_key, grad_value))
    ]
    late = (0, 1, 2, 5)
    lefts = [
        sum(left_factor(merged_qkv[part], factor_qkv[part]) for part in range(3))
        if index == 1
        else left_factor(merged[index], factors[index])
        for index in late
    ]
    sizes = [left.shape[1] for left in lefts] + [vector_part.size // lefts[0].shape[0]]
    lefts = jnp.concatenate(lefts + [vector_part.reshape(lefts[0].shape[0], -1)], 1)
    early_bases, early_terms = orthonormal_all(columns_of(early_lefts, early_sizes))
    early_rights = [right_factor(*pair) for pair in zip(early_merged, early_bases)]
    early_sizes = [right.shape[1] for right in early_rights]
    early_rights = jnp.concatenate(early_rights, 1)
    emb_parts[0], lefts, early_rights = together(emb_parts[0], lefts, early_rights)
    emb_grad_own = to_low(add_up(emb_parts))
    emb_grad = gather_blocks(emb_grad_own, "tensor")
    lefts = summed_over(lefts, "dp")
    early_rights = summed_over(early_rights, "dp")
    emb_grad[0], lefts, early_rights = together(emb_grad[0], lefts, early_rights)
    emb_grad = jnp.concatenate(emb_grad, 0)
    early_parts = columns_of(outer_terms(early_rights), early_sizes)
    early_rights = columns_of(early_rights, early_sizes)

    def error_left(index):
        return merged[index] - dense_first(bases[index], parts_of[index]) * (1.0 / dp_count)

    errors_new = [None] * 6
    for i, index in enumerate(early):
        bases[index] = early_terms[i]
        fresh[index] = early_rights[i]
        parts_of[index] = early_parts[i]
        errors_new[index] = error_left(index)
    lefts = columns_of(lefts, sizes)
    flat = after(jnp.concatenate([lefts[0], lefts[-1]], 1), emb_grad)
    flat = add_pairs(gather_blocks(flat, "tensor"))
    lefts[0] = flat[:, : sizes[0]]
    vector_sum = flat[:, sizes[0] :].reshape(vector_part.shape)
    found_bases, found_terms = orthonormal_all(lefts[:-1])
    rights = [
        jnp.concatenate([right_factor(merged_qkv[part], found_bases[i]) for part in range(3)], 1)
        if index == 1
        else right_factor(merged[index], found_bases[i])
        for i, index in enumerate(late)
    ]
    sizes = [right.shape[1] for right in rights]
    rights = summed_over(jnp.concatenate(rights, 1), "dp")
    grad_in_own = lax.psum_scatter(
        after(to_low(grad_in), emb_grad), "tensor", scatter_dimension=0, tiled=True
    )
    tree_weight = jnp.where(comp_tree.reshape(-1) >= 0, slot_weight, 0.0)
    target_grad = to_low(tree_rows.astype(jnp.float32) * -tree_weight[:, None])
    id_grad = jnp.concatenate([emb_grad, target_grad], 0)

    def deliver(hits):
        listed_rows = to_low(dense(hits, id_grad)).reshape(dp_count, share, -1)
        rows = exchange_blocks([listed_rows[s] for s in range(dp_count)], "dp")
        return jnp.concatenate(rows, 0)

    def deliver_more(turn, state):
        hits, entries = listed(turn)
        asked = jnp.stack(exchange_blocks([entries[s] for s in range(dp_count)], "dp"))
        spots = asked.reshape(-1) - vocab_start
        rows = deliver(hits).astype(jnp.float32)
        rows = jnp.where((spots >= 0)[:, None], rows, 0.0)
        spots = jnp.clip(spots, 0, shard_rows - 1)
        return state[0].at[spots].add(-table_rate * rows), state[1].at[spots].add(rows)

    added, rights, errors_new[3], errors_new[4], grad_in_own = together(
        deliver(hits_first), rights, errors_new[3], errors_new[4], grad_in_own
    )
    updated = list(table_update(
        rows_all, shift_all, added, asked_first.reshape(1, -1) - vocab_start, table, table_moment
    ))
    right_in = gather_blocks(rights[:, : sizes[0]], "tensor")
    grad_in_sum = lax.all_gather(grad_in_own, "tensor", axis=0, tiled=True)
    right_in[0], updated[0] = together(right_in[0], updated[0])
    new_table, new_table_moment = lax.fori_loop(1, rounds, deliver_more, tuple(updated))
    rights = columns_of(rights, sizes)
    rights[0] = add_pairs(right_in)
    right_parts = columns_of(outer_terms(jnp.concatenate(rights, 1)), sizes)
    for i, index in enumerate(late):
        bases[index] = found_terms[i]
        fresh[index] = rights[i]
        parts_of[index] = right_parts[i]
    merged = (grad_in_sum.astype(jnp.float32) + error_in[0],) + merged[1:]
    for index in (0, 2, 5):
        errors_new[index] = error_left(index)
    errors_new[1] = jnp.stack(
        [
            merged_qkv[part]
            - dense_first(bases[1], parts_of[1][:, part * width : (part + 1) * width])
            * (1.0 / dp_count)
            for part in range(3)
        ],
        0,
    ).transpose(1, 0, 2)

    def shard(index, size, axis):
        left, right = bases[index], parts_of[index]
        if axis == 0:
            left = lax.dynamic_slice_in_dim(left, dp_index * size, size, 1)
        else:
            right = lax.dynamic_slice_in_dim(right, dp_index * size, size, 1)
        return dense_first(left, right)

    shard_in = shard(0, w_in.shape[0], 0)
    shard_qkv = shard(1, shard_width, 0)
    shard_qkv = jnp.stack(
        [shard_qkv[:, part * width : (part + 1) * width] for part in range(3)], 1
    )
    shard_proj = shard(2, w_proj.shape[1], 1)
    shard_up = shard(3, w_up.shape[0], 0)
    shard_down = shard(4, w_down.shape[1], 1)
    shard_out = shard(5, w_out.shape[0], 0)
    fresh = [values.T for values in fresh]
    loss_sum = vector_sum[-1, 0]
    vector_grad = vector_sum[:-1]
    new_w_in, new_moment_in = advance(w_in, moment_in, shard_in, matrix_rates[0])
    new_w_qkv, new_moment_qkv = advance(w_qkv, moment_qkv, shard_qkv, matrix_rates[1])
    new_w_proj, new_moment_proj = advance(w_proj, moment_proj, shard_proj, matrix_rates[2])
    new_w_up, new_moment_up = advance(w_up, moment_up, shard_up, matrix_rates[3])
    new_w_down, new_moment_down = advance(w_down, moment_down, shard_down, matrix_rates[4])
    new_w_out, new_moment_out = advance(w_out, moment_out, shard_out, matrix_rates[5])
    new_vectors, new_vector_moment = advance(vectors, vector_moment, vector_grad, vector_rate)
    return (
        loss_sum,
        new_table,
        new_table_moment,
        new_vectors,
        new_vector_moment,
        new_w_in,
        new_moment_in,
        errors_new[0][None],
        fresh[0],
        new_w_qkv,
        new_moment_qkv,
        errors_new[1].reshape(1, model_width, 3, width),
        fresh[1].reshape(3, width, -1),
        new_w_proj,
        new_moment_proj,
        errors_new[2][None],
        fresh[2][None],
        new_w_up,
        new_moment_up,
        errors_new[3][None],
        fresh[3],
        new_w_down,
        new_moment_down,
        errors_new[4][None],
        fresh[4][None],
        new_w_out,
        new_moment_out,
        errors_new[5][None],
        fresh[5],
    )


def solution(mesh):
    return jax.shard_map(
        per_device,
        mesh=mesh,
        in_specs=(
            P("dp", "tensor"),
            P("dp", None),
            P("dp", None),
            P("dp", "tensor"),
            P("dp", "tensor"),
            P("dp", None),
            P("dp", None),
            P(),
            P(),
            P("dp", None),
            P("dp", None),
            P("dp", None, None),
            P(),
            P("dp", None, "tensor"),
            P("dp", None, "tensor"),
            P("dp", None, None, "tensor"),
            P(None, "tensor", None),
            P("tensor", "dp"),
            P("tensor", "dp"),
            P("dp", "tensor", None),
            P("tensor", None, None),
            P("dp", "tensor"),
            P("dp", "tensor"),
            P("dp", None, "tensor"),
            P("tensor", None),
            P("tensor", "dp"),
            P("tensor", "dp"),
            P("dp", "tensor", None),
            P("tensor", None, None),
            P("dp", None),
            P("dp", None),
            P("dp", None, None),
            P(),
        ),
        out_specs=(
            P(),
            P("dp", None),
            P("dp", None),
            P(),
            P(),
            P("dp", None),
            P("dp", None),
            P("dp", None, None),
            P(),
            P("dp", None, "tensor"),
            P("dp", None, "tensor"),
            P("dp", None, None, "tensor"),
            P(None, "tensor", None),
            P("tensor", "dp"),
            P("tensor", "dp"),
            P("dp", "tensor", None),
            P("tensor", None, None),
            P("dp", "tensor"),
            P("dp", "tensor"),
            P("dp", None, "tensor"),
            P("tensor", None),
            P("tensor", "dp"),
            P("tensor", "dp"),
            P("dp", "tensor", None),
            P("tensor", None, None),
            P("dp", None),
            P("dp", None),
            P("dp", None, None),
            P(),
        ),
        check_vma=False,
    )
```

```python
import functools

import jax
import jax.numpy as jnp
from jax import lax
from jax.experimental import pallas as pl
from jax.experimental.pallas import tpu as pltpu
from jax.sharding import PartitionSpec as P

HD = 64


momentum_decay = 0.9
table_rate = 300.0
vector_rate = 1000.0
matrix_rates = (1500.0, 80.0, 3000.0, 80.0, 40.0, 80.0)


def to_low(values):
    return values.astype(jnp.bfloat16)


def dense(left, right):
    return jnp.dot(left, right, preferred_element_type=jnp.float32)


def dense_first(left, right):
    return lax.dot_general(
        left, right, (((0,), (0,)), ((), ())), preferred_element_type=jnp.float32
    )


def dense_last(left, right):
    return lax.dot_general(
        left, right, (((1,), (1,)), ((), ())), preferred_element_type=jnp.float32
    )


left_terms = (0, 0, 1, 1, 0, 2)
right_terms = (0, 1, 0, 1, 2, 0)


def two_terms(values, axis):
    first = coarse(values)
    return to_low(jnp.concatenate([first, values - first], axis))


def left_factor(merged, factor):
    count = factor.shape[1]
    both = lax.dot_general(
        two_terms(factor, 1),
        to_low(merged),
        (((0,), (1,)), ((), ())),
        preferred_element_type=jnp.float32,
    )
    return both[:count] + both[count:]


def right_factor(merged, basis):
    both = dense(two_terms(basis, 0), to_low(merged))
    return both[: basis.shape[0]] + both[basis.shape[0] :]


def layer_norm(values, gain, shift):
    center = values - jnp.mean(values, -1, keepdims=True)
    spread = jnp.mean(center * center, -1, keepdims=True)
    return center * lax.rsqrt(spread + 1e-05) * gain + shift


def gelu_tanh(values):
    return jax.nn.gelu(values, approximate=True)


def swap(values, axis, step):
    return lax.ppermute(values, axis, [(i, i ^ step) for i in range(lax.axis_size(axis))])


def gather_blocks(values, axis):
    return [values] + [swap(values, axis, s) for s in range(1, lax.axis_size(axis))]


def exchange_blocks(blocks, axis):
    return [blocks[0]] + [swap(blocks[s], axis, s) for s in range(1, lax.axis_size(axis))]


def summed_over(values, axis, step=1):
    while step < lax.axis_size(axis):
        values = jax.tree.map(lambda a, s=step: a + swap(a, axis, s), values)
        step *= 2
    return values


def add_up(parts):
    total = parts[0].astype(jnp.float32)
    for part in parts[1:]:
        total = total + part.astype(jnp.float32)
    return total


def add_pairs(parts):
    while len(parts) > 1:
        parts = [left + right for left, right in zip(parts[::2], parts[1::2])]
    return parts[0]


def orthonormal_kernel(*refs):
    many = len(refs) // 3
    left_refs, basis_refs, term_refs = refs[:many], refs[many : 2 * many], refs[2 * many :]
    count = left_refs[0].shape[0]
    longest = max(ref.shape[1] for ref in left_refs)

    def row(ref, index):
        values = ref[index : index + 1, :]
        short = longest - values.shape[1]
        if short == 0:
            return values
        return jnp.concatenate([values, jnp.zeros((1, short), jnp.float32)], 1)

    columns = [jnp.concatenate([row(ref, k) for ref in left_refs], 0) for k in range(count)]
    for index in range(count):
        vector = columns[index]
        vector = vector * lax.rsqrt(jnp.sum(vector * vector, -1, keepdims=True) + 1e-06)
        for place, ref in enumerate(basis_refs):
            ref[index : index + 1, :] = vector[place : place + 1, : ref.shape[1]]
        for later in range(index + 1, count):
            other = columns[later]
            columns[later] = other - jnp.sum(vector * other, -1, keepdims=True) * vector
    for basis_ref, term_ref in zip(basis_refs, term_refs):
        rest = basis_ref[...]
        terms = []
        for _ in range(3):
            terms.append(rest.astype(jnp.bfloat16).astype(jnp.float32))
            rest = rest - terms[-1]
        term_ref[...] = jnp.concatenate([terms[term] for term in left_terms], 0).astype(
            jnp.bfloat16
        )


def orthonormal_all(lefts):
    count = lefts[0].shape[0]
    bases = [jax.ShapeDtypeStruct(left.shape, jnp.float32) for left in lefts]
    terms = [
        jax.ShapeDtypeStruct((len(left_terms) * count, left.shape[1]), jnp.bfloat16)
        for left in lefts
    ]
    both = pl.pallas_call(orthonormal_kernel, out_shape=bases + terms)(*lefts)
    return both[: len(lefts)], both[len(lefts) :]


def outer_terms(rights):
    terms = split_low(rights)
    return jnp.concatenate([terms[term] for term in right_terms], 0)


def coarse(values):
    return lax.reduce_precision(values, 8, 7)


def split_low(values):
    first = coarse(values)
    second = coarse(values - first)
    return [to_low(first), to_low(second), to_low(values - first - second)]


def join_low(terms):
    terms = [term.astype(jnp.float32) for term in terms]
    return terms[0] + (terms[1] + terms[2])


def vocab_tile(shard_rows, most=640):
    tiles = -(-shard_rows // most)
    return -(-(-(-shard_rows // tiles)) // 16) * 16


def head_kernel(shard_rows, rows_ref, table_ref, out_ref, total, stats):
    step = pl.program_id(0)
    tile_rows, wide = table_ref.shape

    @pl.when(step == 0)
    def _():
        total[...] = jnp.zeros_like(total)
        stats[0:1, :] = jnp.full((1, stats.shape[1]), -1e30, jnp.float32)
        stats[1:2, :] = jnp.zeros((1, stats.shape[1]), jnp.float32)

    row_ids = step * tile_rows + lax.broadcasted_iota(jnp.int32, (tile_rows, 1), 0)
    present = row_ids < shard_rows
    tile = jnp.where(present, table_ref[...], 0.0).astype(jnp.bfloat16)
    logits = lax.dot_general(
        tile, rows_ref[...], (((1,), (1,)), ((), ())), preferred_element_type=jnp.float32
    )
    logits = jnp.where(present, logits, -1e30)
    before = stats[0:1, :]
    top = jnp.maximum(before, jnp.max(logits, 0, keepdims=True))
    fade = jnp.exp(before - top)
    expo = jnp.exp(logits - top)
    stats[0:1, :] = top
    stats[1:2, :] = stats[1:2, :] * fade + jnp.sum(expo, 0, keepdims=True)
    total[...] = total[...] * fade + lax.dot_general(
        tile,
        expo.astype(jnp.bfloat16),
        (((0,), (0,)), ((), ())),
        preferred_element_type=jnp.float32,
    )

    @pl.when(step == pl.num_programs(0) - 1)
    def _():
        out_ref[:, :wide] = total[...].T.astype(jnp.bfloat16)
        terms = []
        for index in (0, 1):
            value = stats[index : index + 1, :]
            for _ in range(3):
                part = value.astype(jnp.bfloat16).astype(jnp.float32)
                terms.append(part)
                value = value - part
        spare = jnp.zeros((out_ref.shape[1] - wide - 6, value.shape[1]), jnp.float32)
        out_ref[:, wide:] = jnp.concatenate(terms + [spare], 0).T.astype(jnp.bfloat16)


def head_forward(rows, table):
    count, wide = rows.shape
    shard_rows = table.shape[0]
    tile = vocab_tile(shard_rows, 1280 if count <= 1024 else 640)
    return pl.pallas_call(
        functools.partial(head_kernel, shard_rows),
        grid=(pl.cdiv(shard_rows, tile),),
        in_specs=[
            pl.BlockSpec((count, wide), lambda i: (0, 0)),
            pl.BlockSpec((tile, wide), lambda i: (i, 0)),
        ],
        out_specs=pl.BlockSpec((count, wide + 128), lambda i: (0, 0)),
        out_shape=jax.ShapeDtypeStruct((count, wide + 128), jnp.bfloat16),
        scratch_shapes=[
            pltpu.VMEM((wide, count), jnp.float32),
            pltpu.VMEM((8, count), jnp.float32),
        ],
        compiler_params=pltpu.CompilerParams(vmem_limit_bytes=56 * 2**20),
        cost_estimate=pl.CostEstimate(
            flops=4 * shard_rows * count * wide,
            bytes_accessed=4 * shard_rows * wide,
            transcendentals=shard_rows * count,
        ),
    )(rows, table)


def table_kernel(rows_ref, shift_ref, ids_ref, table_ref, moment_ref, *refs):
    parts, (new_table_ref, new_moment_ref, added_ref) = refs[:-3], refs[-3:]
    tile_rows, wide = table_ref.shape

    @pl.when(pl.program_id(0) == 0)
    def _():
        for index, part in enumerate(parts):
            count = part.shape[0]
            added_ref[index * count : (index + 1) * count, :] = part[...]

    row_ids = pl.program_id(0) * tile_rows
    row_ids = row_ids + lax.broadcasted_iota(jnp.int32, (tile_rows, 1), 0)
    hits = (row_ids == ids_ref[...]).astype(jnp.bfloat16)
    new_moment_ref[...] = momentum_decay * moment_ref[...] + dense(hits, added_ref[...])
    tile = table_ref[...].astype(jnp.bfloat16)
    chunk = min(512, rows_ref.shape[0])

    def one(spot):
        rows = rows_ref[spot, :]
        grad = jnp.exp(dense_last(tile, rows) - shift_ref[0:1, spot])
        return dense(grad.astype(jnp.bfloat16), rows)

    together = 4 * chunk if rows_ref.shape[0] % (4 * chunk) == 0 else chunk

    def some(index, carry):
        begin = pl.multiple_of(index * together, together)
        parts = [one(pl.ds(begin + k * chunk, chunk)) for k in range(together // chunk)]
        new_moment_ref[...] += sum(parts[1:], parts[0])
        return carry

    if rows_ref.shape[0] == together:
        some(0, 0)
    else:
        lax.fori_loop(0, rows_ref.shape[0] // together, some, 0)
    new_table_ref[...] = table_ref[...] - table_rate * new_moment_ref[...]


def table_update(rows, shift, added, ids, table, moment):
    shard_rows, wide = table.shape
    tile = vocab_tile(shard_rows)
    whole = lambda array: pl.BlockSpec(
        array.shape, lambda i: (0, 0), pipeline_mode=pl.Buffered(buffer_count=1)
    )
    part = pl.BlockSpec((tile, wide), lambda i: (i, 0))
    return pl.pallas_call(
        table_kernel,
        grid=(pl.cdiv(shard_rows, tile),),
        in_specs=[whole(rows), whole(shift), whole(ids), part, part] + [whole(a) for a in added],
        out_specs=[part, part],
        out_shape=[jax.ShapeDtypeStruct(table.shape, jnp.float32)] * 2,
        scratch_shapes=[pltpu.VMEM((ids.shape[1], wide), jnp.bfloat16)],
        compiler_params=pltpu.CompilerParams(vmem_limit_bytes=56 * 2**20),
        cost_estimate=pl.CostEstimate(
            flops=shard_rows * wide * (4 * rows.shape[0] + 2 * ids.shape[1]),
            bytes_accessed=16 * shard_rows * wide,
            transcendentals=shard_rows * rows.shape[0],
        ),
    )(rows, shift, ids, table, moment, *added)


def visible_pairs(key_ref, row_ref):
    spots, segs = key_ref[:, 0:1], key_ref[:, 1:2]
    related = (segs == row_ref[1:2, :]) | (segs == row_ref[2:3, :]) | (segs == row_ref[3:4, :])
    return related & (spots <= row_ref[0:1, :])


def head_columns(width, head):
    columns = lax.broadcasted_iota(jnp.int32, (1, width), 1)
    return (columns >= head * HD) & (columns < (head + 1) * HD)


def attend_kernel(
    shard_in,
    emb_ref,
    pack_ref,
    bias_ref,
    key_ref,
    row_ref,
    index_ref,
    x_ref,
    x_rows_ref,
    emb_rows_ref,
    query_ref,
    key_value_ref,
    attn_ref,
    lse_ref,
    in_ref,
):
    length = x_ref.shape[0]
    count, width = query_ref.shape
    block = min(256, length)
    share = pack_ref.shape[1] - 4 * width
    halves = in_ref.shape[1] // share
    for owner in range(in_ref.shape[0] // shard_in):
        for part in range(halves):
            begin = (owner * halves + part) * shard_in
            in_ref[owner * shard_in : (owner + 1) * shard_in, part * share : (part + 1) * share] = (
                pack_ref[begin : begin + shard_in, :share]
            )

    def one_block(index, carry):
        spot = pl.ds(pl.multiple_of(index * block, block), block)
        x_low = to_low(dense(emb_ref[spot, :], in_ref[...]))
        x_ref[spot, :] = x_low
        mixed = dense(x_low, pack_ref[:, share + width : share + 3 * width]) + bias_ref[:, width:]
        key_value_ref[spot, :] = to_low(mixed)
        return carry

    lax.fori_loop(0, length // block, one_block, 0)
    chosen = index_ref[...] == lax.broadcasted_iota(jnp.int32, (count, length), 1)
    emb_rows = to_low(dense(chosen.astype(jnp.bfloat16), emb_ref[:length, :]))
    emb_rows_ref[...] = emb_rows
    x_rows = dense(emb_rows, in_ref[...])
    x_rows_ref[...] = x_rows
    queries = to_low(dense(to_low(x_rows), pack_ref[:, share : share + width]) + bias_ref[:, :width])
    query_ref[...] = queries
    keys_all = key_value_ref[:, :width]
    values_turned = key_value_ref[:, width:].T
    blocked = jnp.where(visible_pairs(key_ref, row_ref), 0.0, -1e30)
    features = lax.broadcasted_iota(jnp.int32, (width, 1), 0)
    attended = jnp.zeros((width, count), jnp.float32)
    for head in range(width // HD):
        own = jnp.where(head_columns(width, head), queries, jnp.zeros_like(queries))
        scores = dense_last(keys_all, own) * HD ** (-0.5) + blocked
        top = jnp.max(scores, 0, keepdims=True)
        expo = jnp.exp(scores - top)
        total = jnp.sum(expo, 0, keepdims=True)
        lse_ref[head : head + 1, :] = top + jnp.log(total)
        result = dense(values_turned, to_low(expo / total))
        mine = (features >= head * HD) & (features < (head + 1) * HD)
        attended = jnp.where(mine, result, attended)
    attn_ref[...] = to_low(attended.T)


def attend(id_rows, pack, shard_in, width, bias, key_facts, row_facts, row_index):
    emb_width = id_rows.shape[1]
    model_width = pack.shape[0]
    length = key_facts.shape[0]
    count = row_index.shape[0]
    low = lambda *shape: jax.ShapeDtypeStruct(shape, jnp.bfloat16)
    full = lambda *shape: jax.ShapeDtypeStruct(shape, jnp.float32)
    return pl.pallas_call(
        functools.partial(attend_kernel, shard_in),
        out_shape=[
            low(length, model_width),
            full(count, model_width),
            low(count, emb_width),
            low(count, width),
            low(length, 2 * width),
            low(count, width),
            full(8, count),
            low(emb_width, model_width),
        ],
        compiler_params=pltpu.CompilerParams(vmem_limit_bytes=48 * 2**20),
        cost_estimate=pl.CostEstimate(
            flops=2 * length * model_width * (emb_width + 2 * width) + 4 * length * count * width,
            bytes_accessed=2 * length * (emb_width + model_width + 2 * width),
            transcendentals=length * count * width // HD,
        ),
    )(id_rows, pack, bias, key_facts, row_facts, row_index)


def attend_back_kernel(
    z_ref,
    proj_ref,
    query_ref,
    key_value_ref,
    lse_ref,
    key_ref,
    row_ref,
    pack_ref,
    in_ref,
    pre_ref,
    query_grad_ref,
    key_value_grad_ref,
    x_part_ref,
    row_part_ref,
    emb_part_ref,
):
    count, width = query_ref.shape
    length = key_value_ref.shape[0]
    slots = pre_ref.shape[0]
    share = pack_ref.shape[1] - 4 * width
    scale = HD ** (-0.5)
    queries = query_ref[...]
    keys_all = key_value_ref[:, :width]
    values_all = key_value_ref[:, width:]
    keys_turned = keys_all.T
    attn_grad = to_low(dense(z_ref[...], proj_ref[...]))
    blocked = jnp.where(visible_pairs(key_ref, row_ref), 0.0, -1e30)
    features = lax.broadcasted_iota(jnp.int32, (width, 1), 0)
    key_grad = jnp.zeros((length, width), jnp.float32)
    value_grad = jnp.zeros((length, width), jnp.float32)
    query_grad = jnp.zeros((width, count), jnp.float32)
    for head in range(width // HD):
        mine = head_columns(width, head)
        own = jnp.where(mine, queries, jnp.zeros_like(queries))
        own_grad = jnp.where(mine, attn_grad, jnp.zeros_like(attn_grad))
        scores = dense_last(keys_all, own) * scale + blocked
        probs = jnp.exp(scores - lse_ref[head : head + 1, :])
        probs_grad = dense_last(values_all, own_grad)
        rowdot = jnp.sum(probs * probs_grad, 0, keepdims=True)
        scores_grad = to_low(probs * (probs_grad - rowdot))
        value_grad += dense(to_low(probs), own_grad)
        key_grad += dense(scores_grad, own)
        rows = (features >= head * HD) & (features < (head + 1) * HD)
        query_grad = jnp.where(rows, dense(keys_turned, scores_grad), query_grad)
    query_grad = to_low((query_grad * scale).T)
    query_grad_ref[...] = query_grad
    key_value_grad_ref[:, :width] = to_low(key_grad * scale)
    key_value_grad_ref[:, width:] = to_low(value_grad)
    row_part = dense_last(query_grad, pack_ref[:, share : share + width])
    row_part_ref[:slots, :] = to_low(row_part[:slots] + pre_ref[...])
    row_part_ref[slots:, :] = to_low(row_part[slots:])
    row_emb = to_low(dense_last(row_part_ref[...], in_ref[...]))
    block = min(256, length)

    def one_block(index, carry):
        begin = pl.multiple_of(index * block, block)
        spot = pl.ds(begin, block)
        x_part = to_low(dense_last(key_value_grad_ref[spot, :], pack_ref[:, share + width : share + 3 * width]))
        x_part_ref[spot, :] = x_part
        places = begin + lax.broadcasted_iota(jnp.int32, (block, 1), 0)
        chosen = (places == row_ref[4:5, :]).astype(jnp.bfloat16)
        emb_part_ref[spot, :] = to_low(dense_last(x_part, in_ref[...]) + dense(chosen, row_emb))
        return carry

    lax.fori_loop(0, length // block, one_block, 0)


def attend_back(
    z_rows, own_proj_t, queries, key_value, lse, key_facts, row_facts, pack, full_in, pre_grad
):
    count, width = queries.shape
    length = key_value.shape[0]
    emb_width, model_width = full_in.shape
    low = lambda *shape: jax.ShapeDtypeStruct(shape, jnp.bfloat16)
    return pl.pallas_call(
        attend_back_kernel,
        out_shape=[
            low(count, width),
            low(length, 2 * width),
            low(length, model_width),
            low(count, model_width),
            low(length, emb_width),
        ],
        compiler_params=pltpu.CompilerParams(vmem_limit_bytes=48 * 2**20),
        cost_estimate=pl.CostEstimate(
            flops=2 * length * model_width * (emb_width + 2 * width) + 10 * length * count * width,
            bytes_accessed=2 * length * (emb_width + model_width + 2 * width),
            transcendentals=length * count * width // HD,
        ),
    )(z_rows, own_proj_t, queries, key_value, lse, key_facts, row_facts, pack, full_in, pre_grad)


def lookup(codes, table_row):
    hits = codes[:, None] == jnp.arange(table_row.shape[0])[None, :]
    return jnp.sum(jnp.where(hits, table_row[None, :], 0), 1)


def after(values, *others):
    return lax.optimization_barrier((values, *others))[0]


def together(*values):
    return lax.optimization_barrier(values)


def columns_of(values, sizes):
    cuts = [sum(sizes[:i]) for i in range(len(sizes) + 1)]
    return [values[:, cuts[i] : cuts[i + 1]] for i in range(len(sizes))]


def advance(weight, moment, approx, rate):
    fresh_moment = momentum_decay * moment + approx
    return (weight - rate * fresh_moment, fresh_moment)


def per_device(
    tokens,
    segments,
    parents,
    completion,
    targets,
    table,
    table_moment,
    vectors,
    vector_moment,
    w_in,
    moment_in,
    error_in,
    factor_in,
    w_qkv,
    moment_qkv,
    error_qkv,
    factor_qkv,
    w_proj,
    moment_proj,
    error_proj,
    factor_proj,
    w_up,
    moment_up,
    error_up,
    factor_up,
    w_down,
    moment_down,
    error_down,
    factor_down,
    w_out,
    moment_out,
    error_out,
    factor_out,
):
    dp_count = lax.axis_size("dp")
    tensor_count = lax.axis_size("tensor")
    dp_index = lax.axis_index("dp")
    tensor_index = lax.axis_index("tensor")
    token_ids = tokens[0]
    comp_row = completion[0]
    target_row = targets[0]
    local_count = token_ids.shape[0]
    slots = comp_row.shape[0]
    segs = segments[0]
    length = segs.shape[0]
    shard_rows, emb_width = table.shape
    vocab_start = dp_index * shard_rows
    width = w_qkv.shape[2]
    hidden_share = w_up.shape[1]
    model_width = vectors.shape[1]
    heads_here = width // HD
    scale = HD ** (-0.5)
    shard_width = w_qkv.shape[0]
    blocks = range(tensor_count)

    meta = gather_blocks(jnp.concatenate([token_ids, comp_row, target_row]), "tensor")

    halves = shard_width // w_in.shape[0]
    share_in = model_width // halves
    in_low = to_low(w_in)
    in_stack = jnp.concatenate(
        [in_low[:, h * share_in : (h + 1) * share_in] for h in range(halves)], 0
    )
    qkv_low = to_low(w_qkv).reshape(shard_width, 3 * width)
    pack_first = lax.all_gather(
        jnp.concatenate([in_stack, qkv_low, to_low(w_proj).T], 1), "dp", axis=0, tiled=True
    )
    pack_rest = lax.all_gather(
        jnp.concatenate([to_low(w_up), to_low(w_down).T, to_low(w_out)], 1),
        "dp",
        axis=0,
        tiled=True,
    )
    full_proj_t = pack_first[:, share_in + 3 * width :]
    full_up = pack_rest[:, :hidden_share]
    full_down_t = pack_rest[:, hidden_share : 2 * hidden_share]
    full_out = pack_rest[:, 2 * hidden_share :]

    meta = jnp.stack(meta)
    comp_tree = meta[:, local_count : local_count + slots]
    ids = jnp.concatenate(
        [meta[:, :local_count].reshape(-1), meta[:, local_count + slots :].reshape(-1)]
    )

    id_count = ids.shape[0]
    share = -(-9 * id_count // (160 * dp_count)) * 16
    owner = ids // shard_rows
    order = jnp.arange(id_count)
    before = order[None, :] < order[:, None]
    same = ids[:, None] == ids[None, :]
    first_one = ~jnp.any(same & before, 1)
    rank = jnp.sum((owner[:, None] == owner[None, :]) & before & first_one[None, :], 1)
    rank = jnp.sum(jnp.where(same & first_one[None, :], rank[None, :], 0), 1)
    rounds_here = jnp.max(rank) // share + 1

    def listed(turn, owners):
        place = rank - turn * share
        place = jnp.where((place >= 0) & (place < share), owners * share + place, -1)
        return place[None, :] == jnp.arange(dp_count * share)[:, None]

    def entries_of(hits):
        return jnp.max(jnp.where(hits, ids[None, :], -1), 1).reshape(dp_count, share)

    def picked_rows(asked, kind):
        spots = jnp.clip(asked - vocab_start, 0, shard_rows - 1)
        return jnp.take(table, spots.reshape(-1), axis=0).astype(kind).reshape(dp_count, share, -1)

    def exchanged(values):
        return lax.all_to_all(values, "dp", 0, 0, tiled=True)

    hits_first = listed(0, owner ^ dp_index)
    entries = entries_of(hits_first)
    hits_first = hits_first.astype(jnp.bfloat16)
    notes = [jnp.concatenate([entries[s], rounds_here[None]]) for s in range(dp_count)]
    notes = jnp.stack(exchange_blocks(notes, "dp"))
    asked_first = notes[:, :share]
    rounds = jnp.max(notes[:, share])

    def fetch_more(turn, rows):
        hits = listed(turn, owner)
        found = exchanged(picked_rows(exchanged(entries_of(hits)), jnp.float32))
        found = to_low(coarse(found.reshape(dp_count * share, -1)))
        return rows + to_low(dense_first(hits.astype(jnp.bfloat16), found))

    found = picked_rows(asked_first, jnp.bfloat16)
    found = exchange_blocks([found[s] for s in range(dp_count)], "dp")
    id_rows = to_low(dense_first(hits_first, jnp.concatenate(found, 0)))
    id_rows = lax.fori_loop(1, rounds, fetch_more, id_rows)
    emb_all = id_rows[:length]
    target_rows = id_rows[length : length + slots].astype(jnp.float32)

    starts = [(tensor_index ^ s) * local_count for s in blocks]
    key_spots = jnp.concatenate([start + jnp.arange(local_count) for start in starts])
    key_segs = jnp.concatenate([lax.dynamic_slice_in_dim(segs, a, local_count) for a in starts])
    slot_local = [
        jnp.clip(comp_tree[s] - starts[s], 0, local_count - 1) for s in blocks
    ]
    row_index = jnp.concatenate([s * local_count + slot_local[s] for s in blocks])
    row_spots = jnp.concatenate([starts[s] + slot_local[s] for s in blocks])
    chosen = row_index[:, None] == jnp.arange(length)[None, :]
    row_segs = jnp.sum(jnp.where(chosen, key_segs[None, :], 0), 1)
    row_first = lookup(row_segs, parents[0])
    row_second = lookup(row_first, parents[0])
    key_facts = jnp.stack([key_spots, key_segs], 1)
    row_facts = jnp.stack(
        [row_spots, row_segs, row_first, row_second, row_index] + [jnp.zeros_like(row_index)] * 3
    )
    bias_query = lax.dynamic_slice_in_dim(vectors[4], tensor_index * width, width)
    bias_value = lax.dynamic_slice_in_dim(vectors[5], tensor_index * width, width)
    bias = jnp.concatenate([bias_query, jnp.zeros_like(bias_query), bias_value])[None]
    x_low, x_rows, emb_rows, queries, key_value, attn_low, lse_keys, full_in = attend(
        id_rows, pack_first, w_in.shape[0], width, bias, key_facts, row_facts, row_index[:, None]
    )
    z_part = to_low(dense_last(attn_low, full_proj_t))
    z_parts = exchange_blocks([z_part[s * slots : (s + 1) * slots] for s in blocks], "tensor")
    x_turned, emb_turned = x_low.T, emb_all.T
    z_parts[0], x_turned, emb_turned = together(z_parts[0], x_turned, emb_turned)
    z_branch = add_up(z_parts)
    pre_one = x_rows[:slots] + z_branch + vectors[6]
    h_one = layer_norm(pre_one, vectors[0], vectors[1])
    h_rows = jnp.concatenate(gather_blocks(to_low(h_one), "tensor"), 0)
    bias_up = lax.dynamic_slice_in_dim(
        vectors[8:].reshape(-1), tensor_index * hidden_share, hidden_share
    )
    upper = dense(h_rows, full_up) + bias_up
    act_low = to_low(gelu_tanh(upper))
    f_part = to_low(dense_last(act_low, full_down_t))
    f_branch = add_up(
        exchange_blocks([f_part[s * slots : (s + 1) * slots] for s in blocks], "tensor")
    )
    pre_two = h_one + f_branch + vectors[7]
    h_two = layer_norm(pre_two, vectors[2], vectors[3])
    h_two_low = to_low(h_two)
    rows_low = to_low(dense(h_two_low, full_out))

    rows_group = lax.all_gather(rows_low, "dp", axis=0, tiled=True)
    parts = head_forward(rows_group, table)
    both_rows = after(jnp.concatenate([h_two_low, rows_low], 1), parts)
    both_rows = gather_blocks(both_rows, "tensor")
    parts = lax.all_to_all(parts, "dp", 0, 0, tiled=True).reshape(dp_count, slots, -1)
    part_tops = join_low([parts[:, :, emb_width + i] for i in range(3)])
    part_sums = join_low([parts[:, :, emb_width + 3 + i] for i in range(3)])
    head_top = jnp.max(part_tops, 0)
    shares = jnp.exp(part_tops - head_top)
    total = jnp.sum(shares * part_sums, 0)
    lse = head_top + jnp.log(total)
    valid = comp_row >= 0
    target_logits = jnp.sum(rows_low.astype(jnp.float32) * target_rows, -1)
    loss_part = jnp.sum(jnp.where(valid, lse - target_logits, 0.0))
    slot_weight = 1.0 / (dp_count * tensor_count * slots)
    weight = jnp.where(valid, slot_weight, 0.0)
    mean = add_up(
        [parts[s, :, :emb_width] * (shares[s] / total)[:, None] for s in range(dp_count)]
    )
    out_low = to_low((mean - target_rows) * weight[:, None])

    shift = jnp.where(valid, lse - jnp.log(slot_weight), 1e30)
    shift = jnp.pad(jnp.stack(split_low(shift), 1), ((0, 0), (0, 125)))

    h_two_grad = dense_last(out_low, full_out)
    norm_two = jax.vjp(layer_norm, pre_two, vectors[2], vectors[3])[1]
    pre_two_grad, gain_two_grad, shift_two_grad = norm_two(h_two_grad)
    pre_two_grad, *both_rows = together(pre_two_grad, *both_rows)
    both_rows = jnp.concatenate(both_rows, 0)
    tree_rows = both_rows[:, model_width:]
    h_two_rows = both_rows[:, :model_width]
    f_rows = gather_blocks(jnp.concatenate([to_low(pre_two_grad), shift], 1), "tensor")
    f_rows = jnp.concatenate(f_rows, 0)
    rows_all = lax.all_gather(after(tree_rows, f_rows), "dp", axis=0, tiled=True)
    tree_shift = join_low([f_rows[:, model_width + i] for i in range(3)])
    f_rows = f_rows[:, :model_width]
    grad_down = dense_first(act_low, f_rows)
    act_grad = dense(f_rows, full_down_t)
    upper_low = to_low(jax.vjp(gelu_tanh, upper)[1](act_grad)[0])
    grad_up = dense_first(h_rows, upper_low)
    h_part = to_low(dense_last(upper_low, full_up))
    h_parts = exchange_blocks([h_part[s * slots : (s + 1) * slots] for s in blocks], "tensor")
    early = (3, 4)
    early_merged = [grad_up + error_up[0], grad_down + error_down[0]]
    early_lefts = [left_factor(*pair) for pair in zip(early_merged, (factor_up, factor_down[0]))]
    own_tree = jnp.arange(dp_count) == dp_index
    shift_all = jnp.where(own_tree[:, None], tree_shift[None], 0.0)
    early_lefts.append(shift_all.reshape(early_lefts[0].shape[0], -1))
    early_sizes = [left.shape[1] for left in early_lefts]
    early_lefts = jnp.concatenate(early_lefts, 1)
    h_parts[0], early_lefts = together(h_parts[0], early_lefts)
    h_one_grad = pre_two_grad + add_up(h_parts)
    norm_one = jax.vjp(layer_norm, pre_one, vectors[0], vectors[1])[1]
    pre_one_grad, gain_one_grad, shift_one_grad = norm_one(h_one_grad)
    z_low = to_low(pre_one_grad)
    z_rows = gather_blocks(jnp.concatenate([z_low, out_low], 1), "tensor")
    early_lefts = summed_over(early_lefts, "dp")
    z_rows[0], early_lefts, rows_all = together(z_rows[0], early_lefts, rows_all)
    *early_lefts, shift_all = columns_of(early_lefts, early_sizes)
    shift_all = shift_all.reshape(1, -1)
    z_rows = jnp.concatenate(z_rows, 0)
    out_rows = z_rows[:, model_width:]
    z_rows = z_rows[:, :model_width]
    query_grad, key_value_grad, x_part, row_part, emb_part = attend_back(
        z_rows,
        full_proj_t,
        queries,
        key_value,
        lse_keys,
        key_facts,
        row_facts,
        pack_first,
        full_in,
        pre_one_grad,
    )
    emb_parts = exchange_blocks(
        [emb_part[s * local_count : (s + 1) * local_count] for s in blocks], "tensor"
    )
    *early_lefts, emb_part = together(*early_lefts, emb_part)
    early_bases, early_terms = orthonormal_all(early_lefts)
    early_rights = [right_factor(*pair) for pair in zip(early_merged, early_bases)]
    early_sizes = [right.shape[1] for right in early_rights]
    early_rights = jnp.concatenate(early_rights, 1)
    emb_parts[1], query_grad, key_value_grad = together(emb_parts[1], query_grad, key_value_grad)
    value_grad = key_value_grad[:, width:]
    merged_qkv = [
        dense(left, right) + error_qkv[0, :, part]
        for part, (left, right) in enumerate(
            (
                (to_low(x_rows).T, query_grad),
                (x_turned, key_value_grad[:, :width]),
                (x_turned, value_grad),
            )
        )
    ]
    emb_parts[0], early_rights, *merged_qkv = together(emb_parts[0], early_rights, *merged_qkv)
    emb_grad_own = to_low(add_up(emb_parts))
    emb_grad = gather_blocks(emb_grad_own, "tensor")
    emb_grad[1], x_part, row_part, z_rows, out_rows, *merged_qkv = together(
        emb_grad[1], x_part, row_part, z_rows, out_rows, *merged_qkv
    )
    grad_out = dense_first(h_two_rows, out_rows)
    grad_proj = dense_first(attn_low, z_rows)
    grad_in = dense(emb_turned, x_part) + dense_first(emb_rows, row_part)

    def placed(values, size, total_size):
        return lax.dynamic_update_slice_in_dim(
            jnp.zeros((total_size,), jnp.float32), values, tensor_index * size, 0
        )

    head_rows = jnp.stack(
        [
            gain_one_grad,
            shift_one_grad,
            gain_two_grad,
            shift_two_grad,
            placed(jnp.sum(query_grad.astype(jnp.float32), 0), width, model_width),
            placed(jnp.sum(value_grad.astype(jnp.float32), 0), width, model_width),
            jnp.sum(pre_one_grad, 0),
            jnp.sum(pre_two_grad, 0),
        ]
    )
    up_rows = placed(
        jnp.sum(upper_low.astype(jnp.float32), 0), hidden_share, hidden_share * tensor_count
    ).reshape(-1, model_width)
    loss_row = jnp.full((1, model_width), loss_part)
    vector_part = jnp.concatenate([head_rows, up_rows, loss_row], 0)

    merged = (
        grad_in + error_in[0] * (1.0 / tensor_count),
        None,
        grad_proj + error_proj[0],
    ) + tuple(early_merged) + (grad_out + error_out[0],)
    factors = (
        factor_in,
        factor_qkv.reshape(3 * width, -1),
        factor_proj[0],
        None,
        None,
        factor_out,
    )
    bases = [None] * 6
    fresh = [None] * 6
    parts_of = [None] * 6
    late = (0, 1, 2, 5)
    emb_grad[2], *merged_qkv = together(emb_grad[2], *merged_qkv)
    lefts = [
        sum(left_factor(merged_qkv[part], factor_qkv[part]) for part in range(3))
        if index == 1
        else left_factor(merged[index], factors[index])
        for index in late
    ]
    sizes = [left.shape[1] for left in lefts] + [vector_part.size // lefts[0].shape[0]]
    emb_grad[-1], vector_part = together(emb_grad[-1], vector_part)
    lefts.append(vector_part.reshape(lefts[0].shape[0], -1))
    lefts = jnp.concatenate(lefts + [early_rights], 1)
    emb_grad[0], lefts = together(emb_grad[0], lefts)
    lefts = summed_over(lefts, "dp")
    emb_grad = jnp.concatenate(emb_grad, 0)
    tree_weight = jnp.where(comp_tree.reshape(-1) >= 0, slot_weight, 0.0)
    target_grad = to_low(tree_rows.astype(jnp.float32) * -tree_weight[:, None])
    id_grad = jnp.concatenate([emb_grad, target_grad], 0)

    def listed_rows(hits):
        return to_low(dense(hits, id_grad)).reshape(dp_count, share, -1)

    def deliver_more(turn, state):
        hits = listed(turn, owner)
        spots = exchanged(entries_of(hits)).reshape(-1) - vocab_start
        rows = exchanged(listed_rows(hits.astype(jnp.bfloat16))).reshape(dp_count * share, -1).astype(jnp.float32)
        rows = jnp.where((spots >= 0)[:, None], rows, 0.0)
        spots = jnp.clip(spots, 0, shard_rows - 1)
        return state[0].at[spots].add(-table_rate * rows), state[1].at[spots].add(rows)

    added = listed_rows(hits_first)
    added = exchange_blocks([added[s] for s in range(dp_count)], "dp")
    added[1], lefts = together(added[1], lefts)
    lefts = columns_of(lefts, sizes + early_sizes)
    flat = jnp.concatenate([lefts[0], lefts[len(sizes) - 1]], 1)
    flat = gather_blocks(flat, "tensor")
    early_rights = lefts[len(sizes) :]
    early_parts = columns_of(outer_terms(jnp.concatenate(early_rights, 1)), early_sizes)

    def error_left(index):
        return merged[index] - dense_first(bases[index], parts_of[index]) * (1.0 / dp_count)

    errors_new = [None] * 6
    for i, index in enumerate(early):
        bases[index] = early_terms[i]
        fresh[index] = early_rights[i]
        parts_of[index] = early_parts[i]
    errors_new[early[0]] = error_left(early[0])
    flat[0], errors_new[early[0]] = together(flat[0], errors_new[early[0]])
    flat = add_pairs(flat)
    vector_sum = flat[:, sizes[0] :].reshape(vector_part.shape)
    found_bases, found_terms = orthonormal_all([flat[:, : sizes[0]]] + lefts[1 : len(late)])
    rights = [
        jnp.concatenate([right_factor(merged_qkv[part], found_bases[i]) for part in range(3)], 1)
        if index == 1
        else right_factor(merged[index], found_bases[i])
        for i, index in enumerate(late)
    ]
    sizes = [right.shape[1] for right in rights]
    rights = jnp.concatenate(rights, 1)
    rights, held = together(rights, early_parts[1])
    parts_of[early[1]] = held
    errors_new[early[1]] = error_left(early[1])
    rights = summed_over(rights, "dp")
    grad_in_own = lax.psum_scatter(
        after(to_low(grad_in), emb_grad), "tensor", scatter_dimension=0, tiled=True
    )
    grad_in_sum = lax.all_gather(grad_in_own, "tensor", axis=0, tiled=True)
    right_in = gather_blocks(rights[:, : sizes[0]], "tensor")
    added[0], rights, errors_new[3], errors_new[4] = together(
        added[0], rights, errors_new[3], errors_new[4]
    )
    updated = list(
        table_update(rows_all, shift_all, added, asked_first.reshape(1, -1) - vocab_start, table, table_moment)
    )
    updated[0], right_in[0], grad_in_sum = together(updated[0], right_in[0], grad_in_sum)
    new_table, new_table_moment = lax.fori_loop(1, rounds, deliver_more, tuple(updated))
    rights = columns_of(rights, sizes)
    rights[0] = add_pairs(right_in)
    right_parts = columns_of(outer_terms(jnp.concatenate(rights, 1)), sizes)
    for i, index in enumerate(late):
        bases[index] = found_terms[i]
        fresh[index] = rights[i]
        parts_of[index] = right_parts[i]
    merged = (grad_in_sum.astype(jnp.float32) + error_in[0],) + merged[1:]
    for index in (0, 2, 5):
        errors_new[index] = error_left(index)
    errors_new[1] = jnp.stack(
        [
            merged_qkv[part]
            - dense_first(bases[1], parts_of[1][:, part * width : (part + 1) * width])
            * (1.0 / dp_count)
            for part in range(3)
        ],
        0,
    ).transpose(1, 0, 2)

    def shard(index, size, axis):
        left, right = bases[index], parts_of[index]
        if axis == 0:
            left = lax.dynamic_slice_in_dim(left, dp_index * size, size, 1)
        else:
            right = lax.dynamic_slice_in_dim(right, dp_index * size, size, 1)
        return dense_first(left, right)

    shard_in = shard(0, w_in.shape[0], 0)
    shard_qkv = shard(1, shard_width, 0)
    shard_qkv = jnp.stack(
        [shard_qkv[:, part * width : (part + 1) * width] for part in range(3)], 1
    )
    shard_proj = shard(2, w_proj.shape[1], 1)
    shard_up = shard(3, w_up.shape[0], 0)
    shard_down = shard(4, w_down.shape[1], 1)
    shard_out = shard(5, w_out.shape[0], 0)
    fresh = [values.T for values in fresh]
    loss_sum = vector_sum[-1, 0]
    vector_grad = vector_sum[:-1]
    new_w_in, new_moment_in = advance(w_in, moment_in, shard_in, matrix_rates[0])
    new_w_qkv, new_moment_qkv = advance(w_qkv, moment_qkv, shard_qkv, matrix_rates[1])
    new_w_proj, new_moment_proj = advance(w_proj, moment_proj, shard_proj, matrix_rates[2])
    new_w_up, new_moment_up = advance(w_up, moment_up, shard_up, matrix_rates[3])
    new_w_down, new_moment_down = advance(w_down, moment_down, shard_down, matrix_rates[4])
    new_w_out, new_moment_out = advance(w_out, moment_out, shard_out, matrix_rates[5])
    new_vectors, new_vector_moment = advance(vectors, vector_moment, vector_grad, vector_rate)
    return (
        loss_sum,
        new_table,
        new_table_moment,
        new_vectors,
        new_vector_moment,
        new_w_in,
        new_moment_in,
        errors_new[0][None],
        fresh[0],
        new_w_qkv,
        new_moment_qkv,
        errors_new[1].reshape(1, model_width, 3, width),
        fresh[1].reshape(3, width, -1),
        new_w_proj,
        new_moment_proj,
        errors_new[2][None],
        fresh[2][None],
        new_w_up,
        new_moment_up,
        errors_new[3][None],
        fresh[3],
        new_w_down,
        new_moment_down,
        errors_new[4][None],
        fresh[4][None],
        new_w_out,
        new_moment_out,
        errors_new[5][None],
        fresh[5],
    )


def solution(mesh):
    return jax.shard_map(
        per_device,
        mesh=mesh,
        in_specs=(
            P("dp", "tensor"),
            P("dp", None),
            P("dp", None),
            P("dp", "tensor"),
            P("dp", "tensor"),
            P("dp", None),
            P("dp", None),
            P(),
            P(),
            P("dp", None),
            P("dp", None),
            P("dp", None, None),
            P(),
            P("dp", None, "tensor"),
            P("dp", None, "tensor"),
            P("dp", None, None, "tensor"),
            P(None, "tensor", None),
            P("tensor", "dp"),
            P("tensor", "dp"),
            P("dp", "tensor", None),
            P("tensor", None, None),
            P("dp", "tensor"),
            P("dp", "tensor"),
            P("dp", None, "tensor"),
            P("tensor", None),
            P("tensor", "dp"),
            P("tensor", "dp"),
            P("dp", "tensor", None),
            P("tensor", None, None),
            P("dp", None),
            P("dp", None),
            P("dp", None, None),
            P(),
        ),
        out_specs=(
            P(),
            P("dp", None),
            P("dp", None),
            P(),
            P(),
            P("dp", None),
            P("dp", None),
            P("dp", None, None),
            P(),
            P("dp", None, "tensor"),
            P("dp", None, "tensor"),
            P("dp", None, None, "tensor"),
            P(None, "tensor", None),
            P("tensor", "dp"),
            P("tensor", "dp"),
            P("dp", "tensor", None),
            P("tensor", None, None),
            P("dp", "tensor"),
            P("dp", "tensor"),
            P("dp", None, "tensor"),
            P("tensor", None),
            P("tensor", "dp"),
            P("tensor", "dp"),
            P("dp", "tensor", None),
            P("tensor", None, None),
            P("dp", None),
            P("dp", None),
            P("dp", None, None),
            P(),
        ),
        check_vma=False,
    )
```

```python
import functools

import jax
import jax.numpy as jnp
from jax import lax
from jax.experimental import pallas as pl
from jax.experimental.pallas import tpu as pltpu
from jax.sharding import PartitionSpec as P

HD = 64


momentum_decay = 0.9
table_rate = 300.0
vector_rate = 1000.0
matrix_rates = (1500.0, 80.0, 3000.0, 80.0, 40.0, 80.0)


def to_low(values):
    return values.astype(jnp.bfloat16)


def dense(left, right):
    return jnp.dot(left, right, preferred_element_type=jnp.float32)


def dense_first(left, right):
    return lax.dot_general(
        left, right, (((0,), (0,)), ((), ())), preferred_element_type=jnp.float32
    )


def dense_last(left, right):
    return lax.dot_general(
        left, right, (((1,), (1,)), ((), ())), preferred_element_type=jnp.float32
    )


left_terms = (0, 0, 1, 1, 0, 2)
right_terms = (0, 1, 0, 1, 2, 0)


def two_terms(values, axis):
    first = coarse(values)
    return to_low(jnp.concatenate([first, values - first], axis))


def left_factor(merged, factor):
    count = factor.shape[1]
    both = lax.dot_general(
        two_terms(factor, 1),
        to_low(merged),
        (((0,), (1,)), ((), ())),
        preferred_element_type=jnp.float32,
    )
    return both[:count] + both[count:]


def right_factor(merged, basis):
    both = dense(two_terms(basis, 0), to_low(merged))
    return both[: basis.shape[0]] + both[basis.shape[0] :]


def layer_norm(values, gain, shift):
    center = values - jnp.mean(values, -1, keepdims=True)
    spread = jnp.mean(center * center, -1, keepdims=True)
    return center * lax.rsqrt(spread + 1e-05) * gain + shift


def gelu_tanh(values):
    return jax.nn.gelu(values, approximate=True)


def swap(values, axis, step):
    return lax.ppermute(values, axis, [(i, i ^ step) for i in range(lax.axis_size(axis))])


def gather_blocks(values, axis):
    return [values] + [swap(values, axis, s) for s in range(1, lax.axis_size(axis))]


def exchange_blocks(blocks, axis):
    return [blocks[0]] + [swap(blocks[s], axis, s) for s in range(1, lax.axis_size(axis))]


def summed_over(values, axis, step=1):
    while step < lax.axis_size(axis):
        values = jax.tree.map(lambda a, s=step: a + swap(a, axis, s), values)
        step *= 2
    return values


def add_up(parts):
    total = parts[0].astype(jnp.float32)
    for part in parts[1:]:
        total = total + part.astype(jnp.float32)
    return total


def add_pairs(parts):
    while len(parts) > 1:
        parts = [left + right for left, right in zip(parts[::2], parts[1::2])]
    return parts[0]


def orthonormal_kernel(*refs):
    many = len(refs) // 3
    left_refs, basis_refs, term_refs = refs[:many], refs[many : 2 * many], refs[2 * many :]
    count = left_refs[0].shape[0]
    longest = max(ref.shape[1] for ref in left_refs)

    def row(ref, index):
        values = ref[index : index + 1, :]
        short = longest - values.shape[1]
        if short == 0:
            return values
        return jnp.concatenate([values, jnp.zeros((1, short), jnp.float32)], 1)

    columns = [jnp.concatenate([row(ref, k) for ref in left_refs], 0) for k in range(count)]
    for index in range(count):
        vector = columns[index]
        vector = vector * lax.rsqrt(jnp.sum(vector * vector, -1, keepdims=True) + 1e-06)
        for place, ref in enumerate(basis_refs):
            ref[index : index + 1, :] = vector[place : place + 1, : ref.shape[1]]
        for later in range(index + 1, count):
            other = columns[later]
            columns[later] = other - jnp.sum(vector * other, -1, keepdims=True) * vector
    for basis_ref, term_ref in zip(basis_refs, term_refs):
        rest = basis_ref[...]
        terms = []
        for _ in range(3):
            terms.append(rest.astype(jnp.bfloat16).astype(jnp.float32))
            rest = rest - terms[-1]
        term_ref[...] = jnp.concatenate([terms[term] for term in left_terms], 0).astype(
            jnp.bfloat16
        )


def orthonormal_all(lefts):
    count = lefts[0].shape[0]
    bases = [jax.ShapeDtypeStruct(left.shape, jnp.float32) for left in lefts]
    terms = [
        jax.ShapeDtypeStruct((len(left_terms) * count, left.shape[1]), jnp.bfloat16)
        for left in lefts
    ]
    both = pl.pallas_call(orthonormal_kernel, out_shape=bases + terms)(*lefts)
    return both[: len(lefts)], both[len(lefts) :]


def outer_terms(rights):
    terms = split_low(rights)
    return jnp.concatenate([terms[term] for term in right_terms], 0)


def coarse(values):
    return lax.reduce_precision(values, 8, 7)


def split_low(values):
    first = coarse(values)
    second = coarse(values - first)
    return [to_low(first), to_low(second), to_low(values - first - second)]


def join_low(terms):
    terms = [term.astype(jnp.float32) for term in terms]
    return terms[0] + (terms[1] + terms[2])


def vocab_tile(shard_rows, most=640):
    tiles = -(-shard_rows // most)
    return -(-(-(-shard_rows // tiles)) // 16) * 16


def head_kernel(shard_rows, rows_ref, table_ref, out_ref, total, stats):
    step = pl.program_id(0)
    tile_rows, wide = table_ref.shape

    @pl.when(step == 0)
    def _():
        total[...] = jnp.zeros_like(total)
        stats[0:1, :] = jnp.full((1, stats.shape[1]), -1e30, jnp.float32)
        stats[1:2, :] = jnp.zeros((1, stats.shape[1]), jnp.float32)

    row_ids = step * tile_rows + lax.broadcasted_iota(jnp.int32, (tile_rows, 1), 0)
    present = row_ids < shard_rows
    tile = jnp.where(present, table_ref[...], 0.0).astype(jnp.bfloat16)
    logits = lax.dot_general(
        tile, rows_ref[...], (((1,), (1,)), ((), ())), preferred_element_type=jnp.float32
    )
    logits = jnp.where(present, logits, -1e30)
    before = stats[0:1, :]
    top = jnp.maximum(before, jnp.max(logits, 0, keepdims=True))
    fade = jnp.exp(before - top)
    expo = jnp.exp(logits - top)
    stats[0:1, :] = top
    stats[1:2, :] = stats[1:2, :] * fade + jnp.sum(expo, 0, keepdims=True)
    total[...] = total[...] * fade + lax.dot_general(
        tile,
        expo.astype(jnp.bfloat16),
        (((0,), (0,)), ((), ())),
        preferred_element_type=jnp.float32,
    )

    @pl.when(step == pl.num_programs(0) - 1)
    def _():
        out_ref[:, :wide] = total[...].T.astype(jnp.bfloat16)
        terms = []
        for index in (0, 1):
            value = stats[index : index + 1, :]
            for _ in range(3):
                part = value.astype(jnp.bfloat16).astype(jnp.float32)
                terms.append(part)
                value = value - part
        spare = jnp.zeros((out_ref.shape[1] - wide - 6, value.shape[1]), jnp.float32)
        out_ref[:, wide:] = jnp.concatenate(terms + [spare], 0).T.astype(jnp.bfloat16)


def head_forward(rows, table):
    count, wide = rows.shape
    shard_rows = table.shape[0]
    tile = vocab_tile(shard_rows, 1280 if count <= 1024 else 640)
    return pl.pallas_call(
        functools.partial(head_kernel, shard_rows),
        grid=(pl.cdiv(shard_rows, tile),),
        in_specs=[
            pl.BlockSpec((count, wide), lambda i: (0, 0)),
            pl.BlockSpec((tile, wide), lambda i: (i, 0)),
        ],
        out_specs=pl.BlockSpec((count, wide + 128), lambda i: (0, 0)),
        out_shape=jax.ShapeDtypeStruct((count, wide + 128), jnp.bfloat16),
        scratch_shapes=[
            pltpu.VMEM((wide, count), jnp.float32),
            pltpu.VMEM((8, count), jnp.float32),
        ],
        compiler_params=pltpu.CompilerParams(vmem_limit_bytes=18 * 2**20 + 24 * tile * count + 10 * count * wide),
        cost_estimate=pl.CostEstimate(
            flops=4 * shard_rows * count * wide,
            bytes_accessed=4 * shard_rows * wide,
            transcendentals=shard_rows * count,
        ),
    )(rows, table)


def table_kernel(rows_ref, shift_ref, ids_ref, table_ref, moment_ref, *refs):
    parts, (new_table_ref, new_moment_ref, added_ref) = refs[:-3], refs[-3:]
    tile_rows, wide = table_ref.shape

    @pl.when(pl.program_id(0) == 0)
    def _():
        for index, part in enumerate(parts):
            count = part.shape[0]
            added_ref[index * count : (index + 1) * count, :] = part[...]

    row_ids = pl.program_id(0) * tile_rows
    row_ids = row_ids + lax.broadcasted_iota(jnp.int32, (tile_rows, 1), 0)
    hits = (row_ids == ids_ref[...]).astype(jnp.bfloat16)
    new_moment_ref[...] = momentum_decay * moment_ref[...] + dense(hits, added_ref[...])
    tile = table_ref[...].astype(jnp.bfloat16)
    chunk = min(512, rows_ref.shape[0])

    def one(spot):
        rows = rows_ref[spot, :]
        grad = jnp.exp(dense_last(tile, rows) - shift_ref[0:1, spot])
        return dense(grad.astype(jnp.bfloat16), rows)

    together = 4 * chunk if rows_ref.shape[0] % (4 * chunk) == 0 else chunk

    def some(index, carry):
        begin = pl.multiple_of(index * together, together)
        parts = [one(pl.ds(begin + k * chunk, chunk)) for k in range(together // chunk)]
        new_moment_ref[...] += sum(parts[1:], parts[0])
        return carry

    if rows_ref.shape[0] == together:
        some(0, 0)
    else:
        lax.fori_loop(0, rows_ref.shape[0] // together, some, 0)
    new_table_ref[...] = table_ref[...] - table_rate * new_moment_ref[...]


def table_update(rows, shift, added, ids, table, moment):
    shard_rows, wide = table.shape
    tile = vocab_tile(shard_rows)
    whole = lambda array: pl.BlockSpec(
        array.shape, lambda i: (0, 0), pipeline_mode=pl.Buffered(buffer_count=1)
    )
    part = pl.BlockSpec((tile, wide), lambda i: (i, 0))
    return pl.pallas_call(
        table_kernel,
        grid=(pl.cdiv(shard_rows, tile),),
        in_specs=[whole(rows), whole(shift), whole(ids), part, part] + [whole(a) for a in added],
        out_specs=[part, part],
        out_shape=[jax.ShapeDtypeStruct(table.shape, jnp.float32)] * 2,
        scratch_shapes=[pltpu.VMEM((ids.shape[1], wide), jnp.bfloat16)],
        compiler_params=pltpu.CompilerParams(vmem_limit_bytes=56 * 2**20),
        cost_estimate=pl.CostEstimate(
            flops=shard_rows * wide * (4 * rows.shape[0] + 2 * ids.shape[1]),
            bytes_accessed=16 * shard_rows * wide,
            transcendentals=shard_rows * rows.shape[0],
        ),
    )(rows, shift, ids, table, moment, *added)


def visible_pairs(key_ref, row_ref):
    spots, segs = key_ref[:, 0:1], key_ref[:, 1:2]
    related = (segs == row_ref[1:2, :]) | (segs == row_ref[2:3, :]) | (segs == row_ref[3:4, :])
    return related & (spots <= row_ref[0:1, :])


def head_columns(width, head):
    columns = lax.broadcasted_iota(jnp.int32, (1, width), 1)
    return (columns >= head * HD) & (columns < (head + 1) * HD)


def attend_kernel(
    shard_in,
    emb_ref,
    pack_ref,
    bias_ref,
    key_ref,
    row_ref,
    index_ref,
    x_ref,
    x_rows_ref,
    emb_rows_ref,
    query_ref,
    key_value_ref,
    attn_ref,
    lse_ref,
    in_ref,
):
    length = x_ref.shape[0]
    count, width = query_ref.shape
    block = min(256, length)
    share = pack_ref.shape[1] - 4 * width
    halves = in_ref.shape[1] // share
    for owner in range(in_ref.shape[0] // shard_in):
        for part in range(halves):
            begin = (owner * halves + part) * shard_in
            in_ref[owner * shard_in : (owner + 1) * shard_in, part * share : (part + 1) * share] = (
                pack_ref[begin : begin + shard_in, :share]
            )

    def one_block(index, carry):
        spot = pl.ds(pl.multiple_of(index * block, block), block)
        x_low = to_low(dense(emb_ref[spot, :], in_ref[...]))
        x_ref[spot, :] = x_low
        mixed = dense(x_low, pack_ref[:, share + width : share + 3 * width]) + bias_ref[:, width:]
        key_value_ref[spot, :] = to_low(mixed)
        return carry

    lax.fori_loop(0, length // block, one_block, 0)
    chosen = index_ref[...] == lax.broadcasted_iota(jnp.int32, (count, length), 1)
    emb_rows = to_low(dense(chosen.astype(jnp.bfloat16), emb_ref[:length, :]))
    emb_rows_ref[...] = emb_rows
    x_rows = dense(emb_rows, in_ref[...])
    x_rows_ref[...] = x_rows
    queries = to_low(dense(to_low(x_rows), pack_ref[:, share : share + width]) + bias_ref[:, :width])
    query_ref[...] = queries
    keys_all = key_value_ref[:, :width]
    values_turned = key_value_ref[:, width:].T
    blocked = jnp.where(visible_pairs(key_ref, row_ref), 0.0, -1e30)
    features = lax.broadcasted_iota(jnp.int32, (width, 1), 0)
    attended = jnp.zeros((width, count), jnp.float32)
    for head in range(width // HD):
        own = jnp.where(head_columns(width, head), queries, jnp.zeros_like(queries))
        scores = dense_last(keys_all, own) * HD ** (-0.5) + blocked
        top = jnp.max(scores, 0, keepdims=True)
        expo = jnp.exp(scores - top)
        total = jnp.sum(expo, 0, keepdims=True)
        lse_ref[head : head + 1, :] = top + jnp.log(total)
        result = dense(values_turned, to_low(expo / total))
        mine = (features >= head * HD) & (features < (head + 1) * HD)
        attended = jnp.where(mine, result, attended)
    attn_ref[...] = to_low(attended.T)


def attend(id_rows, pack, shard_in, width, bias, key_facts, row_facts, row_index):
    emb_width = id_rows.shape[1]
    model_width = pack.shape[0]
    length = key_facts.shape[0]
    count = row_index.shape[0]
    low = lambda *shape: jax.ShapeDtypeStruct(shape, jnp.bfloat16)
    full = lambda *shape: jax.ShapeDtypeStruct(shape, jnp.float32)
    return pl.pallas_call(
        functools.partial(attend_kernel, shard_in),
        out_shape=[
            low(length, model_width),
            full(count, model_width),
            low(count, emb_width),
            low(count, width),
            low(length, 2 * width),
            low(count, width),
            full(8, count),
            low(emb_width, model_width),
        ],
        compiler_params=pltpu.CompilerParams(vmem_limit_bytes=48 * 2**20),
        cost_estimate=pl.CostEstimate(
            flops=2 * length * model_width * (emb_width + 2 * width) + 4 * length * count * width,
            bytes_accessed=2 * length * (emb_width + model_width + 2 * width),
            transcendentals=length * count * width // HD,
        ),
    )(id_rows, pack, bias, key_facts, row_facts, row_index)


def attend_back_kernel(
    z_ref,
    proj_ref,
    query_ref,
    key_value_ref,
    lse_ref,
    key_ref,
    row_ref,
    pack_ref,
    in_ref,
    pre_ref,
    query_grad_ref,
    key_value_grad_ref,
    x_part_ref,
    row_part_ref,
    emb_part_ref,
):
    count, width = query_ref.shape
    length = key_value_ref.shape[0]
    slots = pre_ref.shape[0]
    share = pack_ref.shape[1] - 4 * width
    scale = HD ** (-0.5)
    queries = query_ref[...]
    keys_all = key_value_ref[:, :width]
    values_all = key_value_ref[:, width:]
    keys_turned = keys_all.T
    attn_grad = to_low(dense(z_ref[...], proj_ref[...]))
    blocked = jnp.where(visible_pairs(key_ref, row_ref), 0.0, -1e30)
    features = lax.broadcasted_iota(jnp.int32, (width, 1), 0)
    key_grad = jnp.zeros((length, width), jnp.float32)
    value_grad = jnp.zeros((length, width), jnp.float32)
    query_grad = jnp.zeros((width, count), jnp.float32)
    for head in range(width // HD):
        mine = head_columns(width, head)
        own = jnp.where(mine, queries, jnp.zeros_like(queries))
        own_grad = jnp.where(mine, attn_grad, jnp.zeros_like(attn_grad))
        scores = dense_last(keys_all, own) * scale + blocked
        probs = jnp.exp(scores - lse_ref[head : head + 1, :])
        probs_grad = dense_last(values_all, own_grad)
        rowdot = jnp.sum(probs * probs_grad, 0, keepdims=True)
        scores_grad = to_low(probs * (probs_grad - rowdot))
        value_grad += dense(to_low(probs), own_grad)
        key_grad += dense(scores_grad, own)
        rows = (features >= head * HD) & (features < (head + 1) * HD)
        query_grad = jnp.where(rows, dense(keys_turned, scores_grad), query_grad)
    query_grad = to_low((query_grad * scale).T)
    query_grad_ref[...] = query_grad
    key_value_grad_ref[:, :width] = to_low(key_grad * scale)
    key_value_grad_ref[:, width:] = to_low(value_grad)
    row_part = dense_last(query_grad, pack_ref[:, share : share + width])
    row_part_ref[:slots, :] = to_low(row_part[:slots] + pre_ref[...])
    row_part_ref[slots:, :] = to_low(row_part[slots:])
    row_emb = to_low(dense_last(row_part_ref[...], in_ref[...]))
    block = min(256, length)

    def one_block(index, carry):
        begin = pl.multiple_of(index * block, block)
        spot = pl.ds(begin, block)
        x_part = to_low(dense_last(key_value_grad_ref[spot, :], pack_ref[:, share + width : share + 3 * width]))
        x_part_ref[spot, :] = x_part
        places = begin + lax.broadcasted_iota(jnp.int32, (block, 1), 0)
        chosen = (places == row_ref[4:5, :]).astype(jnp.bfloat16)
        emb_part_ref[spot, :] = to_low(dense_last(x_part, in_ref[...]) + dense(chosen, row_emb))
        return carry

    lax.fori_loop(0, length // block, one_block, 0)


def attend_back(
    z_rows, own_proj_t, queries, key_value, lse, key_facts, row_facts, pack, full_in, pre_grad
):
    count, width = queries.shape
    length = key_value.shape[0]
    emb_width, model_width = full_in.shape
    low = lambda *shape: jax.ShapeDtypeStruct(shape, jnp.bfloat16)
    return pl.pallas_call(
        attend_back_kernel,
        out_shape=[
            low(count, width),
            low(length, 2 * width),
            low(length, model_width),
            low(count, model_width),
            low(length, emb_width),
        ],
        compiler_params=pltpu.CompilerParams(vmem_limit_bytes=48 * 2**20),
        cost_estimate=pl.CostEstimate(
            flops=2 * length * model_width * (emb_width + 2 * width) + 10 * length * count * width,
            bytes_accessed=2 * length * (emb_width + model_width + 2 * width),
            transcendentals=length * count * width // HD,
        ),
    )(z_rows, own_proj_t, queries, key_value, lse, key_facts, row_facts, pack, full_in, pre_grad)


def listed_kernel(many, *refs):
    place_ref, block_refs, out_refs = refs[0], refs[1 : 1 + many], refs[1 + many :]
    share = out_refs[0].shape[0]
    entries = lax.broadcasted_iota(jnp.int32, (share * len(out_refs), 1), 0)
    total = None
    begin = 0
    for ref in block_refs:
        stop = begin + ref.shape[0]
        hits = (entries == place_ref[:, begin:stop]).astype(jnp.bfloat16)
        part = dense(hits, ref[...])
        total = part if total is None else total + part
        begin = stop
    total = to_low(total)
    for owner, ref in enumerate(out_refs):
        ref[...] = total[owner * share : (owner + 1) * share]


def listed_sums(place, blocks, owners, share):
    wide = blocks[0].shape[1]
    return pl.pallas_call(
        functools.partial(listed_kernel, len(blocks)),
        out_shape=[jax.ShapeDtypeStruct((share, wide), jnp.bfloat16)] * owners,
        compiler_params=pltpu.CompilerParams(vmem_limit_bytes=40 * 2**20),
        cost_estimate=pl.CostEstimate(flops=1, bytes_accessed=1, transcendentals=1),
    )(place[None], *blocks)


def lookup(codes, table_row):
    hits = codes[:, None] == jnp.arange(table_row.shape[0])[None, :]
    return jnp.sum(jnp.where(hits, table_row[None, :], 0), 1)


def after(values, *others):
    return lax.optimization_barrier((values, *others))[0]


def together(*values):
    return lax.optimization_barrier(values)


def columns_of(values, sizes):
    cuts = [sum(sizes[:i]) for i in range(len(sizes) + 1)]
    return [values[:, cuts[i] : cuts[i + 1]] for i in range(len(sizes))]


def advance(weight, moment, approx, rate):
    fresh_moment = momentum_decay * moment + approx
    return (weight - rate * fresh_moment, fresh_moment)


def per_device(
    tokens,
    segments,
    parents,
    completion,
    targets,
    table,
    table_moment,
    vectors,
    vector_moment,
    w_in,
    moment_in,
    error_in,
    factor_in,
    w_qkv,
    moment_qkv,
    error_qkv,
    factor_qkv,
    w_proj,
    moment_proj,
    error_proj,
    factor_proj,
    w_up,
    moment_up,
    error_up,
    factor_up,
    w_down,
    moment_down,
    error_down,
    factor_down,
    w_out,
    moment_out,
    error_out,
    factor_out,
):
    dp_count = lax.axis_size("dp")
    tensor_count = lax.axis_size("tensor")
    dp_index = lax.axis_index("dp")
    tensor_index = lax.axis_index("tensor")
    token_ids = tokens[0]
    comp_row = completion[0]
    target_row = targets[0]
    local_count = token_ids.shape[0]
    slots = comp_row.shape[0]
    segs = segments[0]
    length = segs.shape[0]
    shard_rows, emb_width = table.shape
    vocab_start = dp_index * shard_rows
    width = w_qkv.shape[2]
    hidden_share = w_up.shape[1]
    model_width = vectors.shape[1]
    heads_here = width // HD
    scale = HD ** (-0.5)
    shard_width = w_qkv.shape[0]
    blocks = range(tensor_count)

    meta = gather_blocks(jnp.concatenate([token_ids, comp_row, target_row]), "tensor")

    halves = shard_width // w_in.shape[0]
    share_in = model_width // halves
    in_low = to_low(w_in)
    in_stack = jnp.concatenate(
        [in_low[:, h * share_in : (h + 1) * share_in] for h in range(halves)], 0
    )
    qkv_low = to_low(w_qkv).reshape(shard_width, 3 * width)
    pack_first = lax.all_gather(
        jnp.concatenate([in_stack, qkv_low, to_low(w_proj).T], 1), "dp", axis=0, tiled=True
    )
    pack_rest = lax.all_gather(
        jnp.concatenate([to_low(w_up), to_low(w_down).T, to_low(w_out)], 1),
        "dp",
        axis=0,
        tiled=True,
    )
    full_proj_t = pack_first[:, share_in + 3 * width :]
    full_up = pack_rest[:, :hidden_share]
    full_down_t = pack_rest[:, hidden_share : 2 * hidden_share]
    full_out = pack_rest[:, 2 * hidden_share :]

    meta = jnp.stack(meta)
    comp_tree = meta[:, local_count : local_count + slots]
    ids = jnp.concatenate(
        [meta[:, :local_count].reshape(-1), meta[:, local_count + slots :].reshape(-1)]
    )

    id_count = ids.shape[0]
    share = -(-9 * id_count // (160 * dp_count)) * 16
    owner = ids // shard_rows
    order = jnp.arange(id_count)
    before = order[None, :] < order[:, None]
    same = ids[:, None] == ids[None, :]
    first_one = ~jnp.any(same & before, 1)
    rank = jnp.sum((owner[:, None] == owner[None, :]) & before & first_one[None, :], 1)
    rank = jnp.sum(jnp.where(same & first_one[None, :], rank[None, :], 0), 1)
    rounds_here = jnp.max(rank) // share + 1

    def placed_ids(turn, owners):
        place = rank - turn * share
        return jnp.where((place >= 0) & (place < share), owners * share + place, -1)

    def listed(place):
        return place[None, :] == jnp.arange(dp_count * share)[:, None]

    def entries_of(hits):
        return jnp.max(jnp.where(hits, ids[None, :], -1), 1).reshape(dp_count, share)

    def picked_rows(asked, kind):
        spots = jnp.clip(asked - vocab_start, 0, shard_rows - 1)
        return jnp.take(table, spots.reshape(-1), axis=0).astype(kind).reshape(dp_count, share, -1)

    def exchanged(values):
        return lax.all_to_all(values, "dp", 0, 0, tiled=True)

    place_first = placed_ids(0, owner ^ dp_index)
    hits_first = listed(place_first)
    entries = entries_of(hits_first)
    hits_first = hits_first.astype(jnp.bfloat16)
    notes = [jnp.concatenate([entries[s], rounds_here[None]]) for s in range(dp_count)]
    notes = jnp.stack(exchange_blocks(notes, "dp"))
    asked_first = notes[:, :share]
    rounds = jnp.max(notes[:, share])

    def fetch_more(turn, rows):
        hits = listed(placed_ids(turn, owner))
        found = exchanged(picked_rows(exchanged(entries_of(hits)), jnp.float32))
        found = to_low(coarse(found.reshape(dp_count * share, -1)))
        return rows + to_low(dense_first(hits.astype(jnp.bfloat16), found))

    found = picked_rows(asked_first, jnp.bfloat16)
    found = exchange_blocks([found[s] for s in range(dp_count)], "dp")
    id_rows = to_low(dense_first(hits_first, jnp.concatenate(found, 0)))
    id_rows = lax.fori_loop(1, rounds, fetch_more, id_rows)
    emb_all = id_rows[:length]
    target_rows = id_rows[length : length + slots].astype(jnp.float32)

    starts = [(tensor_index ^ s) * local_count for s in blocks]
    key_spots = jnp.concatenate([start + jnp.arange(local_count) for start in starts])
    key_segs = jnp.concatenate([lax.dynamic_slice_in_dim(segs, a, local_count) for a in starts])
    slot_local = [
        jnp.clip(comp_tree[s] - starts[s], 0, local_count - 1) for s in blocks
    ]
    row_index = jnp.concatenate([s * local_count + slot_local[s] for s in blocks])
    row_spots = jnp.concatenate([starts[s] + slot_local[s] for s in blocks])
    chosen = row_index[:, None] == jnp.arange(length)[None, :]
    row_segs = jnp.sum(jnp.where(chosen, key_segs[None, :], 0), 1)
    row_first = lookup(row_segs, parents[0])
    row_second = lookup(row_first, parents[0])
    key_facts = jnp.stack([key_spots, key_segs], 1)
    row_facts = jnp.stack(
        [row_spots, row_segs, row_first, row_second, row_index] + [jnp.zeros_like(row_index)] * 3
    )
    bias_query = lax.dynamic_slice_in_dim(vectors[4], tensor_index * width, width)
    bias_value = lax.dynamic_slice_in_dim(vectors[5], tensor_index * width, width)
    bias = jnp.concatenate([bias_query, jnp.zeros_like(bias_query), bias_value])[None]
    x_low, x_rows, emb_rows, queries, key_value, attn_low, lse_keys, full_in = attend(
        id_rows, pack_first, w_in.shape[0], width, bias, key_facts, row_facts, row_index[:, None]
    )
    z_part = to_low(dense_last(attn_low, full_proj_t))
    z_parts = exchange_blocks([z_part[s * slots : (s + 1) * slots] for s in blocks], "tensor")
    x_turned, emb_turned = x_low.T, emb_all.T
    z_parts[0], x_turned, emb_turned = together(z_parts[0], x_turned, emb_turned)
    z_branch = add_up(z_parts)
    pre_one = x_rows[:slots] + z_branch + vectors[6]
    h_one = layer_norm(pre_one, vectors[0], vectors[1])
    h_rows = jnp.concatenate(gather_blocks(to_low(h_one), "tensor"), 0)
    bias_up = lax.dynamic_slice_in_dim(
        vectors[8:].reshape(-1), tensor_index * hidden_share, hidden_share
    )
    upper = dense(h_rows, full_up) + bias_up
    act_low = to_low(gelu_tanh(upper))
    f_part = to_low(dense_last(act_low, full_down_t))
    f_branch = add_up(
        exchange_blocks([f_part[s * slots : (s + 1) * slots] for s in blocks], "tensor")
    )
    pre_two = h_one + f_branch + vectors[7]
    h_two = layer_norm(pre_two, vectors[2], vectors[3])
    h_two_low = to_low(h_two)
    rows_low = to_low(dense(h_two_low, full_out))

    rows_group = lax.all_gather(rows_low, "dp", axis=0, tiled=True)
    parts = head_forward(rows_group, table)
    both_rows = after(jnp.concatenate([h_two_low, rows_low], 1), parts)
    both_rows = gather_blocks(both_rows, "tensor")
    parts = lax.all_to_all(parts, "dp", 0, 0, tiled=True).reshape(dp_count, slots, -1)
    part_tops = join_low([parts[:, :, emb_width + i] for i in range(3)])
    part_sums = join_low([parts[:, :, emb_width + 3 + i] for i in range(3)])
    head_top = jnp.max(part_tops, 0)
    shares = jnp.exp(part_tops - head_top)
    total = jnp.sum(shares * part_sums, 0)
    lse = head_top + jnp.log(total)
    valid = comp_row >= 0
    target_logits = jnp.sum(rows_low.astype(jnp.float32) * target_rows, -1)
    loss_part = jnp.sum(jnp.where(valid, lse - target_logits, 0.0))
    slot_weight = 1.0 / (dp_count * tensor_count * slots)
    weight = jnp.where(valid, slot_weight, 0.0)
    mean = add_up(
        [parts[s, :, :emb_width] * (shares[s] / total)[:, None] for s in range(dp_count)]
    )
    out_low = to_low((mean - target_rows) * weight[:, None])

    shift = jnp.where(valid, lse - jnp.log(slot_weight), 1e30)
    shift = jnp.pad(jnp.stack(split_low(shift), 1), ((0, 0), (0, 125)))

    h_two_grad = dense_last(out_low, full_out)
    norm_two = jax.vjp(layer_norm, pre_two, vectors[2], vectors[3])[1]
    pre_two_grad, gain_two_grad, shift_two_grad = norm_two(h_two_grad)
    pre_two_grad, *both_rows = together(pre_two_grad, *both_rows)
    both_rows = jnp.concatenate(both_rows, 0)
    tree_rows = both_rows[:, model_width:]
    h_two_rows = both_rows[:, :model_width]
    f_rows = gather_blocks(jnp.concatenate([to_low(pre_two_grad), shift], 1), "tensor")
    f_rows = jnp.concatenate(f_rows, 0)
    rows_all = lax.all_gather(after(tree_rows, f_rows), "dp", axis=0, tiled=True)
    tree_shift = join_low([f_rows[:, model_width + i] for i in range(3)])
    f_rows = f_rows[:, :model_width]
    grad_down = dense_first(act_low, f_rows)
    act_grad = dense(f_rows, full_down_t)
    upper_low = to_low(jax.vjp(gelu_tanh, upper)[1](act_grad)[0])
    grad_up = dense_first(h_rows, upper_low)
    h_part = to_low(dense_last(upper_low, full_up))
    h_parts = exchange_blocks([h_part[s * slots : (s + 1) * slots] for s in blocks], "tensor")
    early = (3, 4)
    early_merged = [grad_up + error_up[0], grad_down + error_down[0]]
    early_lefts = [left_factor(*pair) for pair in zip(early_merged, (factor_up, factor_down[0]))]
    own_tree = jnp.arange(dp_count) == dp_index
    shift_all = jnp.where(own_tree[:, None], tree_shift[None], 0.0)
    early_lefts.append(shift_all.reshape(early_lefts[0].shape[0], -1))
    early_sizes = [left.shape[1] for left in early_lefts]
    early_lefts = jnp.concatenate(early_lefts, 1)
    h_parts[0], early_lefts = together(h_parts[0], early_lefts)
    h_one_grad = pre_two_grad + add_up(h_parts)
    norm_one = jax.vjp(layer_norm, pre_one, vectors[0], vectors[1])[1]
    pre_one_grad, gain_one_grad, shift_one_grad = norm_one(h_one_grad)
    z_low = to_low(pre_one_grad)
    z_rows = gather_blocks(jnp.concatenate([z_low, out_low], 1), "tensor")
    early_lefts = summed_over(early_lefts, "dp")
    z_rows[0], early_lefts, rows_all = together(z_rows[0], early_lefts, rows_all)
    *early_lefts, shift_all = columns_of(early_lefts, early_sizes)
    shift_all = shift_all.reshape(1, -1)
    z_rows = jnp.concatenate(z_rows, 0)
    out_rows = z_rows[:, model_width:]
    z_rows = z_rows[:, :model_width]
    query_grad, key_value_grad, x_part, row_part, emb_part = attend_back(
        z_rows,
        full_proj_t,
        queries,
        key_value,
        lse_keys,
        key_facts,
        row_facts,
        pack_first,
        full_in,
        pre_one_grad,
    )
    emb_parts = exchange_blocks(
        [emb_part[s * local_count : (s + 1) * local_count] for s in blocks], "tensor"
    )
    *early_lefts, emb_part = together(*early_lefts, emb_part)
    early_bases, early_terms = orthonormal_all(early_lefts)
    early_rights = [right_factor(*pair) for pair in zip(early_merged, early_bases)]
    early_sizes = [right.shape[1] for right in early_rights]
    early_rights = jnp.concatenate(early_rights, 1)
    emb_parts[1], query_grad, key_value_grad = together(emb_parts[1], query_grad, key_value_grad)
    value_grad = key_value_grad[:, width:]
    merged_qkv = [
        dense(left, right) + error_qkv[0, :, part]
        for part, (left, right) in enumerate(
            (
                (to_low(x_rows).T, query_grad),
                (x_turned, key_value_grad[:, :width]),
                (x_turned, value_grad),
            )
        )
    ]
    emb_parts[0], early_rights, *merged_qkv = together(emb_parts[0], early_rights, *merged_qkv)
    emb_grad_own = to_low(add_up(emb_parts))
    emb_grad = gather_blocks(emb_grad_own, "tensor")
    x_part, row_part, z_rows, out_rows, *merged_qkv = together(
        x_part, row_part, z_rows, out_rows, *merged_qkv, emb_grad_own
    )[:-1]
    grad_out = dense_first(h_two_rows, out_rows)
    grad_proj = dense_first(attn_low, z_rows)
    grad_in = dense(emb_turned, x_part) + dense_first(emb_rows, row_part)

    def placed(values, size, total_size):
        return lax.dynamic_update_slice_in_dim(
            jnp.zeros((total_size,), jnp.float32), values, tensor_index * size, 0
        )

    head_rows = jnp.stack(
        [
            gain_one_grad,
            shift_one_grad,
            gain_two_grad,
            shift_two_grad,
            placed(jnp.sum(query_grad.astype(jnp.float32), 0), width, model_width),
            placed(jnp.sum(value_grad.astype(jnp.float32), 0), width, model_width),
            jnp.sum(pre_one_grad, 0),
            jnp.sum(pre_two_grad, 0),
        ]
    )
    up_rows = placed(
        jnp.sum(upper_low.astype(jnp.float32), 0), hidden_share, hidden_share * tensor_count
    ).reshape(-1, model_width)
    loss_row = jnp.full((1, model_width), loss_part)
    vector_rows = [head_rows, up_rows, loss_row]
    spare = -sum(rows.shape[0] for rows in vector_rows) % factor_in.shape[1]
    vector_rows.append(jnp.zeros((spare, model_width), jnp.float32))
    vector_part = jnp.concatenate(vector_rows, 0)
    vector_part = jnp.concatenate(
        jnp.split(vector_part, vector_part.shape[0] // factor_in.shape[1], 0), 1
    )

    merged = (
        grad_in + error_in[0] * (1.0 / tensor_count),
        None,
        grad_proj + error_proj[0],
    ) + tuple(early_merged) + (grad_out + error_out[0],)
    factors = (
        factor_in,
        factor_qkv.reshape(3 * width, -1),
        factor_proj[0],
        None,
        None,
        factor_out,
    )
    bases = [None] * 6
    fresh = [None] * 6
    parts_of = [None] * 6
    late = (0, 1, 2, 5)
    lefts = [
        sum(left_factor(merged_qkv[part], factor_qkv[part]) for part in range(3))
        if index == 1
        else left_factor(merged[index], factors[index])
        for index in late
    ]
    sizes = [left.shape[1] for left in lefts] + [vector_part.shape[1]]
    emb_grad[1], lefts[1] = together(emb_grad[1], lefts[1])
    lefts.append(vector_part)
    lefts = jnp.concatenate(lefts + [early_rights], 1)
    lefts = lefts + swap(lefts, "dp", 1)
    *emb_grad[2:], lefts = together(*emb_grad[2:], lefts)
    lefts = summed_over(lefts, "dp", 2)
    tree_weight = jnp.where(comp_tree.reshape(-1) >= 0, slot_weight, 0.0)
    target_grad = to_low(tree_rows.astype(jnp.float32) * -tree_weight[:, None])
    id_grads = emb_grad + [target_grad]

    def deliver_more(turn, state):
        place = placed_ids(turn, owner)
        spots = exchanged(entries_of(listed(place))).reshape(-1) - vocab_start
        rows = exchanged(jnp.stack(listed_sums(place, id_grads, dp_count, share)))
        rows = rows.reshape(dp_count * share, -1).astype(jnp.float32)
        rows = jnp.where((spots >= 0)[:, None], rows, 0.0)
        spots = jnp.clip(spots, 0, shard_rows - 1)
        return state[0].at[spots].add(-table_rate * rows), state[1].at[spots].add(rows)

    added = exchange_blocks(listed_sums(place_first, id_grads, dp_count, share), "dp")
    added[1], lefts = together(added[1], lefts)
    lefts = columns_of(lefts, sizes + early_sizes)
    vector_sum = lefts[len(sizes) - 1]
    flat = gather_blocks(lefts[0], "tensor")
    early_rights = lefts[len(sizes) :]
    early_parts = columns_of(outer_terms(jnp.concatenate(early_rights, 1)), early_sizes)

    def error_left(index):
        return merged[index] - dense_first(bases[index], parts_of[index]) * (1.0 / dp_count)

    errors_new = [None] * 6
    for i, index in enumerate(early):
        bases[index] = early_terms[i]
        fresh[index] = early_rights[i]
        parts_of[index] = early_parts[i]
    errors_new[early[0]] = error_left(early[0])
    flat[0], errors_new[early[0]] = together(flat[0], errors_new[early[0]])
    flat = add_pairs(flat)
    found_bases, found_terms = orthonormal_all([flat[:, : sizes[0]]] + lefts[1 : len(late)])
    rights = [
        jnp.concatenate([right_factor(merged_qkv[part], found_bases[i]) for part in range(3)], 1)
        if index == 1
        else right_factor(merged[index], found_bases[i])
        for i, index in enumerate(late)
    ]
    sizes = [right.shape[1] for right in rights]
    rights = jnp.concatenate(rights, 1)
    rights, held = together(rights, early_parts[1])
    parts_of[early[1]] = held
    errors_new[early[1]] = error_left(early[1])
    rights = summed_over(rights, "dp")
    grad_in_own = lax.psum_scatter(
        after(to_low(grad_in), emb_grad[-1]), "tensor", scatter_dimension=0, tiled=True
    )
    grad_in_sum = lax.all_gather(grad_in_own, "tensor", axis=0, tiled=True)
    right_in = gather_blocks(jnp.concatenate([rights[:, : sizes[0]], vector_sum], 1), "tensor")
    added[0], rights, errors_new[3], errors_new[4] = together(
        added[0], rights, errors_new[3], errors_new[4]
    )
    updated = list(
        table_update(rows_all, shift_all, added, asked_first.reshape(1, -1) - vocab_start, table, table_moment)
    )
    updated[0], right_in[0], grad_in_sum = together(updated[0], right_in[0], grad_in_sum)
    new_table, new_table_moment = lax.fori_loop(1, rounds, deliver_more, tuple(updated))
    rights = columns_of(rights, sizes)
    right_in = add_pairs(right_in)
    rights[0], vector_sum = right_in[:, : sizes[0]], right_in[:, sizes[0] :]
    vector_sum = jnp.concatenate(jnp.split(vector_sum, vector_sum.shape[1] // model_width, 1), 0)
    right_parts = columns_of(outer_terms(jnp.concatenate(rights, 1)), sizes)
    for i, index in enumerate(late):
        bases[index] = found_terms[i]
        fresh[index] = rights[i]
        parts_of[index] = right_parts[i]
    merged = (grad_in_sum.astype(jnp.float32) + error_in[0],) + merged[1:]
    for index in (0, 2, 5):
        errors_new[index] = error_left(index)
    errors_new[1] = jnp.stack(
        [
            merged_qkv[part]
            - dense_first(bases[1], parts_of[1][:, part * width : (part + 1) * width])
            * (1.0 / dp_count)
            for part in range(3)
        ],
        0,
    ).transpose(1, 0, 2)

    def shard(index, size, axis):
        left, right = bases[index], parts_of[index]
        if axis == 0:
            left = lax.dynamic_slice_in_dim(left, dp_index * size, size, 1)
        else:
            right = lax.dynamic_slice_in_dim(right, dp_index * size, size, 1)
        return dense_first(left, right)

    shard_in = shard(0, w_in.shape[0], 0)
    shard_qkv = shard(1, shard_width, 0)
    shard_qkv = jnp.stack(
        [shard_qkv[:, part * width : (part + 1) * width] for part in range(3)], 1
    )
    shard_proj = shard(2, w_proj.shape[1], 1)
    shard_up = shard(3, w_up.shape[0], 0)
    shard_down = shard(4, w_down.shape[1], 1)
    shard_out = shard(5, w_out.shape[0], 0)
    fresh = [values.T for values in fresh]
    loss_sum = vector_sum[vectors.shape[0], 0]
    vector_grad = vector_sum[: vectors.shape[0]]
    new_w_in, new_moment_in = advance(w_in, moment_in, shard_in, matrix_rates[0])
    new_w_qkv, new_moment_qkv = advance(w_qkv, moment_qkv, shard_qkv, matrix_rates[1])
    new_w_proj, new_moment_proj = advance(w_proj, moment_proj, shard_proj, matrix_rates[2])
    new_w_up, new_moment_up = advance(w_up, moment_up, shard_up, matrix_rates[3])
    new_w_down, new_moment_down = advance(w_down, moment_down, shard_down, matrix_rates[4])
    new_w_out, new_moment_out = advance(w_out, moment_out, shard_out, matrix_rates[5])
    new_vectors, new_vector_moment = advance(vectors, vector_moment, vector_grad, vector_rate)
    return (
        loss_sum,
        new_table,
        new_table_moment,
        new_vectors,
        new_vector_moment,
        new_w_in,
        new_moment_in,
        errors_new[0][None],
        fresh[0],
        new_w_qkv,
        new_moment_qkv,
        errors_new[1].reshape(1, model_width, 3, width),
        fresh[1].reshape(3, width, -1),
        new_w_proj,
        new_moment_proj,
        errors_new[2][None],
        fresh[2][None],
        new_w_up,
        new_moment_up,
        errors_new[3][None],
        fresh[3],
        new_w_down,
        new_moment_down,
        errors_new[4][None],
        fresh[4][None],
        new_w_out,
        new_moment_out,
        errors_new[5][None],
        fresh[5],
    )


def solution(mesh):
    return jax.shard_map(
        per_device,
        mesh=mesh,
        in_specs=(
            P("dp", "tensor"),
            P("dp", None),
            P("dp", None),
            P("dp", "tensor"),
            P("dp", "tensor"),
            P("dp", None),
            P("dp", None),
            P(),
            P(),
            P("dp", None),
            P("dp", None),
            P("dp", None, None),
            P(),
            P("dp", None, "tensor"),
            P("dp", None, "tensor"),
            P("dp", None, None, "tensor"),
            P(None, "tensor", None),
            P("tensor", "dp"),
            P("tensor", "dp"),
            P("dp", "tensor", None),
            P("tensor", None, None),
            P("dp", "tensor"),
            P("dp", "tensor"),
            P("dp", None, "tensor"),
            P("tensor", None),
            P("tensor", "dp"),
            P("tensor", "dp"),
            P("dp", "tensor", None),
            P("tensor", None, None),
            P("dp", None),
            P("dp", None),
            P("dp", None, None),
            P(),
        ),
        out_specs=(
            P(),
            P("dp", None),
            P("dp", None),
            P(),
            P(),
            P("dp", None),
            P("dp", None),
            P("dp", None, None),
            P(),
            P("dp", None, "tensor"),
            P("dp", None, "tensor"),
            P("dp", None, None, "tensor"),
            P(None, "tensor", None),
            P("tensor", "dp"),
            P("tensor", "dp"),
            P("dp", "tensor", None),
            P("tensor", None, None),
            P("dp", "tensor"),
            P("dp", "tensor"),
            P("dp", None, "tensor"),
            P("tensor", None),
            P("tensor", "dp"),
            P("tensor", "dp"),
            P("dp", "tensor", None),
            P("tensor", None, None),
            P("dp", None),
            P("dp", None),
            P("dp", None, None),
            P(),
        ),
        check_vma=False,
    )
```

```python
import functools

import jax
import jax.numpy as jnp
from jax import lax
from jax.experimental import pallas as pl
from jax.experimental.pallas import tpu as pltpu
from jax.sharding import PartitionSpec as P

HD = 64


momentum_decay = 0.9
table_rate = 300.0
vector_rate = 1000.0
matrix_rates = (1500.0, 80.0, 3000.0, 80.0, 40.0, 80.0)


def to_low(values):
    return values.astype(jnp.bfloat16)


def dense(left, right):
    return jnp.dot(left, right, preferred_element_type=jnp.float32)


def dense_first(left, right):
    return lax.dot_general(
        left, right, (((0,), (0,)), ((), ())), preferred_element_type=jnp.float32
    )


def dense_last(left, right):
    return lax.dot_general(
        left, right, (((1,), (1,)), ((), ())), preferred_element_type=jnp.float32
    )


left_terms = (0, 0, 1, 1, 0, 2)
right_terms = (0, 1, 0, 1, 2, 0)


def two_terms(values, axis):
    first = coarse(values)
    return to_low(jnp.concatenate([first, values - first], axis))


def left_factor(merged, factor):
    count = factor.shape[1]
    both = lax.dot_general(
        two_terms(factor, 1),
        to_low(merged),
        (((0,), (1,)), ((), ())),
        preferred_element_type=jnp.float32,
    )
    return both[:count] + both[count:]


def right_factor(merged, basis):
    both = dense(two_terms(basis, 0), to_low(merged))
    return both[: basis.shape[0]] + both[basis.shape[0] :]


def layer_norm(values, gain, shift):
    center = values - jnp.mean(values, -1, keepdims=True)
    spread = jnp.mean(center * center, -1, keepdims=True)
    return center * lax.rsqrt(spread + 1e-05) * gain + shift


def gelu_tanh(values):
    return jax.nn.gelu(values, approximate=True)


def swap(values, axis, step):
    return lax.ppermute(values, axis, [(i, i ^ step) for i in range(lax.axis_size(axis))])


def gather_blocks(values, axis):
    return [values] + [swap(values, axis, s) for s in range(1, lax.axis_size(axis))]


def exchange_blocks(blocks, axis):
    return [blocks[0]] + [swap(blocks[s], axis, s) for s in range(1, lax.axis_size(axis))]


def summed_over(values, axis, step=1):
    while step < lax.axis_size(axis):
        values = jax.tree.map(lambda a, s=step: a + swap(a, axis, s), values)
        step *= 2
    return values


def add_up(parts):
    total = parts[0].astype(jnp.float32)
    for part in parts[1:]:
        total = total + part.astype(jnp.float32)
    return total


def add_pairs(parts):
    while len(parts) > 1:
        parts = [left + right for left, right in zip(parts[::2], parts[1::2])]
    return parts[0]


def orthonormal_kernel(*refs):
    many = len(refs) // 3
    left_refs, basis_refs, term_refs = refs[:many], refs[many : 2 * many], refs[2 * many :]
    count = left_refs[0].shape[0]
    longest = max(ref.shape[1] for ref in left_refs)

    def row(ref, index):
        values = ref[index : index + 1, :]
        short = longest - values.shape[1]
        if short == 0:
            return values
        return jnp.concatenate([values, jnp.zeros((1, short), jnp.float32)], 1)

    columns = [jnp.concatenate([row(ref, k) for ref in left_refs], 0) for k in range(count)]
    for index in range(count):
        vector = columns[index]
        vector = vector * lax.rsqrt(jnp.sum(vector * vector, -1, keepdims=True) + 1e-06)
        for place, ref in enumerate(basis_refs):
            ref[index : index + 1, :] = vector[place : place + 1, : ref.shape[1]]
        for later in range(index + 1, count):
            other = columns[later]
            columns[later] = other - jnp.sum(vector * other, -1, keepdims=True) * vector
    for basis_ref, term_ref in zip(basis_refs, term_refs):
        rest = basis_ref[...]
        terms = []
        for _ in range(3):
            terms.append(rest.astype(jnp.bfloat16).astype(jnp.float32))
            rest = rest - terms[-1]
        term_ref[...] = jnp.concatenate([terms[term] for term in left_terms], 0).astype(
            jnp.bfloat16
        )


def orthonormal_all(lefts):
    count = lefts[0].shape[0]
    bases = [jax.ShapeDtypeStruct(left.shape, jnp.float32) for left in lefts]
    terms = [
        jax.ShapeDtypeStruct((len(left_terms) * count, left.shape[1]), jnp.bfloat16)
        for left in lefts
    ]
    both = pl.pallas_call(orthonormal_kernel, out_shape=bases + terms)(*lefts)
    return both[: len(lefts)], both[len(lefts) :]


def outer_terms(rights):
    terms = split_low(rights)
    return jnp.concatenate([terms[term] for term in right_terms], 0)


def coarse(values):
    return lax.reduce_precision(values, 8, 7)


def split_low(values):
    first = coarse(values)
    second = coarse(values - first)
    return [to_low(first), to_low(second), to_low(values - first - second)]


def join_low(terms):
    terms = [term.astype(jnp.float32) for term in terms]
    return terms[0] + (terms[1] + terms[2])


def vocab_tile(shard_rows, most=640):
    tiles = -(-shard_rows // most)
    return -(-(-(-shard_rows // tiles)) // 16) * 16


def head_kernel(shard_rows, rows_ref, table_ref, out_ref, total, stats):
    step = pl.program_id(0)
    tile_rows, wide = table_ref.shape

    @pl.when(step == 0)
    def _():
        total[...] = jnp.zeros_like(total)
        stats[0:1, :] = jnp.full((1, stats.shape[1]), -1e30, jnp.float32)
        stats[1:2, :] = jnp.zeros((1, stats.shape[1]), jnp.float32)

    row_ids = step * tile_rows + lax.broadcasted_iota(jnp.int32, (tile_rows, 1), 0)
    present = row_ids < shard_rows
    tile = jnp.where(present, table_ref[...], 0.0).astype(jnp.bfloat16)
    logits = lax.dot_general(
        tile, rows_ref[...], (((1,), (1,)), ((), ())), preferred_element_type=jnp.float32
    )
    logits = jnp.where(present, logits, -1e30)
    before = stats[0:1, :]
    top = jnp.maximum(before, jnp.max(logits, 0, keepdims=True))
    fade = jnp.exp(before - top)
    expo = jnp.exp(logits - top)
    stats[0:1, :] = top
    stats[1:2, :] = stats[1:2, :] * fade + jnp.sum(expo, 0, keepdims=True)
    total[...] = total[...] * fade + lax.dot_general(
        tile,
        expo.astype(jnp.bfloat16),
        (((0,), (0,)), ((), ())),
        preferred_element_type=jnp.float32,
    )

    @pl.when(step == pl.num_programs(0) - 1)
    def _():
        out_ref[:, :wide] = total[...].T.astype(jnp.bfloat16)
        terms = []
        for index in (0, 1):
            value = stats[index : index + 1, :]
            for _ in range(3):
                part = value.astype(jnp.bfloat16).astype(jnp.float32)
                terms.append(part)
                value = value - part
        spare = jnp.zeros((out_ref.shape[1] - wide - 6, value.shape[1]), jnp.float32)
        out_ref[:, wide:] = jnp.concatenate(terms + [spare], 0).T.astype(jnp.bfloat16)


def head_forward(rows, table):
    count, wide = rows.shape
    shard_rows = table.shape[0]
    tile = vocab_tile(shard_rows, 1280 if count <= 1024 else 640)
    return pl.pallas_call(
        functools.partial(head_kernel, shard_rows),
        grid=(pl.cdiv(shard_rows, tile),),
        in_specs=[
            pl.BlockSpec((count, wide), lambda i: (0, 0)),
            pl.BlockSpec((tile, wide), lambda i: (i, 0)),
        ],
        out_specs=pl.BlockSpec((count, wide + 128), lambda i: (0, 0)),
        out_shape=jax.ShapeDtypeStruct((count, wide + 128), jnp.bfloat16),
        scratch_shapes=[
            pltpu.VMEM((wide, count), jnp.float32),
            pltpu.VMEM((8, count), jnp.float32),
        ],
        compiler_params=pltpu.CompilerParams(vmem_limit_bytes=18 * 2**20 + 24 * tile * count + 10 * count * wide),
        cost_estimate=pl.CostEstimate(
            flops=4 * shard_rows * count * wide,
            bytes_accessed=4 * shard_rows * wide,
            transcendentals=shard_rows * count,
        ),
    )(rows, table)


def table_kernel(rows_ref, shift_ref, ids_ref, table_ref, moment_ref, *refs):
    parts, (new_table_ref, new_moment_ref, added_ref) = refs[:-3], refs[-3:]
    tile_rows, wide = table_ref.shape

    @pl.when(pl.program_id(0) == 0)
    def _():
        for index, part in enumerate(parts):
            count = part.shape[0]
            added_ref[index * count : (index + 1) * count, :] = part[...]

    row_ids = pl.program_id(0) * tile_rows
    row_ids = row_ids + lax.broadcasted_iota(jnp.int32, (tile_rows, 1), 0)
    hits = (row_ids == ids_ref[...]).astype(jnp.bfloat16)
    new_moment_ref[...] = momentum_decay * moment_ref[...] + dense(hits, added_ref[...])
    tile = table_ref[...].astype(jnp.bfloat16)
    chunk = min(512, rows_ref.shape[0])

    def one(spot):
        rows = rows_ref[spot, :]
        grad = jnp.exp(dense_last(tile, rows) - shift_ref[0:1, spot])
        return dense(grad.astype(jnp.bfloat16), rows)

    together = 4 * chunk if rows_ref.shape[0] % (4 * chunk) == 0 else chunk

    def some(index, carry):
        begin = pl.multiple_of(index * together, together)
        parts = [one(pl.ds(begin + k * chunk, chunk)) for k in range(together // chunk)]
        new_moment_ref[...] += sum(parts[1:], parts[0])
        return carry

    if rows_ref.shape[0] == together:
        some(0, 0)
    else:
        lax.fori_loop(0, rows_ref.shape[0] // together, some, 0)
    new_table_ref[...] = table_ref[...] - table_rate * new_moment_ref[...]


def table_update(rows, shift, added, ids, table, moment):
    shard_rows, wide = table.shape
    tile = vocab_tile(shard_rows)
    whole = lambda array: pl.BlockSpec(
        array.shape, lambda i: (0, 0), pipeline_mode=pl.Buffered(buffer_count=1)
    )
    part = pl.BlockSpec((tile, wide), lambda i: (i, 0))
    return pl.pallas_call(
        table_kernel,
        grid=(pl.cdiv(shard_rows, tile),),
        in_specs=[whole(rows), whole(shift), whole(ids), part, part] + [whole(a) for a in added],
        out_specs=[part, part],
        out_shape=[jax.ShapeDtypeStruct(table.shape, jnp.float32)] * 2,
        scratch_shapes=[pltpu.VMEM((ids.shape[1], wide), jnp.bfloat16)],
        compiler_params=pltpu.CompilerParams(vmem_limit_bytes=56 * 2**20),
        cost_estimate=pl.CostEstimate(
            flops=shard_rows * wide * (4 * rows.shape[0] + 2 * ids.shape[1]),
            bytes_accessed=16 * shard_rows * wide,
            transcendentals=shard_rows * rows.shape[0],
        ),
    )(rows, shift, ids, table, moment, *added)


def visible_pairs(key_ref, row_ref):
    spots, segs = key_ref[:, 0:1], key_ref[:, 1:2]
    related = (segs == row_ref[1:2, :]) | (segs == row_ref[2:3, :]) | (segs == row_ref[3:4, :])
    return related & (spots <= row_ref[0:1, :])


def head_columns(width, head):
    columns = lax.broadcasted_iota(jnp.int32, (1, width), 1)
    return (columns >= head * HD) & (columns < (head + 1) * HD)


def attend_kernel(
    shard_in,
    emb_ref,
    pack_ref,
    bias_ref,
    key_ref,
    row_ref,
    index_ref,
    x_ref,
    x_rows_ref,
    emb_rows_ref,
    query_ref,
    key_value_ref,
    attn_ref,
    lse_ref,
    in_ref,
):
    length = x_ref.shape[0]
    count, width = query_ref.shape
    block = min(256, length)
    share = pack_ref.shape[1] - 4 * width
    halves = in_ref.shape[1] // share
    for owner in range(in_ref.shape[0] // shard_in):
        for part in range(halves):
            begin = (owner * halves + part) * shard_in
            in_ref[owner * shard_in : (owner + 1) * shard_in, part * share : (part + 1) * share] = (
                pack_ref[begin : begin + shard_in, :share]
            )

    def one_block(index, carry):
        spot = pl.ds(pl.multiple_of(index * block, block), block)
        x_low = to_low(dense(emb_ref[spot, :], in_ref[...]))
        x_ref[spot, :] = x_low
        mixed = dense(x_low, pack_ref[:, share + width : share + 3 * width]) + bias_ref[:, width:]
        key_value_ref[spot, :] = to_low(mixed)
        return carry

    lax.fori_loop(0, length // block, one_block, 0)
    chosen = index_ref[...] == lax.broadcasted_iota(jnp.int32, (count, length), 1)
    emb_rows = to_low(dense(chosen.astype(jnp.bfloat16), emb_ref[:length, :]))
    emb_rows_ref[...] = emb_rows
    x_rows = dense(emb_rows, in_ref[...])
    x_rows_ref[...] = x_rows
    queries = to_low(dense(to_low(x_rows), pack_ref[:, share : share + width]) + bias_ref[:, :width])
    query_ref[...] = queries
    keys_all = key_value_ref[:, :width]
    values_turned = key_value_ref[:, width:].T
    blocked = jnp.where(visible_pairs(key_ref, row_ref), 0.0, -1e30)
    features = lax.broadcasted_iota(jnp.int32, (width, 1), 0)
    attended = jnp.zeros((width, count), jnp.float32)
    for head in range(width // HD):
        own = jnp.where(head_columns(width, head), queries, jnp.zeros_like(queries))
        scores = dense_last(keys_all, own) * HD ** (-0.5) + blocked
        top = jnp.max(scores, 0, keepdims=True)
        expo = jnp.exp(scores - top)
        total = jnp.sum(expo, 0, keepdims=True)
        lse_ref[head : head + 1, :] = top + jnp.log(total)
        result = dense(values_turned, to_low(expo / total))
        mine = (features >= head * HD) & (features < (head + 1) * HD)
        attended = jnp.where(mine, result, attended)
    attn_ref[...] = to_low(attended.T)


def attend(id_rows, pack, shard_in, width, bias, key_facts, row_facts, row_index):
    emb_width = id_rows.shape[1]
    model_width = pack.shape[0]
    length = key_facts.shape[0]
    count = row_index.shape[0]
    low = lambda *shape: jax.ShapeDtypeStruct(shape, jnp.bfloat16)
    full = lambda *shape: jax.ShapeDtypeStruct(shape, jnp.float32)
    return pl.pallas_call(
        functools.partial(attend_kernel, shard_in),
        out_shape=[
            low(length, model_width),
            full(count, model_width),
            low(count, emb_width),
            low(count, width),
            low(length, 2 * width),
            low(count, width),
            full(8, count),
            low(emb_width, model_width),
        ],
        compiler_params=pltpu.CompilerParams(vmem_limit_bytes=48 * 2**20),
        cost_estimate=pl.CostEstimate(
            flops=2 * length * model_width * (emb_width + 2 * width) + 4 * length * count * width,
            bytes_accessed=2 * length * (emb_width + model_width + 2 * width),
            transcendentals=length * count * width // HD,
        ),
    )(id_rows, pack, bias, key_facts, row_facts, row_index)


def attend_back_kernel(
    z_ref,
    proj_ref,
    query_ref,
    key_value_ref,
    lse_ref,
    key_ref,
    row_ref,
    pack_ref,
    in_ref,
    pre_ref,
    query_grad_ref,
    key_value_grad_ref,
    x_part_ref,
    row_part_ref,
    emb_part_ref,
):
    count, width = query_ref.shape
    length = key_value_ref.shape[0]
    slots = pre_ref.shape[0]
    share = pack_ref.shape[1] - 4 * width
    scale = HD ** (-0.5)
    queries = query_ref[...]
    keys_all = key_value_ref[:, :width]
    values_all = key_value_ref[:, width:]
    keys_turned = keys_all.T
    attn_grad = to_low(dense(z_ref[...], proj_ref[...]))
    blocked = jnp.where(visible_pairs(key_ref, row_ref), 0.0, -1e30)
    features = lax.broadcasted_iota(jnp.int32, (width, 1), 0)
    key_grad = jnp.zeros((length, width), jnp.float32)
    value_grad = jnp.zeros((length, width), jnp.float32)
    query_grad = jnp.zeros((width, count), jnp.float32)
    for head in range(width // HD):
        mine = head_columns(width, head)
        own = jnp.where(mine, queries, jnp.zeros_like(queries))
        own_grad = jnp.where(mine, attn_grad, jnp.zeros_like(attn_grad))
        scores = dense_last(keys_all, own) * scale + blocked
        probs = jnp.exp(scores - lse_ref[head : head + 1, :])
        probs_grad = dense_last(values_all, own_grad)
        rowdot = jnp.sum(probs * probs_grad, 0, keepdims=True)
        scores_grad = to_low(probs * (probs_grad - rowdot))
        value_grad += dense(to_low(probs), own_grad)
        key_grad += dense(scores_grad, own)
        rows = (features >= head * HD) & (features < (head + 1) * HD)
        query_grad = jnp.where(rows, dense(keys_turned, scores_grad), query_grad)
    query_grad = to_low((query_grad * scale).T)
    query_grad_ref[...] = query_grad
    key_value_grad_ref[:, :width] = to_low(key_grad * scale)
    key_value_grad_ref[:, width:] = to_low(value_grad)
    row_part = dense_last(query_grad, pack_ref[:, share : share + width])
    row_part_ref[:slots, :] = to_low(row_part[:slots] + pre_ref[...])
    row_part_ref[slots:, :] = to_low(row_part[slots:])
    row_emb = to_low(dense_last(row_part_ref[...], in_ref[...]))
    block = min(256, length)

    def one_block(index, carry):
        begin = pl.multiple_of(index * block, block)
        spot = pl.ds(begin, block)
        x_part = to_low(dense_last(key_value_grad_ref[spot, :], pack_ref[:, share + width : share + 3 * width]))
        x_part_ref[spot, :] = x_part
        places = begin + lax.broadcasted_iota(jnp.int32, (block, 1), 0)
        chosen = (places == row_ref[4:5, :]).astype(jnp.bfloat16)
        emb_part_ref[spot, :] = to_low(dense_last(x_part, in_ref[...]) + dense(chosen, row_emb))
        return carry

    lax.fori_loop(0, length // block, one_block, 0)


def attend_back(
    z_rows, own_proj_t, queries, key_value, lse, key_facts, row_facts, pack, full_in, pre_grad
):
    count, width = queries.shape
    length = key_value.shape[0]
    emb_width, model_width = full_in.shape
    low = lambda *shape: jax.ShapeDtypeStruct(shape, jnp.bfloat16)
    return pl.pallas_call(
        attend_back_kernel,
        out_shape=[
            low(count, width),
            low(length, 2 * width),
            low(length, model_width),
            low(count, model_width),
            low(length, emb_width),
        ],
        compiler_params=pltpu.CompilerParams(vmem_limit_bytes=48 * 2**20),
        cost_estimate=pl.CostEstimate(
            flops=2 * length * model_width * (emb_width + 2 * width) + 10 * length * count * width,
            bytes_accessed=2 * length * (emb_width + model_width + 2 * width),
            transcendentals=length * count * width // HD,
        ),
    )(z_rows, own_proj_t, queries, key_value, lse, key_facts, row_facts, pack, full_in, pre_grad)


def listed_kernel(many, *refs):
    place_ref, block_refs, out_refs = refs[0], refs[1 : 1 + many], refs[1 + many :]
    share = out_refs[0].shape[0]
    entries = lax.broadcasted_iota(jnp.int32, (share * len(out_refs), 1), 0)
    total = None
    begin = 0
    for ref in block_refs:
        stop = begin + ref.shape[0]
        hits = (entries == place_ref[:, begin:stop]).astype(jnp.bfloat16)
        part = dense(hits, ref[...])
        total = part if total is None else total + part
        begin = stop
    total = to_low(total)
    for owner, ref in enumerate(out_refs):
        ref[...] = total[owner * share : (owner + 1) * share]


def listed_sums(place, blocks, owners, share):
    wide = blocks[0].shape[1]
    return pl.pallas_call(
        functools.partial(listed_kernel, len(blocks)),
        out_shape=[jax.ShapeDtypeStruct((share, wide), jnp.bfloat16)] * owners,
        compiler_params=pltpu.CompilerParams(vmem_limit_bytes=40 * 2**20),
        cost_estimate=pl.CostEstimate(flops=1, bytes_accessed=1, transcendentals=1),
    )(place[None], *blocks)


def lookup(codes, table_row):
    hits = codes[:, None] == jnp.arange(table_row.shape[0])[None, :]
    return jnp.sum(jnp.where(hits, table_row[None, :], 0), 1)


def after(values, *others):
    return lax.optimization_barrier((values, *others))[0]


def together(*values):
    return lax.optimization_barrier(values)


def columns_of(values, sizes):
    cuts = [sum(sizes[:i]) for i in range(len(sizes) + 1)]
    return [values[:, cuts[i] : cuts[i + 1]] for i in range(len(sizes))]


def advance(weight, moment, approx, rate):
    fresh_moment = momentum_decay * moment + approx
    return (weight - rate * fresh_moment, fresh_moment)


def per_device(
    tokens,
    segments,
    parents,
    completion,
    targets,
    table,
    table_moment,
    vectors,
    vector_moment,
    w_in,
    moment_in,
    error_in,
    factor_in,
    w_qkv,
    moment_qkv,
    error_qkv,
    factor_qkv,
    w_proj,
    moment_proj,
    error_proj,
    factor_proj,
    w_up,
    moment_up,
    error_up,
    factor_up,
    w_down,
    moment_down,
    error_down,
    factor_down,
    w_out,
    moment_out,
    error_out,
    factor_out,
):
    dp_count = lax.axis_size("dp")
    tensor_count = lax.axis_size("tensor")
    dp_index = lax.axis_index("dp")
    tensor_index = lax.axis_index("tensor")
    token_ids = tokens[0]
    comp_row = completion[0]
    target_row = targets[0]
    local_count = token_ids.shape[0]
    slots = comp_row.shape[0]
    segs = segments[0]
    length = segs.shape[0]
    shard_rows, emb_width = table.shape
    vocab_start = dp_index * shard_rows
    width = w_qkv.shape[2]
    hidden_share = w_up.shape[1]
    model_width = vectors.shape[1]
    heads_here = width // HD
    scale = HD ** (-0.5)
    shard_width = w_qkv.shape[0]
    blocks = range(tensor_count)

    meta = gather_blocks(jnp.concatenate([token_ids, comp_row, target_row]), "tensor")

    halves = shard_width // w_in.shape[0]
    share_in = model_width // halves
    in_low = to_low(w_in)
    in_stack = jnp.concatenate(
        [in_low[:, h * share_in : (h + 1) * share_in] for h in range(halves)], 0
    )
    qkv_low = to_low(w_qkv).reshape(shard_width, 3 * width)
    pack_first = lax.all_gather(
        jnp.concatenate([in_stack, qkv_low, to_low(w_proj).T], 1), "dp", axis=0, tiled=True
    )
    pack_rest = lax.all_gather(
        jnp.concatenate([to_low(w_up), to_low(w_down).T, to_low(w_out)], 1),
        "dp",
        axis=0,
        tiled=True,
    )
    full_proj_t = pack_first[:, share_in + 3 * width :]
    full_up = pack_rest[:, :hidden_share]
    full_down_t = pack_rest[:, hidden_share : 2 * hidden_share]
    full_out = pack_rest[:, 2 * hidden_share :]

    meta = jnp.stack(meta)
    comp_tree = meta[:, local_count : local_count + slots]
    ids = jnp.concatenate(
        [meta[:, :local_count].reshape(-1), meta[:, local_count + slots :].reshape(-1)]
    )

    id_count = ids.shape[0]
    share = -(-9 * id_count // (160 * dp_count)) * 16
    owner = ids // shard_rows
    order = jnp.arange(id_count)
    before = order[None, :] < order[:, None]
    same = ids[:, None] == ids[None, :]
    first_one = ~jnp.any(same & before, 1)
    rank = jnp.sum((owner[:, None] == owner[None, :]) & before & first_one[None, :], 1)
    rank = jnp.sum(jnp.where(same & first_one[None, :], rank[None, :], 0), 1)
    rounds_here = jnp.max(rank) // share + 1

    def placed_ids(turn, owners):
        place = rank - turn * share
        return jnp.where((place >= 0) & (place < share), owners * share + place, -1)

    def listed(place):
        return place[None, :] == jnp.arange(dp_count * share)[:, None]

    def entries_of(hits):
        return jnp.max(jnp.where(hits, ids[None, :], -1), 1).reshape(dp_count, share)

    def picked_rows(asked, kind):
        spots = jnp.clip(asked - vocab_start, 0, shard_rows - 1)
        return jnp.take(table, spots.reshape(-1), axis=0).astype(kind).reshape(dp_count, share, -1)

    def exchanged(values):
        return lax.all_to_all(values, "dp", 0, 0, tiled=True)

    place_first = placed_ids(0, owner ^ dp_index)
    hits_first = listed(place_first)
    entries = entries_of(hits_first)
    hits_first = hits_first.astype(jnp.bfloat16)
    notes = [jnp.concatenate([entries[s], rounds_here[None]]) for s in range(dp_count)]
    notes = jnp.stack(exchange_blocks(notes, "dp"))
    asked_first = notes[:, :share]
    rounds = jnp.max(notes[:, share])

    def fetch_more(turn, rows):
        hits = listed(placed_ids(turn, owner))
        found = exchanged(picked_rows(exchanged(entries_of(hits)), jnp.float32))
        found = to_low(coarse(found.reshape(dp_count * share, -1)))
        return rows + to_low(dense_first(hits.astype(jnp.bfloat16), found))

    found = picked_rows(asked_first, jnp.bfloat16)
    found = exchange_blocks([found[s] for s in range(dp_count)], "dp")
    id_rows = to_low(dense_first(hits_first, jnp.concatenate(found, 0)))
    id_rows = lax.fori_loop(1, rounds, fetch_more, id_rows)
    emb_all = id_rows[:length]
    target_rows = id_rows[length : length + slots].astype(jnp.float32)

    starts = [(tensor_index ^ s) * local_count for s in blocks]
    key_spots = jnp.concatenate([start + jnp.arange(local_count) for start in starts])
    key_segs = jnp.concatenate([lax.dynamic_slice_in_dim(segs, a, local_count) for a in starts])
    slot_local = [
        jnp.clip(comp_tree[s] - starts[s], 0, local_count - 1) for s in blocks
    ]
    row_index = jnp.concatenate([s * local_count + slot_local[s] for s in blocks])
    row_spots = jnp.concatenate([starts[s] + slot_local[s] for s in blocks])
    chosen = row_index[:, None] == jnp.arange(length)[None, :]
    row_segs = jnp.sum(jnp.where(chosen, key_segs[None, :], 0), 1)
    row_first = lookup(row_segs, parents[0])
    row_second = lookup(row_first, parents[0])
    key_facts = jnp.stack([key_spots, key_segs], 1)
    row_facts = jnp.stack(
        [row_spots, row_segs, row_first, row_second, row_index] + [jnp.zeros_like(row_index)] * 3
    )
    bias_query = lax.dynamic_slice_in_dim(vectors[4], tensor_index * width, width)
    bias_value = lax.dynamic_slice_in_dim(vectors[5], tensor_index * width, width)
    bias = jnp.concatenate([bias_query, jnp.zeros_like(bias_query), bias_value])[None]
    x_low, x_rows, emb_rows, queries, key_value, attn_low, lse_keys, full_in = attend(
        id_rows, pack_first, w_in.shape[0], width, bias, key_facts, row_facts, row_index[:, None]
    )
    z_part = to_low(dense_last(attn_low, full_proj_t))
    z_parts = exchange_blocks([z_part[s * slots : (s + 1) * slots] for s in blocks], "tensor")
    x_turned, emb_turned = x_low.T, emb_all.T
    z_parts[0], x_turned, emb_turned = together(z_parts[0], x_turned, emb_turned)
    z_branch = add_up(z_parts)
    pre_one = x_rows[:slots] + z_branch + vectors[6]
    h_one = layer_norm(pre_one, vectors[0], vectors[1])
    h_rows = jnp.concatenate(gather_blocks(to_low(h_one), "tensor"), 0)
    bias_up = lax.dynamic_slice_in_dim(
        vectors[8:].reshape(-1), tensor_index * hidden_share, hidden_share
    )
    upper = dense(h_rows, full_up) + bias_up
    act_low = to_low(gelu_tanh(upper))
    f_part = to_low(dense_last(act_low, full_down_t))
    f_branch = add_up(
        exchange_blocks([f_part[s * slots : (s + 1) * slots] for s in blocks], "tensor")
    )
    pre_two = h_one + f_branch + vectors[7]
    h_two = layer_norm(pre_two, vectors[2], vectors[3])
    h_two_low = to_low(h_two)
    rows_low = to_low(dense(h_two_low, full_out))

    rows_group = lax.all_gather(rows_low, "dp", axis=0, tiled=True)
    parts = head_forward(rows_group, table)
    both_rows = after(jnp.concatenate([h_two_low, rows_low], 1), parts)
    both_rows = gather_blocks(both_rows, "tensor")
    parts = lax.all_to_all(parts, "dp", 0, 0, tiled=True).reshape(dp_count, slots, -1)
    part_tops = join_low([parts[:, :, emb_width + i] for i in range(3)])
    part_sums = join_low([parts[:, :, emb_width + 3 + i] for i in range(3)])
    head_top = jnp.max(part_tops, 0)
    shares = jnp.exp(part_tops - head_top)
    total = jnp.sum(shares * part_sums, 0)
    lse = head_top + jnp.log(total)
    valid = comp_row >= 0
    target_logits = jnp.sum(rows_low.astype(jnp.float32) * target_rows, -1)
    loss_part = jnp.sum(jnp.where(valid, lse - target_logits, 0.0))
    slot_weight = 1.0 / (dp_count * tensor_count * slots)
    weight = jnp.where(valid, slot_weight, 0.0)
    mean = add_up(
        [parts[s, :, :emb_width] * (shares[s] / total)[:, None] for s in range(dp_count)]
    )
    out_low = to_low((mean - target_rows) * weight[:, None])

    shift = jnp.where(valid, lse - jnp.log(slot_weight), 1e30)
    shift = jnp.pad(jnp.stack(split_low(shift), 1), ((0, 0), (0, 125)))

    h_two_grad = dense_last(out_low, full_out)
    norm_two = jax.vjp(layer_norm, pre_two, vectors[2], vectors[3])[1]
    pre_two_grad, gain_two_grad, shift_two_grad = norm_two(h_two_grad)
    pre_two_grad, *both_rows = together(pre_two_grad, *both_rows)
    both_rows = jnp.concatenate(both_rows, 0)
    tree_rows = both_rows[:, model_width:]
    h_two_rows = both_rows[:, :model_width]
    f_rows = gather_blocks(jnp.concatenate([to_low(pre_two_grad), shift], 1), "tensor")
    f_rows = jnp.concatenate(f_rows, 0)
    rows_all = lax.all_gather(after(tree_rows, f_rows), "dp", axis=0, tiled=True)
    tree_shift = join_low([f_rows[:, model_width + i] for i in range(3)])
    f_rows = f_rows[:, :model_width]
    grad_down = dense_first(act_low, f_rows)
    act_grad = dense(f_rows, full_down_t)
    upper_low = to_low(jax.vjp(gelu_tanh, upper)[1](act_grad)[0])
    grad_up = dense_first(h_rows, upper_low)
    h_part = to_low(dense_last(upper_low, full_up))
    h_parts = exchange_blocks([h_part[s * slots : (s + 1) * slots] for s in blocks], "tensor")
    early = (3, 4)
    early_merged = [grad_up + error_up[0], grad_down + error_down[0]]
    early_lefts = [left_factor(*pair) for pair in zip(early_merged, (factor_up, factor_down[0]))]
    own_tree = jnp.arange(dp_count) == dp_index
    shift_all = jnp.where(own_tree[:, None], tree_shift[None], 0.0)
    early_lefts.append(shift_all.reshape(early_lefts[0].shape[0], -1))
    early_sizes = [left.shape[1] for left in early_lefts]
    early_lefts = jnp.concatenate(early_lefts, 1)
    h_parts[0], early_lefts = together(h_parts[0], early_lefts)
    h_one_grad = pre_two_grad + add_up(h_parts)
    norm_one = jax.vjp(layer_norm, pre_one, vectors[0], vectors[1])[1]
    pre_one_grad, gain_one_grad, shift_one_grad = norm_one(h_one_grad)
    z_low = to_low(pre_one_grad)
    z_rows = gather_blocks(jnp.concatenate([z_low, out_low], 1), "tensor")
    early_lefts = summed_over(early_lefts, "dp")
    z_rows[0], early_lefts, rows_all = together(z_rows[0], early_lefts, rows_all)
    *early_lefts, shift_all = columns_of(early_lefts, early_sizes)
    shift_all = shift_all.reshape(1, -1)
    z_rows = jnp.concatenate(z_rows, 0)
    out_rows = z_rows[:, model_width:]
    z_rows = z_rows[:, :model_width]
    query_grad, key_value_grad, x_part, row_part, emb_part = attend_back(
        z_rows,
        full_proj_t,
        queries,
        key_value,
        lse_keys,
        key_facts,
        row_facts,
        pack_first,
        full_in,
        pre_one_grad,
    )
    emb_parts = exchange_blocks(
        [emb_part[s * local_count : (s + 1) * local_count] for s in blocks], "tensor"
    )
    *early_lefts, emb_part = together(*early_lefts, emb_part)
    early_bases, early_terms = orthonormal_all(early_lefts)
    early_rights = [right_factor(*pair) for pair in zip(early_merged, early_bases)]
    early_sizes = [right.shape[1] for right in early_rights]
    early_rights = jnp.concatenate(early_rights, 1)
    emb_parts[1], query_grad, key_value_grad = together(emb_parts[1], query_grad, key_value_grad)
    value_grad = key_value_grad[:, width:]
    merged_qkv = [
        dense(left, right) + error_qkv[0, :, part]
        for part, (left, right) in enumerate(
            (
                (to_low(x_rows).T, query_grad),
                (x_turned, key_value_grad[:, :width]),
                (x_turned, value_grad),
            )
        )
    ]
    emb_parts[0], early_rights, *merged_qkv = together(emb_parts[0], early_rights, *merged_qkv)
    emb_grad_own = to_low(add_up(emb_parts))
    emb_grad = gather_blocks(emb_grad_own, "tensor")
    x_part, row_part, z_rows, out_rows, *merged_qkv = together(
        x_part, row_part, z_rows, out_rows, *merged_qkv, emb_grad_own
    )[:-1]
    grad_out = dense_first(h_two_rows, out_rows)
    grad_proj = dense_first(attn_low, z_rows)
    grad_in = dense(emb_turned, x_part) + dense_first(emb_rows, row_part)

    def placed(values, size, total_size):
        return lax.dynamic_update_slice_in_dim(
            jnp.zeros((total_size,), jnp.float32), values, tensor_index * size, 0
        )

    head_rows = jnp.stack(
        [
            gain_one_grad,
            shift_one_grad,
            gain_two_grad,
            shift_two_grad,
            placed(jnp.sum(query_grad.astype(jnp.float32), 0), width, model_width),
            placed(jnp.sum(value_grad.astype(jnp.float32), 0), width, model_width),
            jnp.sum(pre_one_grad, 0),
            jnp.sum(pre_two_grad, 0),
        ]
    )
    up_rows = placed(
        jnp.sum(upper_low.astype(jnp.float32), 0), hidden_share, hidden_share * tensor_count
    ).reshape(-1, model_width)
    loss_row = jnp.full((1, model_width), loss_part)
    vector_rows = [head_rows, up_rows, loss_row]
    spare = -sum(rows.shape[0] for rows in vector_rows) % factor_in.shape[1]
    vector_rows.append(jnp.zeros((spare, model_width), jnp.float32))
    vector_part = jnp.concatenate(vector_rows, 0)
    vector_part = jnp.concatenate(
        jnp.split(vector_part, vector_part.shape[0] // factor_in.shape[1], 0), 1
    )

    merged = (
        grad_in + error_in[0] * (1.0 / tensor_count),
        None,
        grad_proj + error_proj[0],
    ) + tuple(early_merged) + (grad_out + error_out[0],)
    factors = (
        factor_in,
        factor_qkv.reshape(3 * width, -1),
        factor_proj[0],
        None,
        None,
        factor_out,
    )
    bases = [None] * 6
    fresh = [None] * 6
    parts_of = [None] * 6
    late = (0, 1, 2, 5)
    lefts = [
        sum(left_factor(merged_qkv[part], factor_qkv[part]) for part in range(3))
        if index == 1
        else left_factor(merged[index], factors[index])
        for index in late
    ]
    sizes = [left.shape[1] for left in lefts] + [vector_part.shape[1]]
    emb_grad[1], lefts[1] = together(emb_grad[1], lefts[1])
    lefts.append(vector_part)
    lefts = jnp.concatenate(lefts + [early_rights], 1)
    lefts = lefts + swap(lefts, "dp", 1)
    if dp_count > 2:
        lefts = lefts + swap(lefts, "dp", 2)
    *emb_grad[2:], lefts = together(*emb_grad[2:], lefts)
    lefts = summed_over(lefts, "dp", 4)
    tree_weight = jnp.where(comp_tree.reshape(-1) >= 0, slot_weight, 0.0)
    target_grad = to_low(tree_rows.astype(jnp.float32) * -tree_weight[:, None])
    id_grads = emb_grad + [target_grad]

    def deliver_more(turn, state):
        place = placed_ids(turn, owner)
        spots = exchanged(entries_of(listed(place))).reshape(-1) - vocab_start
        rows = exchanged(jnp.stack(listed_sums(place, id_grads, dp_count, share)))
        rows = rows.reshape(dp_count * share, -1).astype(jnp.float32)
        rows = jnp.where((spots >= 0)[:, None], rows, 0.0)
        spots = jnp.clip(spots, 0, shard_rows - 1)
        return state[0].at[spots].add(-table_rate * rows), state[1].at[spots].add(rows)

    added = exchange_blocks(listed_sums(place_first, id_grads, dp_count, share), "dp")
    added[1], lefts = together(added[1], lefts)
    lefts = columns_of(lefts, sizes + early_sizes)
    vector_sum = lefts[len(sizes) - 1]
    flat = gather_blocks(lefts[0], "tensor")
    early_rights = lefts[len(sizes) :]
    early_parts = columns_of(outer_terms(jnp.concatenate(early_rights, 1)), early_sizes)

    def error_left(index):
        return merged[index] - dense_first(bases[index], parts_of[index]) * (1.0 / dp_count)

    errors_new = [None] * 6
    for i, index in enumerate(early):
        bases[index] = early_terms[i]
        fresh[index] = early_rights[i]
        parts_of[index] = early_parts[i]
    errors_new[early[0]] = error_left(early[0])
    flat[0], errors_new[early[0]] = together(flat[0], errors_new[early[0]])
    flat = add_pairs(flat)
    found_bases, found_terms = orthonormal_all([flat[:, : sizes[0]]] + lefts[1 : len(late)])
    rights = [
        jnp.concatenate([right_factor(merged_qkv[part], found_bases[i]) for part in range(3)], 1)
        if index == 1
        else right_factor(merged[index], found_bases[i])
        for i, index in enumerate(late)
    ]
    sizes = [right.shape[1] for right in rights]
    rights = jnp.concatenate(rights, 1)
    rights, held = together(rights, early_parts[1])
    parts_of[early[1]] = held
    errors_new[early[1]] = error_left(early[1])
    rights = summed_over(rights, "dp")
    grad_in_own = lax.psum_scatter(
        after(to_low(grad_in), emb_grad[-1]), "tensor", scatter_dimension=0, tiled=True
    )
    grad_in_sum = lax.all_gather(grad_in_own, "tensor", axis=0, tiled=True)
    right_in = gather_blocks(jnp.concatenate([rights[:, : sizes[0]], vector_sum], 1), "tensor")
    added[0], rights, errors_new[3], errors_new[4] = together(
        added[0], rights, errors_new[3], errors_new[4]
    )
    updated = list(
        table_update(rows_all, shift_all, added, asked_first.reshape(1, -1) - vocab_start, table, table_moment)
    )
    updated[0], right_in[0], grad_in_sum = together(updated[0], right_in[0], grad_in_sum)
    new_table, new_table_moment = lax.fori_loop(1, rounds, deliver_more, tuple(updated))
    rights = columns_of(rights, sizes)
    right_in = add_pairs(right_in)
    rights[0], vector_sum = right_in[:, : sizes[0]], right_in[:, sizes[0] :]
    vector_sum = jnp.concatenate(jnp.split(vector_sum, vector_sum.shape[1] // model_width, 1), 0)
    right_parts = columns_of(outer_terms(jnp.concatenate(rights, 1)), sizes)
    for i, index in enumerate(late):
        bases[index] = found_terms[i]
        fresh[index] = rights[i]
        parts_of[index] = right_parts[i]
    merged = (grad_in_sum.astype(jnp.float32) + error_in[0],) + merged[1:]
    for index in (0, 2, 5):
        errors_new[index] = error_left(index)
    errors_new[1] = jnp.stack(
        [
            merged_qkv[part]
            - dense_first(bases[1], parts_of[1][:, part * width : (part + 1) * width])
            * (1.0 / dp_count)
            for part in range(3)
        ],
        0,
    ).transpose(1, 0, 2)

    def shard(index, size, axis):
        left, right = bases[index], parts_of[index]
        if axis == 0:
            left = lax.dynamic_slice_in_dim(left, dp_index * size, size, 1)
        else:
            right = lax.dynamic_slice_in_dim(right, dp_index * size, size, 1)
        return dense_first(left, right)

    shard_in = shard(0, w_in.shape[0], 0)
    shard_qkv = shard(1, shard_width, 0)
    shard_qkv = jnp.stack(
        [shard_qkv[:, part * width : (part + 1) * width] for part in range(3)], 1
    )
    shard_proj = shard(2, w_proj.shape[1], 1)
    shard_up = shard(3, w_up.shape[0], 0)
    shard_down = shard(4, w_down.shape[1], 1)
    shard_out = shard(5, w_out.shape[0], 0)
    fresh = [values.T for values in fresh]
    loss_sum = vector_sum[vectors.shape[0], 0]
    vector_grad = vector_sum[: vectors.shape[0]]
    new_w_in, new_moment_in = advance(w_in, moment_in, shard_in, matrix_rates[0])
    new_w_qkv, new_moment_qkv = advance(w_qkv, moment_qkv, shard_qkv, matrix_rates[1])
    new_w_proj, new_moment_proj = advance(w_proj, moment_proj, shard_proj, matrix_rates[2])
    new_w_up, new_moment_up = advance(w_up, moment_up, shard_up, matrix_rates[3])
    new_w_down, new_moment_down = advance(w_down, moment_down, shard_down, matrix_rates[4])
    new_w_out, new_moment_out = advance(w_out, moment_out, shard_out, matrix_rates[5])
    new_vectors, new_vector_moment = advance(vectors, vector_moment, vector_grad, vector_rate)
    return (
        loss_sum,
        new_table,
        new_table_moment,
        new_vectors,
        new_vector_moment,
        new_w_in,
        new_moment_in,
        errors_new[0][None],
        fresh[0],
        new_w_qkv,
        new_moment_qkv,
        errors_new[1].reshape(1, model_width, 3, width),
        fresh[1].reshape(3, width, -1),
        new_w_proj,
        new_moment_proj,
        errors_new[2][None],
        fresh[2][None],
        new_w_up,
        new_moment_up,
        errors_new[3][None],
        fresh[3],
        new_w_down,
        new_moment_down,
        errors_new[4][None],
        fresh[4][None],
        new_w_out,
        new_moment_out,
        errors_new[5][None],
        fresh[5],
    )


def solution(mesh):
    return jax.shard_map(
        per_device,
        mesh=mesh,
        in_specs=(
            P("dp", "tensor"),
            P("dp", None),
            P("dp", None),
            P("dp", "tensor"),
            P("dp", "tensor"),
            P("dp", None),
            P("dp", None),
            P(),
            P(),
            P("dp", None),
            P("dp", None),
            P("dp", None, None),
            P(),
            P("dp", None, "tensor"),
            P("dp", None, "tensor"),
            P("dp", None, None, "tensor"),
            P(None, "tensor", None),
            P("tensor", "dp"),
            P("tensor", "dp"),
            P("dp", "tensor", None),
            P("tensor", None, None),
            P("dp", "tensor"),
            P("dp", "tensor"),
            P("dp", None, "tensor"),
            P("tensor", None),
            P("tensor", "dp"),
            P("tensor", "dp"),
            P("dp", "tensor", None),
            P("tensor", None, None),
            P("dp", None),
            P("dp", None),
            P("dp", None, None),
            P(),
        ),
        out_specs=(
            P(),
            P("dp", None),
            P("dp", None),
            P(),
            P(),
            P("dp", None),
            P("dp", None),
            P("dp", None, None),
            P(),
            P("dp", None, "tensor"),
            P("dp", None, "tensor"),
            P("dp", None, None, "tensor"),
            P(None, "tensor", None),
            P("tensor", "dp"),
            P("tensor", "dp"),
            P("dp", "tensor", None),
            P("tensor", None, None),
            P("dp", "tensor"),
            P("dp", "tensor"),
            P("dp", None, "tensor"),
            P("tensor", None),
            P("tensor", "dp"),
            P("tensor", "dp"),
            P("dp", "tensor", None),
            P("tensor", None, None),
            P("dp", None),
            P("dp", None),
            P("dp", None, None),
            P(),
        ),
        check_vma=False,
    )
```
